32 devices in a mesh: parts: 2 (over x), group: 16 (over z, y, core).
Axes of the slice: x: 2, y: 2, z: 4, core: 2. Of those that a mesh axis runs over, the one named last changes fastest.
Arguments:
- solve_cols: bfloat16 [64, 512, 512], P(('parts', 'group')), parts along dimension 0
- region_groups: int32 [32, 4], P('group'), may hold values from 0 to 15, as said below
Outputs:
- schur: float32 [32, 7, 128, 128], P(('parts', 'group')), parts along dimension 0
The draws below stay inside these ranges and needn't reach their ends.
There are 2 independent parts, one for each index of `parts`. The reference program is written for one: setup_inputs(seed, part) draws one part's arguments, and reference() takes and returns one part's arrays. A program takes and returns all parts, laid end to end along the dimension named above; an argument that names none is the same for every part. Nothing has to cross between parts.
Inputs may be any that keep to these rules, and one draw needn't show every extreme that they name: `region_groups`: the 4 groups of a region are 4 consecutive groups modulo 16, in any order. The 2 regions of one device together name 8 consecutive groups modulo 16, each once, so the slots of one device name one group at most 1 times, and exactly 1 times for some group.
All inputs are finite; a program needn't handle non-finite values.
Results may differ from the reference program's by a relative error of at most 0.00048.
Values may be sent and summed in bfloat16 or wider, within the bound.
No kernel may reach another device: no remote copies, remote signals or barrier semaphores. Data moves between devices by JAX's collectives and lax.ppermute only.
A program may use at most 128 MiB of HBM per device.

```python
import math
import jax
import jax.numpy as jnp
from jax import lax

GW = 128
SLOTS = 4
COLS = 512
REACH = 3
ROWS = 512
REG_DEV = 2
GROUPS = 16
REGIONS = 32


def draw_solve_cols(key, part):
    key_noise, key_shared, key_gain = jax.random.split(key, 3)
    noise = jax.random.normal(key_noise, (REGIONS, ROWS, SLOTS, GW), jnp.float32)
    shared = jax.random.normal(key_shared, (REGIONS, ROWS, 1, GW), jnp.float32)
    gains = jax.random.uniform(key_gain, (REGIONS, 1, SLOTS, 1), jnp.float32, 0.5, 1.5)
    values = (noise + 0.8 * gains * shared) * (1.0 / math.sqrt(32.0 * ROWS))
    return values.reshape(REGIONS, ROWS, COLS).astype(jnp.bfloat16)


def draw_region_groups(key, part):
    key_hot, key_near, key_far, key_flag, key_perm = jax.random.split(key, 5)
    device_count = REGIONS // REG_DEV
    hot_group = jax.random.randint(key_hot, (), 0, GROUPS)
    near_shift = jax.random.randint(key_near, (device_count,), -(GROUPS // 8), GROUPS // 8 + 1)
    far_base = jax.random.randint(key_far, (device_count,), 0, GROUPS)
    flags = jax.random.randint(key_flag, (device_count,), 0, 2)
    base_group = jnp.where(flags == 1, hot_group + near_shift, far_base) % GROUPS
    starts = base_group[:, None] + SLOTS * jnp.arange(REG_DEV, dtype=jnp.int32)[None, :]
    scores = jax.random.randint(key_perm, (device_count, REG_DEV, SLOTS), 0, 1000) * SLOTS
    scores = scores + jnp.arange(SLOTS, dtype=jnp.int32)[None, None, :]
    slot_order = jnp.argsort(scores, axis=-1).astype(jnp.int32)
    groups = (starts[:, :, None] + slot_order) % GROUPS
    return groups.reshape(REGIONS, SLOTS).astype(jnp.int32)


def setup_inputs(seed: int = 0, part: int = 0) -> dict:
    key_list = jax.random.split(jax.random.key(seed), 3)
    part_splits = jax.random.split(jax.random.fold_in(key_list[2], part), 3)
    solve_cols = draw_solve_cols(jax.random.fold_in(jax.random.fold_in(key_list[2], part), 71), part)
    region_groups = draw_region_groups(jax.random.fold_in(key_list[2], 71), part)
    return dict(solve_cols=solve_cols, region_groups=region_groups)


def reference(solve_cols, region_groups):
    block_width = COLS // SLOTS
    span_count = 2 * REACH + 1

    def add_region(schur_acc, inputs):
        region_cols, region_slots = inputs
        gram_block = jnp.dot(region_cols.T, region_cols, preferred_element_type=jnp.float32).astype(jnp.bfloat16)
        gram_block = lax.optimization_barrier(gram_block).astype(jnp.float32)
        blocks = gram_block.reshape(SLOTS, block_width, SLOTS, block_width).transpose(0, 2, 1, 3)
        blocks = blocks.reshape(SLOTS * SLOTS, block_width, block_width)
        owners = jnp.repeat(region_slots, SLOTS)
        span_index = ((region_slots[None, :] - region_slots[:, None] + REACH) % GROUPS).reshape(-1)
        schur_acc = schur_acc.at[owners, span_index].add(blocks.astype(schur_acc.dtype))
        return schur_acc, None

    initial = jnp.zeros((GROUPS, span_count, block_width, block_width), jnp.float32)
    schur_out, _ = lax.scan(add_region, initial, (solve_cols, region_groups))
    return schur_out
```

```python
import functools

import jax
import jax.numpy as jnp
from jax import lax
from jax.experimental import pallas as pl
from jax.experimental.pallas import tpu as pltpu
from jax.sharding import PartitionSpec as P

VMEM_BYTES = 48 * 1024 * 1024


def gram_kernel(total_groups, half, groups_ref, cols_ref, send_ref):
    region = pl.program_id(0)
    slot_count = groups_ref.shape[1]
    width = cols_ref.shape[2] // slot_count
    my_half = lax.axis_index("group") // half
    cols = cols_ref[0]
    gram = lax.dot_general(
        cols, cols, (((0,), (0,)), ((), ())), preferred_element_type=jnp.float32
    )
    groups = [groups_ref[region, s] for s in range(slot_count)]

    def ahead(s, t):
        return lax.rem(groups[t] - groups[s] + total_groups, total_groups)

    row = lax.broadcasted_iota(jnp.int32, (width, width), 0)
    col = lax.broadcasted_iota(jnp.int32, (width, width), 1)
    for s in range(slot_count):
        place = 0
        for t in range(slot_count):
            if t != s:
                place = place + (ahead(t, s) < slot_count).astype(jnp.int32)
        away = (groups[s] // half != my_half).astype(jnp.int32)
        tag = (place + slot_count * away).astype(jnp.float32)
        slot = lax.rem(groups[s], half)
        for t in range(slot_count):
            block = gram[s * width : (s + 1) * width, t * width : (t + 1) * width]
            if t == s:
                block = jnp.where((row == width - 1) & (col < width - 1), tag, block)
                turn = 0
            else:
                gap = ahead(s, t)
                turn = jnp.where(gap < slot_count, gap, gap - total_groups + slot_count)
            send_ref[slot, turn] = block.astype(send_ref.dtype)


def sum_kernel(got_ref, near_ref, far_ref):
    sources, slot_count, width, _ = got_ref.shape
    reach = slot_count - 1
    near_ref[...] = jnp.zeros_like(near_ref)
    far_ref[...] = jnp.zeros_like(far_ref)

    def add_source(source, carry):
        tag = jnp.max(
            got_ref[source, 0, width - 16 : width, 0:width].astype(jnp.float32)[15:16, 0:1]
        ).astype(jnp.int32)
        away = tag // slot_count
        place = tag - slot_count * away

        def add(into_ref):
            for turn in range(slot_count):
                offset = turn - slot_count * (place + turn >= slot_count).astype(jnp.int32)
                into_ref[reach + offset] += got_ref[source, turn].astype(jnp.float32)

        pl.when(away == 0)(lambda: add(near_ref))
        pl.when(away != 0)(lambda: add(far_ref))
        return carry

    lax.fori_loop(0, sources, add_source, 0)
    row = lax.broadcasted_iota(jnp.int32, (width, width), 0)
    col = lax.broadcasted_iota(jnp.int32, (width, width), 1)
    for into_ref in (near_ref, far_ref):
        block = into_ref[reach]
        into_ref[reach] = jnp.where((row == width - 1) & (col < width - 1), block.T, block)


def shards(solve_cols, region_groups):
    region_count, row_count, col_count = solve_cols.shape
    slot_count = region_groups.shape[1]
    width = col_count // slot_count
    total_groups = lax.axis_size("group")
    half = region_count * slot_count
    span_count = 2 * slot_count - 1
    send = pl.pallas_call(
        functools.partial(gram_kernel, total_groups, half),
        grid=(region_count,),
        in_specs=[
            pl.BlockSpec(memory_space=pltpu.SMEM),
            pl.BlockSpec((1, row_count, col_count), lambda r: (r, 0, 0)),
        ],
        out_specs=pl.BlockSpec((half, slot_count, width, width), lambda r: (0, 0, 0, 0)),
        out_shape=jax.ShapeDtypeStruct((half, slot_count, width, width), jnp.bfloat16),
        compiler_params=pltpu.CompilerParams(vmem_limit_bytes=VMEM_BYTES),
        name="gram_rows",
    )(region_groups, solve_cols)
    halves = [list(range(at, at + half)) for at in range(0, total_groups, half)]
    got = lax.all_to_all(
        send, "group", split_axis=0, concat_axis=0, axis_index_groups=halves, tiled=True
    )
    part = jax.ShapeDtypeStruct((span_count, width, width), jnp.float32)
    near, far = pl.pallas_call(
        sum_kernel,
        out_shape=(part, part),
        compiler_params=pltpu.CompilerParams(vmem_limit_bytes=VMEM_BYTES),
        name="sum_offsets",
    )(got)
    swap = [(d, (d + half) % total_groups) for d in range(total_groups)]
    return (near + lax.ppermute(far, "group", swap))[None]


def solution(mesh):
    return jax.shard_map(
        shards,
        mesh=mesh,
        in_specs=(P(("parts", "group"), None, None), P("group", None)),
        out_specs=P(("parts", "group"), None, None, None),
        check_vma=False,
    )
```

```python
import functools

import jax
import jax.numpy as jnp
from jax import lax
from jax.experimental import pallas as pl
from jax.experimental.pallas import tpu as pltpu
from jax.sharding import PartitionSpec as P

VMEM_BYTES = 48 * 1024 * 1024


def gram_kernel(total_groups, half, groups_ref, cols_ref, *refs):
    send_refs, rows_ref = refs[:-1], refs[-1]
    region = pl.program_id(0)
    slot_count = groups_ref.shape[1]
    width = cols_ref.shape[2] // slot_count
    me = lax.axis_index("group")
    my_half, my_slot = me // half, lax.rem(me, half)
    cols = cols_ref[0]
    gram = lax.dot_general(
        cols, cols, (((0,), (0,)), ((), ())), preferred_element_type=jnp.float32
    )
    groups = [groups_ref[region, s] for s in range(slot_count)]

    def ahead(s, t):
        return lax.rem(groups[t] - groups[s] + total_groups, total_groups)

    row = lax.broadcasted_iota(jnp.int32, (width, width), 0)
    col = lax.broadcasted_iota(jnp.int32, (width, width), 1)
    for s in range(slot_count):
        place = 0
        for t in range(slot_count):
            if t != s:
                place = place + (ahead(t, s) < slot_count).astype(jnp.int32)
        away = (groups[s] // half != my_half).astype(jnp.int32)
        tag = (place + slot_count * away).astype(jnp.float32)
        slot = lax.rem(groups[s] - my_slot + total_groups, half)
        for t in range(slot_count):
            block = gram[s * width : (s + 1) * width, t * width : (t + 1) * width]
            if t == s:
                block = jnp.where((row == width - 1) & (col < width - 1), tag, block)
                turn = 0
            else:
                gap = ahead(s, t)
                turn = jnp.where(gap < slot_count, gap, gap - total_groups + slot_count)
            rows_ref[slot, turn] = block.astype(rows_ref.dtype)

    @pl.when(region == pl.num_programs(0) - 1)
    def _():
        for step, send_ref in enumerate(send_refs):
            send_ref[...] = rows_ref[step]


def sum_kernel(*refs):
    got_refs, (near_ref, far_ref) = refs[:-2], refs[-2:]
    slot_count, width, _ = got_refs[0].shape
    reach = slot_count - 1
    near_ref[...] = jnp.zeros_like(near_ref)
    far_ref[...] = jnp.zeros_like(far_ref)

    def add_source(got_ref):
        tag = jnp.max(
            got_ref[0, width - 16 : width, 0:width].astype(jnp.float32)[15:16, 0:1]
        ).astype(jnp.int32)
        away = tag // slot_count
        place = tag - slot_count * away

        def add(into_ref):
            for turn in range(slot_count):
                offset = turn - slot_count * (place + turn >= slot_count).astype(jnp.int32)
                into_ref[reach + offset] += got_ref[turn].astype(jnp.float32)

        pl.when(away == 0)(lambda: add(near_ref))
        pl.when(away != 0)(lambda: add(far_ref))

    for got_ref in got_refs:
        add_source(got_ref)
    row = lax.broadcasted_iota(jnp.int32, (width, width), 0)
    col = lax.broadcasted_iota(jnp.int32, (width, width), 1)
    for into_ref in (near_ref, far_ref):
        block = into_ref[reach]
        into_ref[reach] = jnp.where((row == width - 1) & (col < width - 1), block.T, block)


def shards(solve_cols, region_groups):
    region_count, row_count, col_count = solve_cols.shape
    slot_count = region_groups.shape[1]
    width = col_count // slot_count
    total_groups = lax.axis_size("group")
    half = region_count * slot_count
    span_count = 2 * slot_count - 1
    rows = jax.ShapeDtypeStruct((slot_count, width, width), jnp.bfloat16)
    sends = pl.pallas_call(
        functools.partial(gram_kernel, total_groups, half),
        grid=(region_count,),
        in_specs=[
            pl.BlockSpec(memory_space=pltpu.SMEM),
            pl.BlockSpec((1, row_count, col_count), lambda r: (r, 0, 0)),
        ],
        out_specs=[pl.BlockSpec(rows.shape, lambda r: (0, 0, 0))] * half,
        out_shape=[rows] * half,
        scratch_shapes=[pltpu.VMEM((half,) + rows.shape, rows.dtype)],
        compiler_params=pltpu.CompilerParams(vmem_limit_bytes=VMEM_BYTES),
        name="gram_rows",
    )(region_groups, solve_cols)
    gots = [sends[0]]
    for step in range(1, half):
        turn_half = [
            (at + d, at + (d + step) % half)
            for at in range(0, total_groups, half)
            for d in range(half)
        ]
        gots.append(lax.ppermute(sends[step], "group", turn_half))
    part = jax.ShapeDtypeStruct((span_count, width, width), jnp.float32)
    near, far = pl.pallas_call(
        sum_kernel,
        out_shape=(part, part),
        compiler_params=pltpu.CompilerParams(vmem_limit_bytes=VMEM_BYTES),
        name="sum_offsets",
    )(*gots)
    swap = [(d, (d + half) % total_groups) for d in range(total_groups)]
    return (near + lax.ppermute(far, "group", swap))[None]


def solution(mesh):
    return jax.shard_map(
        shards,
        mesh=mesh,
        in_specs=(P(("parts", "group"), None, None), P("group", None)),
        out_specs=P(("parts", "group"), None, None, None),
        check_vma=False,
    )
```

```python
import functools

import jax
import jax.numpy as jnp
from jax import lax
from jax.experimental import pallas as pl
from jax.experimental.pallas import tpu as pltpu
from jax.sharding import PartitionSpec as P

VMEM_BYTES = 48 * 1024 * 1024
LEAST_POWER = -100.0
TOP_POWER = 13.0


def gram_kernel(total_groups, half, groups_ref, cols_ref, *refs):
    send_refs, rows_ref = refs[:-1], refs[-1]
    region = pl.program_id(0)
    slot_count = groups_ref.shape[1]
    width = cols_ref.shape[2] // slot_count
    me = lax.axis_index("group")
    my_half, my_slot = me // half, lax.rem(me, half)
    cols = cols_ref[0]
    gram = lax.dot_general(
        cols, cols, (((0,), (0,)), ((), ())), preferred_element_type=jnp.float32
    )
    groups = [groups_ref[region, s] for s in range(slot_count)]

    def ahead(s, t):
        return lax.rem(groups[t] - groups[s] + total_groups, total_groups)

    row = lax.broadcasted_iota(jnp.int32, (width, width), 0)
    col = lax.broadcasted_iota(jnp.int32, (width, width), 1)
    for s in range(slot_count):
        place = 0
        for t in range(slot_count):
            if t != s:
                place = place + (ahead(t, s) < slot_count).astype(jnp.int32)
        away = (groups[s] // half != my_half).astype(jnp.int32)
        tag = (place + slot_count * away).astype(jnp.float32)
        slot = lax.rem(groups[s] - my_slot + total_groups, half)
        for t in range(slot_count):
            block = gram[s * width : (s + 1) * width, t * width : (t + 1) * width]
            if t == s:
                block = jnp.where((row == width - 1) & (col < width - 1), tag, block)
                turn = 0
            else:
                gap = ahead(s, t)
                turn = jnp.where(gap < slot_count, gap, gap - total_groups + slot_count)
            rows_ref[slot, turn] = block.astype(rows_ref.dtype)

    @pl.when(region == pl.num_programs(0) - 1)
    def _():
        for step, send_ref in enumerate(send_refs):
            send_ref[...] = rows_ref[step]


def sum_kernel(*refs):
    got_refs, (near_ref, scaled_ref, far_ref) = refs[:-3], refs[-3:]
    slot_count, width, _ = got_refs[0].shape
    reach = slot_count - 1
    near_ref[...] = jnp.zeros_like(near_ref)
    far_ref[...] = jnp.zeros_like(far_ref)

    def add_source(got_ref):
        tag = jnp.max(
            got_ref[0, width - 16 : width, 0:width].astype(jnp.float32)[15:16, 0:1]
        ).astype(jnp.int32)
        away = tag // slot_count
        place = tag - slot_count * away

        def add(into_ref):
            for turn in range(slot_count):
                offset = turn - slot_count * (place + turn >= slot_count).astype(jnp.int32)
                into_ref[reach + offset] += got_ref[turn].astype(jnp.float32)

        pl.when(away == 0)(lambda: add(near_ref))
        pl.when(away != 0)(lambda: add(far_ref))

    for got_ref in got_refs:
        add_source(got_ref)
    row = lax.broadcasted_iota(jnp.int32, (width, width), 0)
    col = lax.broadcasted_iota(jnp.int32, (width, width), 1)
    for into_ref in (near_ref, far_ref):
        block = into_ref[reach]
        into_ref[reach] = jnp.where((row == width - 1) & (col < width - 1), block.T, block)

    span_count = far_ref.shape[0]
    largest = jnp.max(jnp.abs(far_ref[0]), axis=0, keepdims=True)
    for span in range(1, span_count):
        top = jnp.max(jnp.abs(far_ref[span]), axis=0, keepdims=True)
        largest = jnp.maximum(largest, top)
    largest = jnp.max(jnp.broadcast_to(largest, (8, width)), axis=1, keepdims=True)
    power = jnp.floor(jnp.log2(jnp.maximum(largest, 2.0**LEAST_POWER))) - TOP_POWER
    factor = jnp.exp2(-power)[0:1]
    for span in range(span_count):
        scaled_ref[span * width : (span + 1) * width] = far_ref[span] * factor
    scaled_ref[span_count * width :] = jnp.broadcast_to(power[0:1], (16, width))


def shards(solve_cols, region_groups):
    region_count, row_count, col_count = solve_cols.shape
    slot_count = region_groups.shape[1]
    width = col_count // slot_count
    total_groups = lax.axis_size("group")
    half = region_count * slot_count
    span_count = 2 * slot_count - 1
    rows = jax.ShapeDtypeStruct((slot_count, width, width), jnp.bfloat16)
    sends = pl.pallas_call(
        functools.partial(gram_kernel, total_groups, half),
        grid=(region_count,),
        in_specs=[
            pl.BlockSpec(memory_space=pltpu.SMEM),
            pl.BlockSpec((1, row_count, col_count), lambda r: (r, 0, 0)),
        ],
        out_specs=[pl.BlockSpec(rows.shape, lambda r: (0, 0, 0))] * half,
        out_shape=[rows] * half,
        scratch_shapes=[pltpu.VMEM((half,) + rows.shape, rows.dtype)],
        compiler_params=pltpu.CompilerParams(vmem_limit_bytes=VMEM_BYTES),
        name="gram_rows",
    )(region_groups, solve_cols)
    gots = [sends[0]]
    for step in range(1, half):
        turn_half = [
            (at + d, at + (d + step) % half)
            for at in range(0, total_groups, half)
            for d in range(half)
        ]
        gots.append(lax.ppermute(sends[step], "group", turn_half))
    part = jax.ShapeDtypeStruct((span_count, width, width), jnp.float32)
    scaled = jax.ShapeDtypeStruct((span_count * width + 16, width), jnp.float32)
    near, far = pl.pallas_call(
        sum_kernel,
        out_shape=(part, scaled),
        scratch_shapes=[pltpu.VMEM(part.shape, part.dtype)],
        compiler_params=pltpu.CompilerParams(vmem_limit_bytes=VMEM_BYTES),
        name="sum_offsets",
    )(*gots)
    swap = [(d, (d + half) % total_groups) for d in range(total_groups)]
    far = lax.ppermute(far.astype(jnp.float16), "group", swap).astype(jnp.float32)
    far = far[:-16] * jnp.exp2(far[-16:-15])
    return (near + far.reshape(part.shape))[None]


def solution(mesh):
    return jax.shard_map(
        shards,
        mesh=mesh,
        in_specs=(P(("parts", "group"), None, None), P("group", None)),
        out_specs=P(("parts", "group"), None, None, None),
        check_vma=False,
    )
```

```python
import functools

import jax
import jax.numpy as jnp
from jax import lax
from jax.experimental import pallas as pl
from jax.experimental.pallas import tpu as pltpu
from jax.sharding import PartitionSpec as P

VMEM_BYTES = 48 * 1024 * 1024
LEAST_POWER = -100.0
TOP_POWER = 13.0


def gram_kernel(total_groups, half, groups_hbm, cols_hbm, *refs):
    send_refs = refs[:half]
    groups_ref, cols_ref, rows_ref, groups_sem, cols_sems = refs[half:]
    region_count, slot_count = groups_ref.shape
    width = cols_ref.shape[2] // slot_count
    me = lax.axis_index("group")
    my_half, my_slot = me // half, lax.rem(me, half)
    groups_copy = pltpu.make_async_copy(groups_hbm, groups_ref, groups_sem)
    groups_copy.start()

    def cols_copy(region):
        return pltpu.make_async_copy(
            cols_hbm.at[region], cols_ref.at[region], cols_sems.at[region]
        )

    for region in range(region_count):
        cols_copy(region).start()
    groups_copy.wait()
    row = lax.broadcasted_iota(jnp.int32, (width, width), 0)
    col = lax.broadcasted_iota(jnp.int32, (width, width), 1)

    def add_region(region, carry):
        cols_copy(region).wait()
        cols = cols_ref[region]
        gram = lax.dot_general(
            cols, cols, (((0,), (0,)), ((), ())), preferred_element_type=jnp.float32
        )
        groups = [groups_ref[region, s] for s in range(slot_count)]

        def ahead(s, t):
            return lax.rem(groups[t] - groups[s] + total_groups, total_groups)

        for s in range(slot_count):
            place = 0
            for t in range(slot_count):
                if t != s:
                    place = place + (ahead(t, s) < slot_count).astype(jnp.int32)
            away = (groups[s] // half != my_half).astype(jnp.int32)
            tag = (place + slot_count * away).astype(jnp.float32)
            slot = lax.rem(groups[s], half) ^ my_slot
            for t in range(slot_count):
                block = gram[s * width : (s + 1) * width, t * width : (t + 1) * width]
                if t == s:
                    block = jnp.where((row == width - 1) & (col < width - 1), tag, block)
                    turn = 0
                else:
                    gap = ahead(s, t)
                    turn = jnp.where(gap < slot_count, gap, gap - total_groups + slot_count)
                rows_ref[slot, turn] = block.astype(rows_ref.dtype)
        return carry

    lax.fori_loop(0, region_count, add_region, 0, unroll=region_count <= 2)
    for step, send_ref in enumerate(send_refs):
        send_ref[...] = rows_ref[step]


def sum_kernel(*refs):
    got_refs, (near_ref, scaled_ref, far_ref) = refs[:-3], refs[-3:]
    slot_count, width, _ = got_refs[0].shape
    reach = slot_count - 1
    near_ref[...] = jnp.zeros_like(near_ref)
    far_ref[...] = jnp.zeros_like(far_ref)

    def add_source(got_ref):
        tag = jnp.max(
            got_ref[0, width - 16 : width, 0:width].astype(jnp.float32)[15:16, 0:1]
        ).astype(jnp.int32)
        away = tag // slot_count
        place = tag - slot_count * away

        def add(into_ref):
            for turn in range(slot_count):
                offset = turn - slot_count * (place + turn >= slot_count).astype(jnp.int32)
                into_ref[reach + offset] += got_ref[turn].astype(jnp.float32)

        pl.when(away == 0)(lambda: add(near_ref))
        pl.when(away != 0)(lambda: add(far_ref))

    for got_ref in got_refs:
        add_source(got_ref)
    row = lax.broadcasted_iota(jnp.int32, (width, width), 0)
    col = lax.broadcasted_iota(jnp.int32, (width, width), 1)
    for into_ref in (near_ref, far_ref):
        block = into_ref[reach]
        into_ref[reach] = jnp.where((row == width - 1) & (col < width - 1), block.T, block)

    span_count = far_ref.shape[0]
    largest = jnp.max(jnp.abs(far_ref[0]), axis=0, keepdims=True)
    for span in range(1, span_count):
        top = jnp.max(jnp.abs(far_ref[span]), axis=0, keepdims=True)
        largest = jnp.maximum(largest, top)
    largest = jnp.max(jnp.broadcast_to(largest, (8, width)), axis=1, keepdims=True)
    power = jnp.floor(jnp.log2(jnp.maximum(largest, 2.0**LEAST_POWER))) - TOP_POWER
    factor = jnp.exp2(-power)[0:1]
    for span in range(span_count):
        scaled_ref[span * width : (span + 1) * width] = far_ref[span] * factor
    scaled_ref[span_count * width :] = jnp.broadcast_to(power[0:1], (16, width))


def shards(solve_cols, region_groups):
    region_count, row_count, col_count = solve_cols.shape
    slot_count = region_groups.shape[1]
    width = col_count // slot_count
    total_groups = lax.axis_size("group")
    half = region_count * slot_count
    span_count = 2 * slot_count - 1
    rows = jax.ShapeDtypeStruct((slot_count, width, width), jnp.bfloat16)
    sends = pl.pallas_call(
        functools.partial(gram_kernel, total_groups, half),
        in_specs=[pl.BlockSpec(memory_space=pltpu.HBM)] * 2,
        out_specs=[pl.BlockSpec(memory_space=pltpu.VMEM)] * half,
        out_shape=[rows] * half,
        scratch_shapes=[
            pltpu.SMEM(region_groups.shape, region_groups.dtype),
            pltpu.VMEM(solve_cols.shape, solve_cols.dtype),
            pltpu.VMEM((half,) + rows.shape, rows.dtype),
            pltpu.SemaphoreType.DMA,
            pltpu.SemaphoreType.DMA((region_count,)),
        ],
        compiler_params=pltpu.CompilerParams(vmem_limit_bytes=VMEM_BYTES),
        name="gram_rows",
    )(
        pltpu.with_memory_space_constraint(region_groups, pltpu.HBM),
        pltpu.with_memory_space_constraint(solve_cols, pltpu.HBM),
    )
    gots = [sends[0]]
    for step in range(half - 1, 0, -1):
        pairs = [(d, d ^ step) for d in range(total_groups)]
        gots.append(lax.ppermute(sends[step], "group", pairs))
    part = jax.ShapeDtypeStruct((span_count, width, width), jnp.float32)
    scaled = jax.ShapeDtypeStruct((span_count * width + 16, width), jnp.float32)
    near, far = pl.pallas_call(
        sum_kernel,
        out_shape=(part, scaled),
        scratch_shapes=[pltpu.VMEM(part.shape, part.dtype)],
        compiler_params=pltpu.CompilerParams(vmem_limit_bytes=VMEM_BYTES),
        name="sum_offsets",
    )(*gots)
    swap = [(d, (d + half) % total_groups) for d in range(total_groups)]
    far = lax.ppermute(far.astype(jnp.float16), "group", swap).astype(jnp.float32)
    far = far[:-16] * jnp.exp2(far[-16:-15])
    return (near + far.reshape(part.shape))[None]


def solution(mesh):
    return jax.shard_map(
        shards,
        mesh=mesh,
        in_specs=(P(("parts", "group"), None, None), P("group", None)),
        out_specs=P(("parts", "group"), None, None, None),
        check_vma=False,
    )
```

```python
import functools

import jax
import jax.numpy as jnp
from jax import lax
from jax.experimental import pallas as pl
from jax.experimental.pallas import tpu as pltpu
from jax.sharding import PartitionSpec as P

VMEM_BYTES = 48 * 1024 * 1024
LEAST_POWER = -100.0
TOP_POWER = 13.0
CHUNKS = 2
CORES = 2
JOIN_WEIGHT = 16 * 1024 * 1024


def gram_kernel(total_groups, half, groups_hbm, cols_hbm, *refs):
    groups_ref, cols_ref, rows_ref, groups_sem, cols_sems = refs[-5:]
    send_refs = refs[:-5]
    region_count, slot_count = groups_ref.shape
    width = cols_ref.shape[2] // slot_count
    me = lax.axis_index("group")
    my_half, my_slot = me // half, lax.rem(me, half)
    groups_copy = pltpu.make_async_copy(groups_hbm, groups_ref, groups_sem)
    groups_copy.start()

    def cols_copy(region):
        return pltpu.make_async_copy(
            cols_hbm.at[region], cols_ref.at[region], cols_sems.at[region]
        )

    for region in range(region_count):
        cols_copy(region).start()
    groups_copy.wait()
    row = lax.broadcasted_iota(jnp.int32, (width, width), 0)
    col = lax.broadcasted_iota(jnp.int32, (width, width), 1)

    def add_region(region, carry):
        cols_copy(region).wait()
        cols = cols_ref[region]
        gram = lax.dot_general(
            cols, cols, (((0,), (0,)), ((), ())), preferred_element_type=jnp.float32
        )
        groups = [groups_ref[region, s] for s in range(slot_count)]

        def ahead(s, t):
            return lax.rem(groups[t] - groups[s] + total_groups, total_groups)

        for s in range(slot_count):
            place = 0
            for t in range(slot_count):
                if t != s:
                    place = place + (ahead(t, s) < slot_count).astype(jnp.int32)
            away = (groups[s] // half != my_half).astype(jnp.int32)
            tag = (place + slot_count * away).astype(jnp.float32)
            slot = lax.rem(groups[s], half) ^ my_slot
            for t in range(slot_count):
                block = gram[s * width : (s + 1) * width, t * width : (t + 1) * width]
                if t == s:
                    block = jnp.where((row == width - 1) & (col < width - 1), tag, block)
                    turn = 0
                else:
                    gap = ahead(s, t)
                    turn = jnp.where(gap < slot_count, gap, gap - total_groups + slot_count)
                rows_ref[slot, turn] = block.astype(rows_ref.dtype)
        return carry

    lax.fori_loop(0, region_count, add_region, 0, unroll=region_count <= 2)
    for at, send_ref in enumerate(send_refs):
        turns = turns_of(at % CHUNKS, slot_count)
        for core in range(CORES):
            slot = CORES * (at // CHUNKS) + core
            send_ref[core] = rows_ref[slot, turns[0] : turns[-1] + 1]


def turns_of(chunk, slot_count):
    return range(slot_count - 1) if chunk == 0 else range(slot_count - 1, slot_count)


def spans_of(chunk, slot_count):
    turns = turns_of(chunk, slot_count)
    return [o for t in turns for o in ([t, t - slot_count] if t else [0])]


def sum_kernel(chunk, slot_count, has_core, *refs):
    near_ref, scaled_ref, far_ref = refs[-3:]
    source_count = len(has_core)
    tag_refs, got_refs = refs[:source_count], refs[:-3][-source_count:]
    width = near_ref.shape[1]
    turns, spans = turns_of(chunk, slot_count), spans_of(chunk, slot_count)
    near_ref[...] = jnp.zeros_like(near_ref)
    far_ref[...] = jnp.zeros_like(far_ref)

    for tag_ref, got_ref, core in zip(tag_refs, got_refs, has_core):
        if core:
            tag_ref, got_ref = tag_ref.at[0], got_ref.at[0]
        tag = jnp.max(
            tag_ref[0, width - 16 : width, 0:width].astype(jnp.float32)[15:16, 0:1]
        ).astype(jnp.int32)
        away = tag // slot_count
        place = tag - slot_count * away

        def add(into_ref):
            for turn in turns:
                at = spans.index(turn)
                if turn:
                    at = at + (place + turn >= slot_count).astype(jnp.int32)
                into_ref[at] += got_ref[turn - turns[0]].astype(jnp.float32)

        pl.when(away == 0)(lambda: add(near_ref))
        pl.when(away != 0)(lambda: add(far_ref))

    if chunk == 0:
        row = lax.broadcasted_iota(jnp.int32, (width, width), 0)
        col = lax.broadcasted_iota(jnp.int32, (width, width), 1)
        for into_ref in (near_ref, far_ref):
            block = into_ref[0]
            into_ref[0] = jnp.where((row == width - 1) & (col < width - 1), block.T, block)

    largest = jnp.max(jnp.abs(far_ref[0]), axis=0, keepdims=True)
    for span in range(1, len(spans)):
        top = jnp.max(jnp.abs(far_ref[span]), axis=0, keepdims=True)
        largest = jnp.maximum(largest, top)
    largest = jnp.max(jnp.broadcast_to(largest, (8, width)), axis=1, keepdims=True)
    power = jnp.floor(jnp.log2(jnp.maximum(largest, 2.0**LEAST_POWER))) - TOP_POWER
    factor = jnp.exp2(-power)[0:1]
    for span in range(len(spans)):
        scaled_ref[span * width : (span + 1) * width] = far_ref[span] * factor
    scaled_ref[len(spans) * width :] = jnp.broadcast_to(power[0:1], (16, width))


def pick_kernel(*refs):
    count = len(refs) // 2
    for got_ref, pick_ref in zip(refs[:count], refs[count + 1 :]):
        pick_ref[...] = got_ref[1]


def join_kernel(chunk, slot_count, near_ref, far_ref, *refs):
    out_hbm, sum_ref, sems = refs[-3:]
    width = near_ref.shape[1]
    spans = spans_of(chunk, slot_count)
    factor = jnp.exp2(far_ref[len(spans) * width : len(spans) * width + 1])
    copies = []
    for at, offset in enumerate(spans):
        sum_ref[at] = near_ref[at] + far_ref[at * width : (at + 1) * width] * factor
        copies.append(
            pltpu.make_async_copy(
                sum_ref.at[at], out_hbm.at[offset + slot_count - 1], sems.at[at]
            )
        )
        copies[-1].start()
    for copy in copies:
        copy.wait()


def shards(solve_cols, region_groups):
    region_count, row_count, col_count = solve_cols.shape
    slot_count = region_groups.shape[1]
    width = col_count // slot_count
    total_groups = lax.axis_size("group")
    half = region_count * slot_count
    span_count = 2 * slot_count - 1
    pair_count = half // CORES
    params = pltpu.CompilerParams(vmem_limit_bytes=VMEM_BYTES)

    def permute(values, step):
        pairs = [(d, d ^ step) for d in range(total_groups)]
        return lax.ppermute(values, "group", pairs)

    rows = [
        jax.ShapeDtypeStruct(
            (CORES, len(turns_of(chunk, slot_count)), width, width), jnp.bfloat16
        )
        for chunk in range(CHUNKS)
    ]
    sends = pl.pallas_call(
        functools.partial(gram_kernel, total_groups, half),
        in_specs=[pl.BlockSpec(memory_space=pltpu.HBM)] * 2,
        out_specs=[pl.BlockSpec(memory_space=pltpu.VMEM)] * (pair_count * CHUNKS),
        out_shape=rows * pair_count,
        scratch_shapes=[
            pltpu.SMEM(region_groups.shape, region_groups.dtype),
            pltpu.VMEM(solve_cols.shape, solve_cols.dtype),
            pltpu.VMEM((half, slot_count, width, width), solve_cols.dtype),
            pltpu.SemaphoreType.DMA,
            pltpu.SemaphoreType.DMA((region_count,)),
        ],
        compiler_params=params,
        name="gram_rows",
    )(
        pltpu.with_memory_space_constraint(region_groups, pltpu.HBM),
        pltpu.with_memory_space_constraint(solve_cols, pltpu.HBM),
    )

    near, far, tagged = [], [], []
    has_core = (True,) * pair_count + (False,) * pair_count
    for chunk in range(CHUNKS):
        gots = [sends[chunk]] + [
            permute(sends[pair * CHUNKS + chunk], CORES * pair)
            for pair in range(pair_count - 1, 0, -1)
        ]
        if chunk == 0:
            picks = [got[1] for got in gots]
        else:
            vmem = pl.BlockSpec(memory_space=pltpu.VMEM)
            picks = pl.pallas_call(
                pick_kernel,
                in_specs=[vmem] * pair_count + [pl.BlockSpec(memory_space=pl.ANY)],
                out_specs=[vmem] * pair_count,
                out_shape=[jax.ShapeDtypeStruct(gots[0].shape[1:], gots[0].dtype)] * pair_count,
                compiler_params=params,
                name="pick_units",
            )(*gots, far_chunk)
        gots = gots + [permute(pick, 1) for pick in picks]
        tagged = tagged or gots
        spans = spans_of(chunk, slot_count)
        part = jax.ShapeDtypeStruct((len(spans), width, width), jnp.float32)
        scaled = jax.ShapeDtypeStruct((len(spans) * width + 16, width), jnp.float32)
        near_chunk, far_chunk = pl.pallas_call(
            functools.partial(sum_kernel, chunk, slot_count, has_core),
            out_shape=(part, scaled),
            scratch_shapes=[pltpu.VMEM(part.shape, part.dtype)],
            compiler_params=params,
            name="sum_offsets",
        )(*(tagged if chunk == 0 else tagged + gots))
        near.append(near_chunk)

        far.append(permute(far_chunk.astype(jnp.float16), half))

    schur = ()
    for chunk in range(CHUNKS):
        vmem = pl.BlockSpec(memory_space=pltpu.VMEM)
        hbm = pl.BlockSpec(memory_space=pltpu.HBM)
        schur = (
            pl.pallas_call(
                functools.partial(join_kernel, chunk, slot_count),
                in_specs=[vmem, vmem] + [hbm] * len(schur),
                out_specs=hbm,
                out_shape=jax.ShapeDtypeStruct((span_count, width, width), jnp.float32),
                input_output_aliases={2: 0} if schur else {},
                scratch_shapes=[
                    pltpu.VMEM(near[chunk].shape, jnp.float32),
                    pltpu.SemaphoreType.DMA((near[chunk].shape[0],)),
                ],
                cost_estimate=pl.CostEstimate(
                    flops=0, bytes_accessed=JOIN_WEIGHT, transcendentals=0
                ),
                compiler_params=params,
                name="join_offsets",
            )(near[chunk], far[chunk].astype(jnp.float32), *schur),
        )
    return schur[0][None]


def solution(mesh):
    return jax.shard_map(
        shards,
        mesh=mesh,
        in_specs=(P(("parts", "group"), None, None), P("group", None)),
        out_specs=P(("parts", "group"), None, None, None),
        check_vma=False,
    )
```

```python
import functools

import jax
import jax.numpy as jnp
from jax import lax
from jax.experimental import pallas as pl
from jax.experimental.pallas import tpu as pltpu
from jax.sharding import PartitionSpec as P

VMEM_BYTES = 48 * 1024 * 1024
LEAST_POWER = -100.0
TOP_POWER = 13.0
CHUNKS = 2
CORES = 2


def gram_kernel(total_groups, half, groups_hbm, cols_hbm, *refs):
    groups_ref, cols_ref, rows_ref, groups_sem, cols_sems = refs[-5:]
    send_refs = refs[:-5]
    region_count, slot_count = groups_ref.shape
    width = cols_ref.shape[2] // slot_count
    me = lax.axis_index("group")
    my_half, my_slot = me // half, lax.rem(me, half)
    groups_copy = pltpu.make_async_copy(groups_hbm, groups_ref, groups_sem)
    groups_copy.start()

    def cols_copy(region):
        return pltpu.make_async_copy(
            cols_hbm.at[region], cols_ref.at[region], cols_sems.at[region]
        )

    for region in range(region_count):
        cols_copy(region).start()
    groups_copy.wait()
    row = lax.broadcasted_iota(jnp.int32, (width, width), 0)
    col = lax.broadcasted_iota(jnp.int32, (width, width), 1)

    def add_region(region, carry):
        cols_copy(region).wait()
        cols = cols_ref[region]
        gram = lax.dot_general(
            cols, cols, (((0,), (0,)), ((), ())), preferred_element_type=jnp.float32
        )
        groups = [groups_ref[region, s] for s in range(slot_count)]

        def ahead(s, t):
            return lax.rem(groups[t] - groups[s] + total_groups, total_groups)

        for s in range(slot_count):
            place = 0
            for t in range(slot_count):
                if t != s:
                    place = place + (ahead(t, s) < slot_count).astype(jnp.int32)
            away = (groups[s] // half != my_half).astype(jnp.int32)
            tag = (place + slot_count * away).astype(jnp.float32)
            slot = lax.rem(groups[s], half) ^ my_slot
            for t in range(slot_count):
                block = gram[s * width : (s + 1) * width, t * width : (t + 1) * width]
                if t == s:
                    block = jnp.where((row == width - 1) & (col < width - 1), tag, block)
                    turn = 0
                else:
                    gap = ahead(s, t)
                    turn = jnp.where(gap < slot_count, gap, gap - total_groups + slot_count)
                rows_ref[slot, turn] = block.astype(rows_ref.dtype)
        return carry

    lax.fori_loop(0, region_count, add_region, 0, unroll=region_count <= 2)
    for at, send_ref in enumerate(send_refs):
        turns = turns_of(at // CORES, slot_count)
        for pair in range(send_ref.shape[0]):
            send_ref[pair] = rows_ref[CORES * pair + at % CORES, turns[0] : turns[-1] + 1]


def turns_of(chunk, slot_count):
    size = slot_count // CHUNKS
    return range(chunk * size, (chunk + 1) * size)


def spans_of(chunk, slot_count):
    turns = turns_of(chunk, slot_count)
    return [o for t in turns for o in ([t, t - slot_count] if t else [0])]


def pieces_of(chunk, slot_count):
    places = list(range(len(spans_of(chunk, slot_count))))
    size = len(spans_of(0, slot_count))
    while chunk and len(places) % size:
        size -= 1
    return [places[at : at + size] for at in range(0, len(places), size)]


def sum_kernel(chunk, slot_count, *refs):
    pieces = pieces_of(chunk, slot_count)
    arrays, near_ref, scaled_refs, far_ref = (
        refs[: -2 - len(pieces)],
        refs[-2 - len(pieces)],
        refs[-1 - len(pieces) : -1],
        refs[-1],
    )
    width = near_ref.shape[1]
    turns, spans = turns_of(chunk, slot_count), spans_of(chunk, slot_count)
    near_ref[...] = jnp.zeros_like(near_ref)
    far_ref[...] = jnp.zeros_like(far_ref)

    def units(arrays):
        return [arrays[0].at[0], arrays[1].at[0]] + [
            x.at[core] for x in arrays[2:] for core in range(CORES)
        ]

    count = len(arrays) if chunk == 0 else len(arrays) // 2
    for tag_ref, got_ref in zip(units(arrays[:count]), units(arrays[-count:])):
        tag = jnp.max(
            tag_ref[0, width - 16 : width, 0:width].astype(jnp.float32)[15:16, 0:1]
        ).astype(jnp.int32)
        away = tag // slot_count
        place = tag - slot_count * away

        def add(into_ref):
            for turn in turns:
                at = spans.index(turn)
                if turn:
                    at = at + (place + turn >= slot_count).astype(jnp.int32)
                into_ref[at] += got_ref[turn - turns[0]].astype(jnp.float32)

        pl.when(away == 0)(lambda: add(near_ref))
        pl.when(away != 0)(lambda: add(far_ref))

    if chunk == 0:
        row = lax.broadcasted_iota(jnp.int32, (width, width), 0)
        col = lax.broadcasted_iota(jnp.int32, (width, width), 1)
        for into_ref in (near_ref, far_ref):
            block = into_ref[0]
            into_ref[0] = jnp.where((row == width - 1) & (col < width - 1), block.T, block)

    largest = jnp.max(jnp.abs(far_ref[0]), axis=0, keepdims=True)
    for span in range(1, len(spans)):
        top = jnp.max(jnp.abs(far_ref[span]), axis=0, keepdims=True)
        largest = jnp.maximum(largest, top)
    largest = jnp.max(jnp.broadcast_to(largest, (8, width)), axis=1, keepdims=True)
    power = jnp.floor(jnp.log2(jnp.maximum(largest, 2.0**LEAST_POWER))) - TOP_POWER
    factor = jnp.exp2(-power)[0:1]
    for scaled_ref, places in zip(scaled_refs, pieces):
        for at, place in enumerate(places):
            scaled_ref[at * width : (at + 1) * width] = far_ref[place] * factor
        scaled_ref[len(places) * width :] = jnp.broadcast_to(power[0:1], (16, width))


def merge_kernel(keep_ref, got_ref, *send_refs):
    for at, send_ref in enumerate(send_refs):
        send_ref[0] = keep_ref[at + 1]
        send_ref[1] = got_ref[at + 1]


def join_kernel(chunk, slot_count, near_ref, *refs):
    pieces = pieces_of(chunk, slot_count)
    far_refs = refs[: len(pieces)]
    out_hbm, sum_ref, sems = refs[-3:]
    width = near_ref.shape[1]
    spans = spans_of(chunk, slot_count)
    copies = []
    for far_ref, places in zip(far_refs, pieces):
        factor = jnp.exp2(far_ref[len(places) * width : len(places) * width + 1])
        for at, place in enumerate(places):
            far = far_ref[at * width : (at + 1) * width] * factor
            sum_ref[place] = near_ref[place] + far
            copies.append(
                pltpu.make_async_copy(
                    sum_ref.at[place],
                    out_hbm.at[spans[place] + slot_count - 1],
                    sems.at[place],
                )
            )
            copies[-1].start()
    for copy in copies:
        copy.wait()


def shards(solve_cols, region_groups):
    region_count, row_count, col_count = solve_cols.shape
    slot_count = region_groups.shape[1]
    width = col_count // slot_count
    total_groups = lax.axis_size("group")
    half = region_count * slot_count
    span_count = 2 * slot_count - 1
    pair_count = half // CORES
    params = pltpu.CompilerParams(vmem_limit_bytes=VMEM_BYTES)
    light = pl.CostEstimate(flops=0, bytes_accessed=0, transcendentals=0)
    vmem = pl.BlockSpec(memory_space=pltpu.VMEM)
    hbm = pl.BlockSpec(memory_space=pltpu.HBM)

    def permute(values, step):
        pairs = [(d, d ^ step) for d in range(total_groups)]
        return lax.ppermute(values, "group", pairs)

    def blocks(count, chunk):
        turns = turns_of(chunk, slot_count)
        return jax.ShapeDtypeStruct((count, len(turns), width, width), solve_cols.dtype)

    sends = pl.pallas_call(
        functools.partial(gram_kernel, total_groups, half),
        in_specs=[hbm] * 2,
        out_specs=[vmem] * (CHUNKS * CORES),
        out_shape=[
            blocks(pair_count, chunk) for chunk in range(CHUNKS) for core in range(CORES)
        ],
        scratch_shapes=[
            pltpu.SMEM(region_groups.shape, region_groups.dtype),
            pltpu.VMEM(solve_cols.shape, solve_cols.dtype),
            pltpu.VMEM((half, slot_count, width, width), solve_cols.dtype),
            pltpu.SemaphoreType.DMA,
            pltpu.SemaphoreType.DMA((region_count,)),
        ],
        cost_estimate=light,
        compiler_params=params,
        name="gram_rows",
    )(
        pltpu.with_memory_space_constraint(region_groups, pltpu.HBM),
        pltpu.with_memory_space_constraint(solve_cols, pltpu.HBM),
    )

    near, far, tagged = [], [], []
    for chunk in range(CHUNKS):
        keep, give = sends[CORES * chunk : CORES * (chunk + 1)]
        gots = [keep, permute(give, 1)]
        merged = pl.pallas_call(
            merge_kernel,
            out_shape=[blocks(CORES, chunk)] * (pair_count - 1),
            cost_estimate=light,
            compiler_params=params,
            name="merge_units",
        )(*gots)
        for pair in range(pair_count - 1, 0, -1):
            gots.append(permute(merged[pair - 1], CORES * pair))
        tagged = tagged or gots
        spans, pieces = spans_of(chunk, slot_count), pieces_of(chunk, slot_count)
        part = jax.ShapeDtypeStruct((len(spans), width, width), jnp.float32)
        near_chunk, *scaled = pl.pallas_call(
            functools.partial(sum_kernel, chunk, slot_count),
            out_shape=[part]
            + [jax.ShapeDtypeStruct((len(p) * width + 16, width), jnp.float32) for p in pieces],
            scratch_shapes=[pltpu.VMEM(part.shape, part.dtype)],
            cost_estimate=light,
            compiler_params=params,
            name="sum_offsets",
        )(*(tagged if chunk == 0 else tagged + gots))
        near.append(near_chunk)
        far.append([permute(piece.astype(jnp.float16), half) for piece in scaled])

    schur = ()
    for chunk in range(CHUNKS):
        schur = (
            pl.pallas_call(
                functools.partial(join_kernel, chunk, slot_count),
                in_specs=[vmem] * (1 + len(far[chunk])) + [hbm] * len(schur),
                out_specs=hbm,
                out_shape=jax.ShapeDtypeStruct((span_count, width, width), jnp.float32),
                input_output_aliases={1 + len(far[chunk]): 0} if schur else {},
                scratch_shapes=[
                    pltpu.VMEM(near[chunk].shape, jnp.float32),
                    pltpu.SemaphoreType.DMA((near[chunk].shape[0],)),
                ],
                cost_estimate=light,
                compiler_params=params,
                name="join_offsets",
            )(near[chunk], *[piece.astype(jnp.float32) for piece in far[chunk]], *schur),
        )
    return schur[0][None]


def solution(mesh):
    return jax.shard_map(
        shards,
        mesh=mesh,
        in_specs=(P(("parts", "group"), None, None), P("group", None)),
        out_specs=P(("parts", "group"), None, None, None),
        check_vma=False,
    )
```

```python
import functools

import jax
import jax.numpy as jnp
from jax import lax
from jax.experimental import pallas as pl
from jax.experimental.pallas import tpu as pltpu
from jax.sharding import PartitionSpec as P

VMEM_BYTES = 48 * 1024 * 1024
LEAST_POWER = -100.0
TOP_POWER = 13.0
CHUNKS = 2
CORES = 2
COPIES = 4


def gram_kernel(total_groups, half, groups_hbm, cols_hbm, *refs):
    groups_ref, cols_ref, rows_ref, groups_sem, cols_sems = refs[-5:]
    send_refs = refs[:-5]
    region_count, slot_count = groups_ref.shape
    width = cols_ref.shape[2] // slot_count
    me = lax.axis_index("group")
    my_half, my_slot = me // half, lax.rem(me, half)
    groups_copy = pltpu.make_async_copy(groups_hbm, groups_ref, groups_sem)
    groups_copy.start()

    depth = cols_ref.shape[1] // COPIES

    def cols_copy(region, part):
        rows = pl.ds(part * depth, depth)
        return pltpu.make_async_copy(
            cols_hbm.at[region, rows], cols_ref.at[region, rows], cols_sems.at[region, part]
        )

    for region in range(region_count):
        for part in range(COPIES):
            cols_copy(region, part).start()
    groups_copy.wait()
    row = lax.broadcasted_iota(jnp.int32, (width, width), 0)
    col = lax.broadcasted_iota(jnp.int32, (width, width), 1)

    def add_region(region, carry):
        for part in range(COPIES):
            cols_copy(region, part).wait()
        cols = cols_ref[region]
        gram = lax.dot_general(
            cols, cols, (((0,), (0,)), ((), ())), preferred_element_type=jnp.float32
        )
        groups = [groups_ref[region, s] for s in range(slot_count)]

        def ahead(s, t):
            return lax.rem(groups[t] - groups[s] + total_groups, total_groups)

        for s in range(slot_count):
            place = 0
            for t in range(slot_count):
                if t != s:
                    place = place + (ahead(t, s) < slot_count).astype(jnp.int32)
            away = (groups[s] // half != my_half).astype(jnp.int32)
            tag = (place + slot_count * away).astype(jnp.float32)
            slot = lax.rem(groups[s], half) ^ my_slot
            for t in range(slot_count):
                block = gram[s * width : (s + 1) * width, t * width : (t + 1) * width]
                if t == s:
                    block = jnp.where((row == width - 1) & (col < width - 1), tag, block)
                    turn = 0
                else:
                    gap = ahead(s, t)
                    turn = jnp.where(gap < slot_count, gap, gap - total_groups + slot_count)
                rows_ref[slot, turn] = block.astype(rows_ref.dtype)
        return carry

    lax.fori_loop(0, region_count, add_region, 0, unroll=region_count <= 2)
    for at, send_ref in enumerate(send_refs):
        turns = turns_of(at // CORES, slot_count)
        for pair in range(send_ref.shape[0]):
            send_ref[pair] = rows_ref[CORES * pair + at % CORES, turns[0] : turns[-1] + 1]


def turns_of(chunk, slot_count):
    last = slot_count - 1
    return range(last) if chunk == 0 else range(last, slot_count)


def spans_of(chunk, slot_count):
    turns = turns_of(chunk, slot_count)
    return [o for t in turns for o in ([t, t - slot_count] if t else [0])]


def pieces_of(chunk, slot_count):
    count = len(spans_of(chunk, slot_count))
    size = len(spans_of(1, slot_count))
    starts = range(count % size, count, size)
    pieces = [range(0 if at == starts[0] else at, at + size) for at in starts]
    return pieces, 16 * (CHUNKS - chunk)


def sum_kernel(chunk, slot_count, *refs):
    pieces, tail = pieces_of(chunk, slot_count)
    arrays, scaled_refs = refs[: -1 - len(pieces)], refs[-len(pieces) :]
    sums_ref = refs[-1 - len(pieces)]
    width = sums_ref.shape[1]
    turns, spans = turns_of(chunk, slot_count), spans_of(chunk, slot_count)
    count = len(spans)
    sums_ref[...] = jnp.zeros_like(sums_ref)

    def units(arrays):
        return [(arrays[0], 0), (arrays[1], 0)] + [
            (x, core) for x in arrays[2:] for core in range(CORES)
        ]

    array_count = len(arrays) if chunk == 0 else len(arrays) // 2
    tags = [
        jnp.max(
            ref[at, 0, width - 16 : width, 0:width].astype(jnp.float32)[15:16, 0:1]
        ).astype(jnp.int32)
        for ref, at in units(arrays[:array_count])
    ]
    for tag, (ref, at) in zip(tags, units(arrays[-array_count:])):
        away = tag // slot_count
        place = tag - slot_count * away
        for turn in turns:
            to = count * away + spans.index(turn)
            if turn:
                to = to + (place + turn >= slot_count).astype(jnp.int32)
            sums_ref[to] += ref[at, turn - turns[0]].astype(jnp.float32)

    if chunk == 0:
        row = lax.broadcasted_iota(jnp.int32, (width, width), 0)
        col = lax.broadcasted_iota(jnp.int32, (width, width), 1)
        for at in (0, count):
            block = sums_ref[at]
            sums_ref[at] = jnp.where((row == width - 1) & (col < width - 1), block.T, block)

    tops = jnp.max(jnp.abs(sums_ref[count]), axis=0, keepdims=True)
    for at in range(1, count):
        tops = jnp.maximum(tops, jnp.max(jnp.abs(sums_ref[count + at]), axis=0, keepdims=True))
    largest = jnp.max(jnp.broadcast_to(tops, (8, width)), axis=1, keepdims=True)
    power = jnp.floor(jnp.log2(jnp.maximum(largest, 2.0**LEAST_POWER))) - TOP_POWER
    factor = jnp.exp2(-power)[0:1]
    for scaled_ref, piece in zip(scaled_refs, pieces):
        for at, place in enumerate(piece):
            scaled_ref[at * width : (at + 1) * width] = sums_ref[count + place] * factor
        scaled_ref[len(piece) * width :] = jnp.broadcast_to(power[0:1], (tail, width))


def merge_kernel(keep_ref, got_ref, *send_refs):
    for at, send_ref in enumerate(send_refs):
        send_ref[0] = keep_ref[at + 1]
        send_ref[1] = got_ref[at + 1]


def join_kernel(chunk, slot_count, sums_ref, *refs):
    pieces, _ = pieces_of(chunk, slot_count)
    out_hbm, joined_ref, sems = refs[-3:]
    width = sums_ref.shape[1]
    spans = spans_of(chunk, slot_count)
    copies = []
    for far_ref, piece in zip(refs, pieces):
        factor = jnp.exp2(far_ref[len(piece) * width : len(piece) * width + 1])
        for at, place in enumerate(piece):
            far = far_ref[at * width : (at + 1) * width] * factor
            joined_ref[place] = sums_ref[place] + far
            copies.append(
                pltpu.make_async_copy(
                    joined_ref.at[place],
                    out_hbm.at[spans[place] + slot_count - 1],
                    sems.at[place],
                )
            )
            copies[-1].start()
    for copy in copies:
        copy.wait()


def shards(solve_cols, region_groups):
    region_count, row_count, col_count = solve_cols.shape
    slot_count = region_groups.shape[1]
    width = col_count // slot_count
    total_groups = lax.axis_size("group")
    half = region_count * slot_count
    span_count = 2 * slot_count - 1
    pair_count = half // CORES
    params = pltpu.CompilerParams(vmem_limit_bytes=VMEM_BYTES)
    light = pl.CostEstimate(flops=0, bytes_accessed=0, transcendentals=0)
    vmem = pl.BlockSpec(memory_space=pltpu.VMEM)
    hbm = pl.BlockSpec(memory_space=pltpu.HBM)

    def permute(values, step):
        pairs = [(d, d ^ step) for d in range(total_groups)]
        return lax.ppermute(values, "group", pairs)

    def blocks(count, chunk):
        turns = turns_of(chunk, slot_count)
        return jax.ShapeDtypeStruct((count, len(turns), width, width), solve_cols.dtype)

    sends = pl.pallas_call(
        functools.partial(gram_kernel, total_groups, half),
        in_specs=[hbm] * 2,
        out_specs=[vmem] * (CHUNKS * CORES),
        out_shape=[
            blocks(pair_count, chunk) for chunk in range(CHUNKS) for core in range(CORES)
        ],
        scratch_shapes=[
            pltpu.SMEM(region_groups.shape, region_groups.dtype),
            pltpu.VMEM(solve_cols.shape, solve_cols.dtype),
            pltpu.VMEM((half, slot_count, width, width), solve_cols.dtype),
            pltpu.SemaphoreType.DMA,
            pltpu.SemaphoreType.DMA((region_count, COPIES)),
        ],
        cost_estimate=light,
        compiler_params=params,
        name="gram_rows",
    )(
        pltpu.with_memory_space_constraint(region_groups, pltpu.HBM),
        pltpu.with_memory_space_constraint(solve_cols, pltpu.HBM),
    )

    sums, far, tagged = [], [], []
    for chunk in range(CHUNKS):
        keep, give = sends[CORES * chunk : CORES * (chunk + 1)]
        gots = [keep, permute(give, 1)]
        merged = pl.pallas_call(
            merge_kernel,
            out_shape=[blocks(CORES, chunk)] * (pair_count - 1),
            cost_estimate=light,
            compiler_params=params,
            name="merge_units",
        )(*gots)
        for pair in range(pair_count - 1, 0, -1):
            gots.append(permute(merged[pair - 1], CORES * pair))
        tagged = tagged or gots
        count = len(spans_of(chunk, slot_count))
        pieces, tail = pieces_of(chunk, slot_count)
        sums_chunk, *scaled = pl.pallas_call(
            functools.partial(sum_kernel, chunk, slot_count),
            out_shape=[jax.ShapeDtypeStruct((2 * count, width, width), jnp.float32)]
            + [
                jax.ShapeDtypeStruct((len(piece) * width + tail, width), jnp.float32)
                for piece in pieces
            ],
            cost_estimate=light,
            compiler_params=params,
            name="sum_offsets",
        )(*(tagged if chunk == 0 else tagged + gots))
        sums.append(sums_chunk)
        far.append([permute(piece.astype(jnp.float16), half) for piece in scaled])

    schur = ()
    for chunk in range(CHUNKS):
        count = len(spans_of(chunk, slot_count))
        schur = (
            pl.pallas_call(
                functools.partial(join_kernel, chunk, slot_count),
                in_specs=[vmem] * (1 + len(far[chunk])) + [hbm] * len(schur),
                out_specs=hbm,
                out_shape=jax.ShapeDtypeStruct((span_count, width, width), jnp.float32),
                input_output_aliases={1 + len(far[chunk]): 0} if schur else {},
                scratch_shapes=[
                    pltpu.VMEM((count, width, width), jnp.float32),
                    pltpu.SemaphoreType.DMA((count,)),
                ],
                cost_estimate=light,
                compiler_params=params,
                name="join_offsets",
            )(sums[chunk], *[piece.astype(jnp.float32) for piece in far[chunk]], *schur),
        )
    return schur[0][None]


def solution(mesh):
    return jax.shard_map(
        shards,
        mesh=mesh,
        in_specs=(P(("parts", "group"), None, None), P("group", None)),
        out_specs=P(("parts", "group"), None, None, None),
        check_vma=False,
    )
```

```python
import functools

import jax
import jax.numpy as jnp
from jax import lax
from jax.experimental import pallas as pl
from jax.experimental.pallas import tpu as pltpu
from jax.sharding import PartitionSpec as P

VMEM_BYTES = 48 * 1024 * 1024
LEAST_POWER = -100.0
TOP_POWER = 13.0
CHUNKS = 3
CORES = 2
COPIES = 4


def gram_kernel(total_groups, half, groups_hbm, cols_hbm, *refs):
    groups_ref, cols_ref, rows_ref, groups_sem, cols_sems = refs[-5:]
    send_refs = refs[:-5]
    region_count, slot_count = groups_ref.shape
    width = cols_ref.shape[2] // slot_count
    me = lax.axis_index("group")
    my_half, my_slot = me // half, lax.rem(me, half)
    groups_copy = pltpu.make_async_copy(groups_hbm, groups_ref, groups_sem)
    groups_copy.start()

    depth = cols_ref.shape[1] // COPIES

    def cols_copy(region, part):
        rows = pl.ds(part * depth, depth)
        return pltpu.make_async_copy(
            cols_hbm.at[region, rows], cols_ref.at[region, rows], cols_sems.at[region, part]
        )

    for region in range(region_count):
        for part in range(COPIES):
            cols_copy(region, part).start()
    groups_copy.wait()
    row = lax.broadcasted_iota(jnp.int32, (width, width), 0)
    col = lax.broadcasted_iota(jnp.int32, (width, width), 1)

    def add_region(region, carry):
        for part in range(COPIES):
            cols_copy(region, part).wait()
        cols = cols_ref[region]
        gram = lax.dot_general(
            cols, cols, (((0,), (0,)), ((), ())), preferred_element_type=jnp.float32
        )
        groups = [groups_ref[region, s] for s in range(slot_count)]

        def ahead(s, t):
            return lax.rem(groups[t] - groups[s] + total_groups, total_groups)

        for s in range(slot_count):
            place = 0
            for t in range(slot_count):
                if t != s:
                    place = place + (ahead(t, s) < slot_count).astype(jnp.int32)
            away = (groups[s] // half != my_half).astype(jnp.int32)
            tag = (place + slot_count * away).astype(jnp.float32)
            slot = lax.rem(groups[s], half) ^ my_slot
            for t in range(slot_count):
                block = gram[s * width : (s + 1) * width, t * width : (t + 1) * width]
                if t == s:
                    block = jnp.where((row == width - 1) & (col < width - 1), tag, block)
                    turn = 0
                else:
                    gap = ahead(s, t)
                    turn = jnp.where(gap < slot_count, gap, gap - total_groups + slot_count)
                rows_ref[slot, turn] = block.astype(rows_ref.dtype)
        return carry

    lax.fori_loop(0, region_count, add_region, 0, unroll=region_count <= 2)
    for at, send_ref in enumerate(send_refs):
        first, last = groups_of_chunks(slot_count)[at // CORES]
        for pair in range(send_ref.shape[0]):
            send_ref[pair] = rows_ref[CORES * pair + at % CORES, first:last]


def turns_of(chunk, slot_count):
    last = slot_count - CHUNKS + 1
    return range(last) if chunk == 0 else range(last + chunk - 1, last + chunk)


def groups_of_chunks(slot_count):
    last = slot_count - CHUNKS + 1
    return [(0, last), (last, slot_count)]


def spans_of(chunk, slot_count):
    turns = turns_of(chunk, slot_count)
    return [o for t in turns for o in ([t, t - slot_count] if t else [0])]


def tail_of(chunk):
    return 16 * (CHUNKS - chunk)


def sum_kernel(chunk, slot_count, *refs):
    arrays, (sums_ref, scaled_ref) = refs[:-2], refs[-2:]
    width = sums_ref.shape[1]
    turns, spans = turns_of(chunk, slot_count), spans_of(chunk, slot_count)
    group = turns[0] - groups_of_chunks(slot_count)[min(chunk, 1)][0]
    count = len(spans)
    sums_ref[...] = jnp.zeros_like(sums_ref)

    def units(arrays, group):
        return [(arrays[0], 0, group), (arrays[1], 0, group)] + [
            (x, core, 0) for x in arrays[2:] for core in range(CORES)
        ]

    array_count = len(arrays) if chunk == 0 else len(arrays) // 2
    tags = [
        jnp.max(
            ref[at, 0, width - 16 : width, 0:width].astype(jnp.float32)[15:16, 0:1]
        ).astype(jnp.int32)
        for ref, at, _ in units(arrays[:array_count], 0)
    ]
    for tag, (ref, at, first) in zip(tags, units(arrays[-array_count:], group)):
        away = tag // slot_count
        place = tag - slot_count * away
        for turn in turns:
            to = count * away + spans.index(turn)
            if turn:
                to = to + (place + turn >= slot_count).astype(jnp.int32)
            sums_ref[to] += ref[at, first + turn - turns[0]].astype(jnp.float32)

    if chunk == 0:
        row = lax.broadcasted_iota(jnp.int32, (width, width), 0)
        col = lax.broadcasted_iota(jnp.int32, (width, width), 1)
        for at in (0, count):
            block = sums_ref[at]
            sums_ref[at] = jnp.where((row == width - 1) & (col < width - 1), block.T, block)

    tops = jnp.max(jnp.abs(sums_ref[count]), axis=0, keepdims=True)
    for at in range(1, count):
        tops = jnp.maximum(tops, jnp.max(jnp.abs(sums_ref[count + at]), axis=0, keepdims=True))
    largest = jnp.max(jnp.broadcast_to(tops, (8, width)), axis=1, keepdims=True)
    power = jnp.floor(jnp.log2(jnp.maximum(largest, 2.0**LEAST_POWER))) - TOP_POWER
    factor = jnp.exp2(-power)[0:1]
    for at in range(count):
        scaled_ref[at * width : (at + 1) * width] = sums_ref[count + at] * factor
    scaled_ref[count * width :] = jnp.broadcast_to(power[0:1], (tail_of(chunk), width))


def merge_kernel(chunks, slot_count, keep_ref, got_ref, *send_refs):
    base = turns_of(chunks[0], slot_count)[0]
    pairs = len(send_refs) // len(chunks)
    for at, send_ref in enumerate(send_refs):
        turns = turns_of(chunks[at // pairs], slot_count)
        for core, ref in enumerate((keep_ref, got_ref)):
            send_ref[core] = ref[at % pairs + 1, turns[0] - base : turns[-1] + 1 - base]


def join_kernel(slot_count, *refs):
    out_hbm, joined_ref, sems = refs[-3:]
    width = joined_ref.shape[1]
    copies = []
    for chunk in range(CHUNKS):
        sums_ref, far_ref = refs[2 * chunk : 2 * chunk + 2]
        spans = spans_of(chunk, slot_count)
        factor = jnp.exp2(far_ref[len(spans) * width : len(spans) * width + 1])
        for at, offset in enumerate(spans):
            to = offset + slot_count - 1
            joined_ref[to] = sums_ref[at] + far_ref[at * width : (at + 1) * width] * factor
            copies.append(
                pltpu.make_async_copy(joined_ref.at[to], out_hbm.at[to], sems.at[to])
            )
            copies[-1].start()
    for copy in copies:
        copy.wait()


def shards(solve_cols, region_groups):
    region_count, row_count, col_count = solve_cols.shape
    slot_count = region_groups.shape[1]
    width = col_count // slot_count
    total_groups = lax.axis_size("group")
    half = region_count * slot_count
    span_count = 2 * slot_count - 1
    pair_count = half // CORES
    params = pltpu.CompilerParams(vmem_limit_bytes=VMEM_BYTES)
    light = pl.CostEstimate(flops=0, bytes_accessed=0, transcendentals=0)
    vmem = pl.BlockSpec(memory_space=pltpu.VMEM)
    hbm = pl.BlockSpec(memory_space=pltpu.HBM)

    def permute(values, step):
        pairs = [(d, d ^ step) for d in range(total_groups)]
        return lax.ppermute(values, "group", pairs)

    def blocks(count, turn_count):
        return jax.ShapeDtypeStruct((count, turn_count, width, width), solve_cols.dtype)

    turn_groups = groups_of_chunks(slot_count)
    sends = pl.pallas_call(
        functools.partial(gram_kernel, total_groups, half),
        in_specs=[hbm] * 2,
        out_specs=[vmem] * (len(turn_groups) * CORES),
        out_shape=[
            blocks(pair_count, last - first) for first, last in turn_groups for _ in range(CORES)
        ],
        scratch_shapes=[
            pltpu.SMEM(region_groups.shape, region_groups.dtype),
            pltpu.VMEM(solve_cols.shape, solve_cols.dtype),
            pltpu.VMEM((half, slot_count, width, width), solve_cols.dtype),
            pltpu.SemaphoreType.DMA,
            pltpu.SemaphoreType.DMA((region_count, COPIES)),
        ],
        cost_estimate=light,
        compiler_params=params,
        name="gram_rows",
    )(
        pltpu.with_memory_space_constraint(region_groups, pltpu.HBM),
        pltpu.with_memory_space_constraint(solve_cols, pltpu.HBM),
    )

    gots = []
    for at, chunks in enumerate((range(1), range(1, CHUNKS))):
        keep, give = sends[CORES * at : CORES * (at + 1)]
        got = permute(give, 1)
        merged = pl.pallas_call(
            functools.partial(merge_kernel, chunks, slot_count),
            out_shape=[
                blocks(CORES, len(turns_of(chunk, slot_count)))
                for chunk in chunks
                for _ in range(pair_count - 1)
            ],
            cost_estimate=light,
            compiler_params=params,
            name="merge_units",
        )(keep, got)
        for place in range(len(chunks)):
            chips = merged[place * (pair_count - 1) : (place + 1) * (pair_count - 1)]
            gots.append([keep, got])
            for pair in range(pair_count - 1, 0, -1):
                gots[-1].append(permute(chips[pair - 1], CORES * pair))

    pieces = []
    for chunk in range(CHUNKS):
        count = len(spans_of(chunk, slot_count))
        sums, scaled = pl.pallas_call(
            functools.partial(sum_kernel, chunk, slot_count),
            out_shape=(
                jax.ShapeDtypeStruct((2 * count, width, width), jnp.float32),
                jax.ShapeDtypeStruct((count * width + tail_of(chunk), width), jnp.float32),
            ),
            cost_estimate=light,
            compiler_params=params,
            name="sum_offsets",
        )(*(gots[0] if chunk == 0 else gots[0] + gots[chunk]))
        far = permute(scaled.astype(jnp.float16), half)
        pieces += [sums, far.astype(jnp.float32)]

    return pl.pallas_call(
        functools.partial(join_kernel, slot_count),
        in_specs=[vmem] * len(pieces),
        out_specs=hbm,
        out_shape=jax.ShapeDtypeStruct((span_count, width, width), jnp.float32),
        scratch_shapes=[
            pltpu.VMEM((span_count, width, width), jnp.float32),
            pltpu.SemaphoreType.DMA((span_count,)),
        ],
        cost_estimate=light,
        compiler_params=params,
        name="join_offsets",
    )(*pieces)[None]


def solution(mesh):
    return jax.shard_map(
        shards,
        mesh=mesh,
        in_specs=(P(("parts", "group"), None, None), P("group", None)),
        out_specs=P(("parts", "group"), None, None, None),
        check_vma=False,
    )
```

```python
import functools

import jax
import jax.numpy as jnp
from jax import lax
from jax.experimental import pallas as pl
from jax.experimental.pallas import tpu as pltpu
from jax.sharding import PartitionSpec as P

VMEM_BYTES = 48 * 1024 * 1024
LEAST_POWER = -100.0
TOP_POWER = 13.0
CHUNKS = 2
CORES = 2
COPIES = 4


def gram_kernel(total_groups, half, groups_hbm, cols_hbm, *refs):
    groups_ref, cols_ref, rows_ref, groups_sem, cols_sems = refs[-5:]
    send_refs = refs[:-5]
    region_count, slot_count = groups_ref.shape
    width = cols_ref.shape[2] // slot_count
    me = lax.axis_index("group")
    my_half, my_slot = me // half, lax.rem(me, half)
    groups_copy = pltpu.make_async_copy(groups_hbm, groups_ref, groups_sem)
    groups_copy.start()

    depth = cols_ref.shape[1] // COPIES

    def cols_copy(region, part):
        rows = pl.ds(part * depth, depth)
        return pltpu.make_async_copy(
            cols_hbm.at[region, rows], cols_ref.at[region, rows], cols_sems.at[region, part]
        )

    for region in range(region_count):
        for part in range(COPIES):
            cols_copy(region, part).start()
    groups_copy.wait()
    row = lax.broadcasted_iota(jnp.int32, (width, width), 0)
    col = lax.broadcasted_iota(jnp.int32, (width, width), 1)

    def add_region(region, carry):
        for part in range(COPIES):
            cols_copy(region, part).wait()
        cols = cols_ref[region]
        gram = lax.dot_general(
            cols, cols, (((0,), (0,)), ((), ())), preferred_element_type=jnp.float32
        )
        groups = [groups_ref[region, s] for s in range(slot_count)]

        def ahead(s, t):
            return lax.rem(groups[t] - groups[s] + total_groups, total_groups)

        for s in range(slot_count):
            place = 0
            for t in range(slot_count):
                if t != s:
                    place = place + (ahead(t, s) < slot_count).astype(jnp.int32)
            away = (groups[s] // half != my_half).astype(jnp.int32)
            tag = (place + slot_count * away).astype(jnp.float32)
            slot = lax.rem(groups[s], half) ^ my_slot
            for t in range(slot_count):
                block = gram[s * width : (s + 1) * width, t * width : (t + 1) * width]
                if t == s:
                    block = jnp.where((row == width - 1) & (col < width - 1), tag, block)
                    turn = 0
                else:
                    gap = ahead(s, t)
                    turn = jnp.where(gap < slot_count, gap, gap - total_groups + slot_count)
                rows_ref[slot, turn] = block.astype(rows_ref.dtype)
        return carry

    lax.fori_loop(0, region_count, add_region, 0, unroll=region_count <= 2)
    for at, send_ref in enumerate(send_refs):
        turns = turns_of(at // CORES, slot_count)
        for pair in range(send_ref.shape[0]):
            send_ref[pair] = rows_ref[CORES * pair + at % CORES, turns[0] : turns[-1] + 1]


def turns_of(chunk, slot_count):
    size = slot_count // CHUNKS
    return range(chunk * size, (chunk + 1) * size)


def spans_of(chunk, slot_count):
    turns = turns_of(chunk, slot_count)
    return [o for t in turns for o in ([t, t - slot_count] if t else [0])]


def pieces_of(chunk, slot_count):
    count = len(spans_of(chunk, slot_count))
    size = count if chunk == 0 else count // 2
    return [range(at, at + size) for at in range(0, count, size)]


def sum_kernel(chunk, slot_count, *refs):
    pieces = pieces_of(chunk, slot_count)
    arrays, scaled_refs = refs[: -1 - len(pieces)], refs[-len(pieces) :]
    sums_ref = refs[-1 - len(pieces)]
    width = sums_ref.shape[1]
    turns, spans = turns_of(chunk, slot_count), spans_of(chunk, slot_count)
    count = len(spans)
    sums_ref[...] = jnp.zeros_like(sums_ref)

    def units(arrays):
        return [(arrays[0], 0), (arrays[1], 0)] + [
            (x, core) for x in arrays[2:] for core in range(CORES)
        ]

    array_count = len(arrays) if chunk == 0 else len(arrays) // 2
    tags = [
        jnp.max(
            ref[at, 0, width - 16 : width, 0:width].astype(jnp.float32)[15:16, 0:1]
        ).astype(jnp.int32)
        for ref, at in units(arrays[:array_count])
    ]
    for tag, (ref, at) in zip(tags, units(arrays[-array_count:])):
        away = tag // slot_count
        place = tag - slot_count * away
        for turn in turns:
            to = count * away + spans.index(turn)
            if turn:
                to = to + (place + turn >= slot_count).astype(jnp.int32)
            sums_ref[to] += ref[at, turn - turns[0]].astype(jnp.float32)

    if chunk == 0:
        row = lax.broadcasted_iota(jnp.int32, (width, width), 0)
        col = lax.broadcasted_iota(jnp.int32, (width, width), 1)
        for at in (0, count):
            block = sums_ref[at]
            sums_ref[at] = jnp.where((row == width - 1) & (col < width - 1), block.T, block)

    tops = jnp.max(jnp.abs(sums_ref[count]), axis=0, keepdims=True)
    for at in range(1, count):
        tops = jnp.maximum(tops, jnp.max(jnp.abs(sums_ref[count + at]), axis=0, keepdims=True))
    largest = jnp.max(jnp.broadcast_to(tops, (8, width)), axis=1, keepdims=True)
    power = jnp.floor(jnp.log2(jnp.maximum(largest, 2.0**LEAST_POWER))) - TOP_POWER
    factor = jnp.exp2(-power)[0:1]
    for scaled_ref, piece in zip(scaled_refs, pieces):
        for at, place in enumerate(piece):
            scaled_ref[at * width : (at + 1) * width] = sums_ref[count + place] * factor
        scaled_ref[len(piece) * width :] = jnp.broadcast_to(power[0:1], (16, width))


def merge_kernel(keep_ref, got_ref, *send_refs):
    for at, send_ref in enumerate(send_refs):
        send_ref[0] = keep_ref[at + 1]
        send_ref[1] = got_ref[at + 1]


def join_kernel(slot_count, *refs):
    out_hbm, joined_ref, sems = refs[-3:]
    width = joined_ref.shape[1]
    copies = []
    refs = list(refs[:-3])
    for chunk in range(CHUNKS):
        sums_ref, spans = refs.pop(0), spans_of(chunk, slot_count)
        for piece in pieces_of(chunk, slot_count):
            far_ref = refs.pop(0)
            factor = jnp.exp2(far_ref[len(piece) * width : len(piece) * width + 1])
            for at, place in enumerate(piece):
                to = spans[place] + slot_count - 1
                far = far_ref[at * width : (at + 1) * width] * factor
                joined_ref[to] = sums_ref[place] + far
                copies.append(
                    pltpu.make_async_copy(joined_ref.at[to], out_hbm.at[to], sems.at[to])
                )
                copies[-1].start()
    for copy in copies:
        copy.wait()


def shards(solve_cols, region_groups):
    region_count, row_count, col_count = solve_cols.shape
    slot_count = region_groups.shape[1]
    width = col_count // slot_count
    total_groups = lax.axis_size("group")
    half = region_count * slot_count
    span_count = 2 * slot_count - 1
    pair_count = half // CORES
    params = pltpu.CompilerParams(vmem_limit_bytes=VMEM_BYTES)
    light = pl.CostEstimate(flops=0, bytes_accessed=0, transcendentals=0)
    vmem = pl.BlockSpec(memory_space=pltpu.VMEM)
    hbm = pl.BlockSpec(memory_space=pltpu.HBM)

    def permute(values, step):
        pairs = [(d, d ^ step) for d in range(total_groups)]
        return lax.ppermute(values, "group", pairs)

    def blocks(count, chunk):
        turns = turns_of(chunk, slot_count)
        return jax.ShapeDtypeStruct((count, len(turns), width, width), solve_cols.dtype)

    sends = pl.pallas_call(
        functools.partial(gram_kernel, total_groups, half),
        in_specs=[hbm] * 2,
        out_specs=[vmem] * (CHUNKS * CORES),
        out_shape=[blocks(pair_count, chunk) for chunk in range(CHUNKS) for _ in range(CORES)],
        scratch_shapes=[
            pltpu.SMEM(region_groups.shape, region_groups.dtype),
            pltpu.VMEM(solve_cols.shape, solve_cols.dtype),
            pltpu.VMEM((half, slot_count, width, width), solve_cols.dtype),
            pltpu.SemaphoreType.DMA,
            pltpu.SemaphoreType.DMA((region_count, COPIES)),
        ],
        cost_estimate=light,
        compiler_params=params,
        name="gram_rows",
    )(
        pltpu.with_memory_space_constraint(region_groups, pltpu.HBM),
        pltpu.with_memory_space_constraint(solve_cols, pltpu.HBM),
    )

    pieces, tagged = [], []
    for chunk in range(CHUNKS):
        keep, give = sends[CORES * chunk : CORES * (chunk + 1)]
        gots = [keep, permute(give, 1)]
        merged = pl.pallas_call(
            merge_kernel,
            out_shape=[blocks(CORES, chunk)] * (pair_count - 1),
            cost_estimate=light,
            compiler_params=params,
            name="merge_units",
        )(*gots)
        for pair in range(pair_count - 1, 0, -1):
            gots.append(permute(merged[pair - 1], CORES * pair))
        tagged = tagged or gots
        count = len(spans_of(chunk, slot_count))
        sums, *scaled = pl.pallas_call(
            functools.partial(sum_kernel, chunk, slot_count),
            out_shape=[jax.ShapeDtypeStruct((2 * count, width, width), jnp.float32)]
            + [
                jax.ShapeDtypeStruct((len(piece) * width + 16, width), jnp.float32)
                for piece in pieces_of(chunk, slot_count)
            ],
            cost_estimate=light,
            compiler_params=params,
            name="sum_offsets",
        )(*(tagged if chunk == 0 else tagged + gots))
        pieces.append(sums)
        for far in scaled:
            pieces.append(permute(far.astype(jnp.float16), half).astype(jnp.float32))

    return pl.pallas_call(
        functools.partial(join_kernel, slot_count),
        in_specs=[vmem] * len(pieces),
        out_specs=hbm,
        out_shape=jax.ShapeDtypeStruct((span_count, width, width), jnp.float32),
        scratch_shapes=[
            pltpu.VMEM((span_count, width, width), jnp.float32),
            pltpu.SemaphoreType.DMA((span_count,)),
        ],
        cost_estimate=light,
        compiler_params=params,
        name="join_offsets",
    )(*pieces)[None]


def solution(mesh):
    return jax.shard_map(
        shards,
        mesh=mesh,
        in_specs=(P(("parts", "group"), None, None), P("group", None)),
        out_specs=P(("parts", "group"), None, None, None),
        check_vma=False,
    )
```

```python
import functools

import jax
import jax.numpy as jnp
from jax import lax
from jax.experimental import pallas as pl
from jax.experimental.pallas import tpu as pltpu
from jax.sharding import PartitionSpec as P

VMEM_BYTES = 48 * 1024 * 1024
LEAST_POWER = -100.0
TOP_POWER = 13.0
CHUNKS = 2
CORES = 2
COPIES = 2
TILE = 16


def packed_rows(width):
    return width // 2 + TILE


def unit_rows(width, slot_count):
    return packed_rows(width) + (slot_count - 1) * width


def parts_of(chunk, slot_count):
    halves = [(turn, at) for turn in range(1, slot_count) for at in range(2)]
    size = len(halves) // CHUNKS
    return halves[chunk * size : (chunk + 1) * size]


def row_range(chunk, width, slot_count):
    size = len(parts_of(chunk, slot_count)) * (width // 2)
    first = packed_rows(width) + chunk * size
    return (0 if chunk == 0 else first), first + size


def sum_rows(chunk, width, slot_count):
    count = 2 * len(parts_of(chunk, slot_count)) * (width // 2)
    return count + (packed_rows(width) if chunk == 0 else 0)


def half_iota(width):
    shape = (width // 2, width)
    return (
        lax.broadcasted_iota(jnp.int32, shape, 0),
        lax.broadcasted_iota(jnp.int32, shape, 1),
    )


def pack(block, tag):
    width = block.shape[1]
    half = width // 2
    row, col = half_iota(width)
    lower = pltpu.roll(block[half:], half, 1)
    packed = jnp.where((col >= half) | (row <= col), block[:half], lower)
    diagonal = jnp.sum(jnp.where(row == col, lower, 0.0), axis=0, keepdims=True)
    rest = jnp.where(col[:1] < half, diagonal, tag)
    return packed, jnp.broadcast_to(rest, (TILE, width))


def unpack(packed, diagonal):
    half, width = packed.shape
    row, col = half_iota(width)
    turned = jnp.concatenate([packed, jnp.zeros_like(packed)], axis=0).T
    upper = jnp.where((col >= half) | (row <= col), packed, turned[:half])
    last = jnp.where(row > col, packed, jnp.where(row < col, turned[:half], diagonal))
    return upper, jnp.where(col < half, turned[half:], pltpu.roll(last, half, 1))


def gram_kernel(total_groups, half, groups_hbm, cols_hbm, *refs):
    groups_ref, cols_ref, rows_ref, groups_sem, cols_sems = refs[-5:]
    send_refs = refs[:-5]
    region_count, slot_count = groups_ref.shape
    width = cols_ref.shape[2] // slot_count
    me = lax.axis_index("group")
    my_half, my_slot = me // half, lax.rem(me, half)
    groups_copy = pltpu.make_async_copy(groups_hbm, groups_ref, groups_sem)
    groups_copy.start()

    depth = cols_ref.shape[1] // COPIES

    def cols_copy(region, part):
        rows = pl.ds(part * depth, depth)
        return pltpu.make_async_copy(
            cols_hbm.at[region, rows], cols_ref.at[region, rows], cols_sems.at[region, part]
        )

    for region in range(region_count):
        for part in range(COPIES):
            cols_copy(region, part).start()
    groups_copy.wait()
    packed = packed_rows(width)

    def add_region(region, carry):
        for part in range(COPIES):
            cols_copy(region, part).wait()
        cols = cols_ref[region]
        gram = lax.dot_general(
            cols, cols, (((0,), (0,)), ((), ())), preferred_element_type=jnp.float32
        )
        groups = [groups_ref[region, s] for s in range(slot_count)]

        def ahead(s, t):
            return lax.rem(groups[t] - groups[s] + total_groups, total_groups)

        for s in range(slot_count):
            place = 0
            for t in range(slot_count):
                if t != s:
                    place = place + (ahead(t, s) < slot_count).astype(jnp.int32)
            away = (groups[s] // half != my_half).astype(jnp.int32)
            tag = (place + slot_count * away).astype(jnp.float32)
            slot = lax.rem(groups[s], half) ^ my_slot
            for t in range(slot_count):
                block = gram[s * width : (s + 1) * width, t * width : (t + 1) * width]
                if t == s:
                    block, rest = pack(block, tag)
                    rows_ref[slot, : width // 2] = block.astype(rows_ref.dtype)
                    rows_ref[slot, width // 2 : packed] = rest.astype(rows_ref.dtype)
                else:
                    gap = ahead(s, t)
                    turn = jnp.where(gap < slot_count, gap, gap - total_groups + slot_count)
                    at = pl.multiple_of(packed + (turn - 1) * width, TILE)
                    rows_ref[slot, pl.ds(at, width)] = block.astype(rows_ref.dtype)
        return carry

    lax.fori_loop(0, region_count, add_region, 0, unroll=region_count <= 2)
    for at, send_ref in enumerate(send_refs):
        first, last = row_range(at // CORES, width, slot_count)
        for pair in range(send_ref.shape[0]):
            send_ref[pair] = rows_ref[CORES * pair + at % CORES, first:last]


def sum_kernel(chunk, slot_count, *refs):
    arrays, (sums_ref, scaled_ref) = refs[:-2], refs[-2:]
    width = sums_ref.shape[1]
    half, packed = width // 2, packed_rows(width)
    count = sum_rows(chunk, width, slot_count)
    base = packed if chunk == 0 else 0
    sums_ref[...] = jnp.zeros_like(sums_ref)

    def units(arrays):
        return [(arrays[0], 0), (arrays[1], 0)] + [
            (x, core) for x in arrays[2:] for core in range(CORES)
        ]

    array_count = len(arrays) if chunk == 0 else len(arrays) // 2
    tags = [
        jnp.max(ref[at, half:packed].astype(jnp.float32)[TILE - 1 :, width - 1 :]).astype(
            jnp.int32
        )
        for ref, at in units(arrays[:array_count])
    ]
    for tag, (ref, at) in zip(tags, units(arrays[-array_count:])):
        away = tag // slot_count
        place = tag - slot_count * away
        if chunk == 0:
            to = pl.ds(pl.multiple_of(count * away, TILE), packed)
            sums_ref[to] += ref[at, :packed].astype(jnp.float32)
        for part, (turn, _) in enumerate(parts_of(chunk, slot_count)):
            wraps = (place + turn >= slot_count).astype(jnp.int32)
            to = count * away + base + (2 * part + wraps) * half
            block = ref[at, base + part * half : base + (part + 1) * half]
            sums_ref[pl.ds(pl.multiple_of(to, TILE), half)] += block.astype(jnp.float32)

    if chunk == 0:
        col = lax.broadcasted_iota(jnp.int32, (TILE, width), 1)
        for at in (half, count + half):
            sums_ref[at : at + TILE] = jnp.where(col < half, sums_ref[at : at + TILE], 0.0)

    tops = jnp.max(jnp.abs(sums_ref[count:]), axis=0, keepdims=True)
    largest = jnp.max(jnp.broadcast_to(tops, (8, width)), axis=1, keepdims=True)
    power = jnp.floor(jnp.log2(jnp.maximum(largest, 2.0**LEAST_POWER))) - TOP_POWER
    scaled_ref[:count] = sums_ref[count:] * jnp.exp2(-power)[0:1]
    scaled_ref[count:] = jnp.broadcast_to(power[0:1], (TILE, width))


def merge_kernel(keep_ref, got_ref, *send_refs):
    for at, send_ref in enumerate(send_refs):
        send_ref[0] = keep_ref[at + 1]
        send_ref[1] = got_ref[at + 1]


def join_kernel(slot_count, *refs):
    out_hbm, joined_ref, sems = refs[-3:]
    width = joined_ref.shape[1]
    half, packed = width // 2, packed_rows(width)
    for chunk in range(CHUNKS):
        sums_ref, far_ref = refs[2 * chunk : 2 * chunk + 2]
        count = sum_rows(chunk, width, slot_count)
        factor = jnp.exp2(far_ref[count : count + 1])

        def joined(first, size):
            return sums_ref[first : first + size] + far_ref[first : first + size] * factor

        if chunk == 0:
            blocks = unpack(joined(0, half), joined(half, 8)[:1])
            for at, block in enumerate(blocks):
                joined_ref[slot_count - 1, at * half : (at + 1) * half] = block
        base = packed if chunk == 0 else 0
        for part, (turn, at) in enumerate(parts_of(chunk, slot_count)):
            for wraps in range(2):
                to = turn - slot_count * wraps + slot_count - 1
                joined_ref[to, at * half : (at + 1) * half] = joined(
                    base + (2 * part + wraps) * half, half
                )
    copies = [
        pltpu.make_async_copy(joined_ref.at[to], out_hbm.at[to], sems.at[to])
        for to in range(joined_ref.shape[0])
    ]
    for copy in copies:
        copy.start()
    for copy in copies:
        copy.wait()


def shards(solve_cols, region_groups):
    region_count, row_count, col_count = solve_cols.shape
    slot_count = region_groups.shape[1]
    width = col_count // slot_count
    total_groups = lax.axis_size("group")
    half = region_count * slot_count
    span_count = 2 * slot_count - 1
    pair_count = half // CORES
    params = pltpu.CompilerParams(vmem_limit_bytes=VMEM_BYTES)
    light = pl.CostEstimate(flops=0, bytes_accessed=0, transcendentals=0)
    vmem = pl.BlockSpec(memory_space=pltpu.VMEM)
    hbm = pl.BlockSpec(memory_space=pltpu.HBM)

    def permute(values, step):
        pairs = [(d, d ^ step) for d in range(total_groups)]
        return lax.ppermute(values, "group", pairs)

    def blocks(count, chunk):
        first, last = row_range(chunk, width, slot_count)
        return jax.ShapeDtypeStruct((count, last - first, width), solve_cols.dtype)

    sends = pl.pallas_call(
        functools.partial(gram_kernel, total_groups, half),
        in_specs=[hbm] * 2,
        out_specs=[vmem] * (CHUNKS * CORES),
        out_shape=[blocks(pair_count, chunk) for chunk in range(CHUNKS) for _ in range(CORES)],
        scratch_shapes=[
            pltpu.SMEM(region_groups.shape, region_groups.dtype),
            pltpu.VMEM(solve_cols.shape, solve_cols.dtype),
            pltpu.VMEM((half, unit_rows(width, slot_count), width), solve_cols.dtype),
            pltpu.SemaphoreType.DMA,
            pltpu.SemaphoreType.DMA((region_count, COPIES)),
        ],
        cost_estimate=light,
        compiler_params=params,
        name="gram_rows",
    )(
        pltpu.with_memory_space_constraint(region_groups, pltpu.HBM),
        pltpu.with_memory_space_constraint(solve_cols, pltpu.HBM),
    )

    pieces, tagged = [], []
    for chunk in range(CHUNKS):
        keep, give = sends[CORES * chunk : CORES * (chunk + 1)]
        gots = [keep, permute(give, 1)]
        merged = pl.pallas_call(
            merge_kernel,
            out_shape=[blocks(CORES, chunk)] * (pair_count - 1),
            cost_estimate=light,
            compiler_params=params,
            name="merge_units",
        )(*gots)
        for pair in range(pair_count - 1, 0, -1):
            gots.append(permute(merged[pair - 1], CORES * pair))
        tagged = tagged or gots
        count = sum_rows(chunk, width, slot_count)
        sums, scaled = pl.pallas_call(
            functools.partial(sum_kernel, chunk, slot_count),
            out_shape=(
                jax.ShapeDtypeStruct((2 * count, width), jnp.float32),
                jax.ShapeDtypeStruct((count + TILE, width), jnp.float32),
            ),
            cost_estimate=light,
            compiler_params=params,
            name="sum_offsets",
        )(*(tagged if chunk == 0 else tagged + gots))
        far = permute(scaled.astype(jnp.float16), half)
        pieces += [sums, far.astype(jnp.float32)]

    return pl.pallas_call(
        functools.partial(join_kernel, slot_count),
        in_specs=[vmem] * len(pieces),
        out_specs=hbm,
        out_shape=jax.ShapeDtypeStruct((span_count, width, width), jnp.float32),
        scratch_shapes=[
            pltpu.VMEM((span_count, width, width), jnp.float32),
            pltpu.SemaphoreType.DMA((span_count,)),
        ],
        cost_estimate=light,
        compiler_params=params,
        name="join_offsets",
    )(*pieces)[None]


def solution(mesh):
    return jax.shard_map(
        shards,
        mesh=mesh,
        in_specs=(P(("parts", "group"), None, None), P("group", None)),
        out_specs=P(("parts", "group"), None, None, None),
        check_vma=False,
    )
```

```python
import functools

import jax
import jax.numpy as jnp
from jax import lax
from jax.experimental import pallas as pl
from jax.experimental.pallas import tpu as pltpu
from jax.sharding import PartitionSpec as P

VMEM_BYTES = 48 * 1024 * 1024
LEAST_POWER = -100.0
TOP_POWER = 13.0
CHUNKS = 2
CORES = 2
COPIES = 2
TILE = 16


def packed_rows(width):
    return width // 2 + TILE


def unit_rows(width, slot_count):
    return packed_rows(width) + (slot_count - 1) * width


def parts_of(chunk, slot_count):
    halves = [(turn, at) for turn in range(1, slot_count) for at in range(2)]
    size = len(halves) // CHUNKS
    return halves[chunk * size : (chunk + 1) * size]


def row_range(chunk, width, slot_count):
    size = len(parts_of(chunk, slot_count)) * (width // 2)
    first = packed_rows(width) + chunk * size
    return (0 if chunk == 0 else first), first + size


def sum_rows(chunk, width, slot_count):
    count = 2 * len(parts_of(chunk, slot_count)) * (width // 2)
    return count + (packed_rows(width) if chunk == 0 else 0)


def half_iota(width):
    shape = (width // 2, width)
    return (
        lax.broadcasted_iota(jnp.int32, shape, 0),
        lax.broadcasted_iota(jnp.int32, shape, 1),
    )


def pack(block, tag):
    width = block.shape[1]
    half = width // 2
    row, col = half_iota(width)
    lower = pltpu.roll(block[half:], half, 1)
    packed = jnp.where((col >= half) | (row <= col), block[:half], lower)
    diagonal = jnp.sum(jnp.where(row == col, lower, 0.0), axis=0, keepdims=True)
    rest = jnp.where(col[:1] < half, diagonal, tag)
    return packed, jnp.broadcast_to(rest, (TILE, width))


def unpack(packed, diagonal):
    half, width = packed.shape
    row, col = half_iota(width)
    turned = jnp.concatenate([packed, jnp.zeros_like(packed)], axis=0).T
    upper = jnp.where((col >= half) | (row <= col), packed, turned[:half])
    last = jnp.where(row > col, packed, jnp.where(row < col, turned[:half], diagonal))
    return upper, jnp.where(col < half, turned[half:], pltpu.roll(last, half, 1))


def gram_kernel(total_groups, half, groups_hbm, cols_hbm, *refs):
    groups_ref, cols_ref, rows_ref, groups_sem, cols_sems = refs[-5:]
    send_refs = refs[:-5]
    region_count, slot_count = groups_ref.shape
    width = cols_ref.shape[2] // slot_count
    me = lax.axis_index("group")
    my_half, my_slot = me // half, lax.rem(me, half)
    groups_copy = pltpu.make_async_copy(groups_hbm, groups_ref, groups_sem)
    groups_copy.start()

    depth = cols_ref.shape[1] // COPIES

    def cols_copy(region, part):
        rows = pl.ds(part * depth, depth)
        return pltpu.make_async_copy(
            cols_hbm.at[region, rows], cols_ref.at[region, rows], cols_sems.at[region, part]
        )

    for region in range(region_count):
        for part in range(COPIES):
            cols_copy(region, part).start()
    groups_copy.wait()
    packed = packed_rows(width)

    def add_region(region, carry):
        for part in range(COPIES):
            cols_copy(region, part).wait()
        cols = cols_ref[region]
        gram = lax.dot_general(
            cols, cols, (((0,), (0,)), ((), ())), preferred_element_type=jnp.float32
        )
        groups = [groups_ref[region, s] for s in range(slot_count)]

        def ahead(s, t):
            return lax.rem(groups[t] - groups[s] + total_groups, total_groups)

        for s in range(slot_count):
            place = 0
            for t in range(slot_count):
                if t != s:
                    place = place + (ahead(t, s) < slot_count).astype(jnp.int32)
            away = (groups[s] // half != my_half).astype(jnp.int32)
            tag = (place + slot_count * away).astype(jnp.float32)
            slot = lax.rem(groups[s], half) ^ my_slot
            for t in range(slot_count):
                block = gram[s * width : (s + 1) * width, t * width : (t + 1) * width]
                if t == s:
                    block, rest = pack(block, tag)
                    rows_ref[slot, : width // 2] = block.astype(rows_ref.dtype)
                    rows_ref[slot, width // 2 : packed] = rest.astype(rows_ref.dtype)
                else:
                    gap = ahead(s, t)
                    turn = jnp.where(gap < slot_count, gap, gap - total_groups + slot_count)
                    at = pl.multiple_of(packed + (turn - 1) * width, TILE)
                    rows_ref[slot, pl.ds(at, width)] = block.astype(rows_ref.dtype)
        return carry

    lax.fori_loop(0, region_count, add_region, 0, unroll=region_count <= 2)
    for at, send_ref in enumerate(send_refs):
        first, last = row_range(at // CORES, width, slot_count)
        for pair in range(send_ref.shape[0]):
            send_ref[pair] = rows_ref[CORES * pair + at % CORES, first:last]


def sum_kernel(chunk, slot_count, *refs):
    arrays, (sums_ref, scaled_ref) = refs[:-2], refs[-2:]
    width = sums_ref.shape[1]
    half, packed = width // 2, packed_rows(width)
    count = sum_rows(chunk, width, slot_count)
    base = packed if chunk == 0 else 0
    sums_ref[...] = jnp.zeros_like(sums_ref)

    def units(arrays):
        return [(arrays[0], 0), (arrays[1], 0)] + [
            (x, core) for x in arrays[2:] for core in range(CORES)
        ]

    array_count = len(arrays) if chunk == 0 else len(arrays) // 2
    tags = [
        jnp.max(ref[at, half:packed].astype(jnp.float32)[TILE - 1 :, width - 1 :]).astype(
            jnp.int32
        )
        for ref, at in units(arrays[:array_count])
    ]
    for tag, (ref, at) in zip(tags, units(arrays[-array_count:])):
        away = tag // slot_count
        place = tag - slot_count * away
        if chunk == 0:
            to = pl.ds(pl.multiple_of(count * away, TILE), packed)
            sums_ref[to] += ref[at, :packed].astype(jnp.float32)
        for part, (turn, _) in enumerate(parts_of(chunk, slot_count)):
            wraps = (place + turn >= slot_count).astype(jnp.int32)
            to = count * away + base + (2 * part + wraps) * half
            block = ref[at, base + part * half : base + (part + 1) * half]
            sums_ref[pl.ds(pl.multiple_of(to, TILE), half)] += block.astype(jnp.float32)

    if chunk == 0:
        col = lax.broadcasted_iota(jnp.int32, (TILE, width), 1)
        for at in (half, count + half):
            sums_ref[at : at + TILE] = jnp.where(col < half, sums_ref[at : at + TILE], 0.0)

    tops = jnp.max(jnp.abs(sums_ref[count:]), axis=0, keepdims=True)
    largest = jnp.max(jnp.broadcast_to(tops, (8, width)), axis=1, keepdims=True)
    power = jnp.floor(jnp.log2(jnp.maximum(largest, 2.0**LEAST_POWER))) - TOP_POWER
    scaled_ref[:count] = sums_ref[count:] * jnp.exp2(-power)[0:1]
    scaled_ref[count:] = jnp.broadcast_to(power[0:1], (TILE, width))


def merge_kernel(keep_ref, got_ref, *refs):
    after_ref, send_refs = refs[0], refs[1:]
    pair_count = keep_ref.shape[0]
    for at in range(1, pair_count):
        send_refs[at - 1][0] = keep_ref[at]
        send_refs[at - 1][1] = got_ref[at]
    if len(send_refs) == pair_count:
        send_refs[-1][...] = after_ref[...]


def join_kernel(slot_count, *refs):
    out_hbm, joined_ref, sems = refs[-3:]
    width = joined_ref.shape[1]
    half, packed = width // 2, packed_rows(width)
    for chunk in range(CHUNKS):
        sums_ref, far_ref = refs[2 * chunk : 2 * chunk + 2]
        count = sum_rows(chunk, width, slot_count)
        factor = jnp.exp2(far_ref[count : count + 1])

        def joined(first, size):
            return sums_ref[first : first + size] + far_ref[first : first + size] * factor

        if chunk == 0:
            blocks = unpack(joined(0, half), joined(half, 8)[:1])
            for at, block in enumerate(blocks):
                joined_ref[slot_count - 1, at * half : (at + 1) * half] = block
        base = packed if chunk == 0 else 0
        for part, (turn, at) in enumerate(parts_of(chunk, slot_count)):
            for wraps in range(2):
                to = turn - slot_count * wraps + slot_count - 1
                joined_ref[to, at * half : (at + 1) * half] = joined(
                    base + (2 * part + wraps) * half, half
                )
    copies = [
        pltpu.make_async_copy(joined_ref.at[to], out_hbm.at[to], sems.at[to])
        for to in range(joined_ref.shape[0])
    ]
    for copy in copies:
        copy.start()
    for copy in copies:
        copy.wait()


def shards(solve_cols, region_groups):
    region_count, row_count, col_count = solve_cols.shape
    slot_count = region_groups.shape[1]
    width = col_count // slot_count
    total_groups = lax.axis_size("group")
    half = region_count * slot_count
    span_count = 2 * slot_count - 1
    pair_count = half // CORES
    params = pltpu.CompilerParams(vmem_limit_bytes=VMEM_BYTES)
    light = pl.CostEstimate(flops=0, bytes_accessed=0, transcendentals=0)
    vmem = pl.BlockSpec(memory_space=pltpu.VMEM)
    hbm = pl.BlockSpec(memory_space=pltpu.HBM)

    def permute(values, step):
        pairs = [(d, d ^ step) for d in range(total_groups)]
        return lax.ppermute(values, "group", pairs)

    def blocks(count, chunk):
        first, last = row_range(chunk, width, slot_count)
        return jax.ShapeDtypeStruct((count, last - first, width), solve_cols.dtype)

    sends = pl.pallas_call(
        functools.partial(gram_kernel, total_groups, half),
        in_specs=[hbm] * 2,
        out_specs=[vmem] * (CHUNKS * CORES),
        out_shape=[blocks(pair_count, chunk) for chunk in range(CHUNKS) for _ in range(CORES)],
        scratch_shapes=[
            pltpu.SMEM(region_groups.shape, region_groups.dtype),
            pltpu.VMEM(solve_cols.shape, solve_cols.dtype),
            pltpu.VMEM((half, unit_rows(width, slot_count), width), solve_cols.dtype),
            pltpu.SemaphoreType.DMA,
            pltpu.SemaphoreType.DMA((region_count, COPIES)),
        ],
        cost_estimate=light,
        compiler_params=params,
        name="gram_rows",
    )(
        pltpu.with_memory_space_constraint(region_groups, pltpu.HBM),
        pltpu.with_memory_space_constraint(solve_cols, pltpu.HBM),
    )

    pieces, tagged = [], []
    for chunk in range(CHUNKS):
        keep, give = sends[CORES * chunk : CORES * (chunk + 1)]
        gots = [keep, permute(give if chunk == 0 else later, 1)]
        after = sends[CORES + 1] if chunk == 0 else tagged[CORES]
        merged = pl.pallas_call(
            merge_kernel,
            out_shape=[blocks(CORES, chunk)] * (pair_count - 1)
            + ([blocks(pair_count, 1)] if chunk == 0 else []),
            cost_estimate=light,
            compiler_params=params,
            name="merge_units",
        )(*gots, after)
        later = merged[-1]
        for pair in range(pair_count - 1, 0, -1):
            gots.append(permute(merged[pair - 1], CORES * pair))
        tagged = tagged or gots
        count = sum_rows(chunk, width, slot_count)
        sums, scaled = pl.pallas_call(
            functools.partial(sum_kernel, chunk, slot_count),
            out_shape=(
                jax.ShapeDtypeStruct((2 * count, width), jnp.float32),
                jax.ShapeDtypeStruct((count + TILE, width), jnp.float32),
            ),
            cost_estimate=light,
            compiler_params=params,
            name="sum_offsets",
        )(*(tagged if chunk == 0 else tagged + gots))
        far = permute(scaled.astype(jnp.float16), half)
        pieces += [sums, far.astype(jnp.float32)]

    return pl.pallas_call(
        functools.partial(join_kernel, slot_count),
        in_specs=[vmem] * len(pieces),
        out_specs=hbm,
        out_shape=jax.ShapeDtypeStruct((span_count, width, width), jnp.float32),
        scratch_shapes=[
            pltpu.VMEM((span_count, width, width), jnp.float32),
            pltpu.SemaphoreType.DMA((span_count,)),
        ],
        cost_estimate=light,
        compiler_params=params,
        name="join_offsets",
    )(*pieces)[None]


def solution(mesh):
    return jax.shard_map(
        shards,
        mesh=mesh,
        in_specs=(P(("parts", "group"), None, None), P("group", None)),
        out_specs=P(("parts", "group"), None, None, None),
        check_vma=False,
    )
```

```python
import functools

import jax
import jax.numpy as jnp
from jax import lax
from jax.experimental import pallas as pl
from jax.experimental.pallas import tpu as pltpu
from jax.sharding import PartitionSpec as P

VMEM_BYTES = 48 * 1024 * 1024
LEAST_POWER = -100.0
TOP_POWER = 13.0
CHUNKS = 2
CORES = 2
COPIES = 2
TILE = 16


def packed_rows(width):
    return width // 2 + TILE


def unit_rows(width, slot_count):
    return packed_rows(width) + (slot_count - 1) * width


def parts_of(chunk, slot_count):
    halves = [(turn, at) for turn in range(1, slot_count) for at in range(2)]
    size = len(halves) // CHUNKS
    return halves[chunk * size : (chunk + 1) * size]


def row_range(chunk, width, slot_count):
    size = len(parts_of(chunk, slot_count)) * (width // 2)
    first = packed_rows(width) + chunk * size
    return (0 if chunk == 0 else first), first + size


def sum_rows(chunk, width, slot_count):
    count = 2 * len(parts_of(chunk, slot_count)) * (width // 2)
    return count + (packed_rows(width) if chunk == 0 else 0)


def half_iota(width):
    shape = (width // 2, width)
    return (
        lax.broadcasted_iota(jnp.int32, shape, 0),
        lax.broadcasted_iota(jnp.int32, shape, 1),
    )


def pack(block, tag):
    width = block.shape[1]
    half = width // 2
    row, col = half_iota(width)
    lower = pltpu.roll(block[half:], half, 1)
    packed = jnp.where((col >= half) | (row <= col), block[:half], lower)
    diagonal = jnp.sum(jnp.where(row == col, lower, 0.0), axis=0, keepdims=True)
    rest = jnp.where(col[:1] < half, diagonal, tag)
    return packed, jnp.broadcast_to(rest, (TILE, width))


def unpack(packed, diagonal):
    half, width = packed.shape
    row, col = half_iota(width)
    turned = jnp.concatenate([packed, jnp.zeros_like(packed)], axis=0).T
    upper = jnp.where((col >= half) | (row <= col), packed, turned[:half])
    last = jnp.where(row > col, packed, jnp.where(row < col, turned[:half], diagonal))
    return upper, jnp.where(col < half, turned[half:], pltpu.roll(last, half, 1))


def gram_kernel(total_groups, half, groups_hbm, cols_hbm, *refs):
    groups_ref, cols_ref, rows_ref, groups_sem, cols_sems = refs[-5:]
    send_refs = refs[:-5]
    region_count, slot_count = groups_ref.shape
    width = cols_ref.shape[2] // slot_count
    me = lax.axis_index("group")
    my_half, my_slot = me // half, lax.rem(me, half)
    groups_copy = pltpu.make_async_copy(groups_hbm, groups_ref, groups_sem)
    groups_copy.start()

    depth = cols_ref.shape[1] // COPIES

    def cols_copy(region, part):
        rows = pl.ds(part * depth, depth)
        return pltpu.make_async_copy(
            cols_hbm.at[region, rows], cols_ref.at[region, rows], cols_sems.at[region, part]
        )

    for region in range(region_count):
        for part in range(COPIES):
            cols_copy(region, part).start()
    groups_copy.wait()
    packed = packed_rows(width)

    def add_region(region, carry):
        for part in range(COPIES):
            cols_copy(region, part).wait()
        cols = cols_ref[region]
        gram = lax.dot_general(
            cols, cols, (((0,), (0,)), ((), ())), preferred_element_type=jnp.float32
        )
        groups = [groups_ref[region, s] for s in range(slot_count)]

        def ahead(s, t):
            return lax.rem(groups[t] - groups[s] + total_groups, total_groups)

        for s in range(slot_count):
            place = 0
            for t in range(slot_count):
                if t != s:
                    place = place + (ahead(t, s) < slot_count).astype(jnp.int32)
            away = (groups[s] // half != my_half).astype(jnp.int32)
            tag = (place + slot_count * away).astype(jnp.float32)
            slot = lax.rem(groups[s], half) ^ my_slot
            for t in range(slot_count):
                block = gram[s * width : (s + 1) * width, t * width : (t + 1) * width]
                if t == s:
                    block, rest = pack(block, tag)
                    rows_ref[slot, : width // 2] = block.astype(rows_ref.dtype)
                    rows_ref[slot, width // 2 : packed] = rest.astype(rows_ref.dtype)
                else:
                    gap = ahead(s, t)
                    turn = jnp.where(gap < slot_count, gap, gap - total_groups + slot_count)
                    at = pl.multiple_of(packed + (turn - 1) * width, TILE)
                    rows_ref[slot, pl.ds(at, width)] = block.astype(rows_ref.dtype)
        return carry

    lax.fori_loop(0, region_count, add_region, 0, unroll=region_count <= 2)
    for at, send_ref in enumerate(send_refs):
        first, last = row_range(at // CORES, width, slot_count)
        for pair in range(send_ref.shape[0]):
            send_ref[pair] = rows_ref[CORES * pair + at % CORES, first:last]


def sum_kernel(chunk, slot_count, *refs):
    arrays, (sums_ref, scaled_ref) = refs[:-2], refs[-2:]
    width = sums_ref.shape[1]
    half, packed = width // 2, packed_rows(width)
    count = sum_rows(chunk, width, slot_count)
    base = packed if chunk == 0 else 0
    sums_ref[...] = jnp.zeros_like(sums_ref)

    def units(arrays):
        return [(arrays[0], 0), (arrays[1], 0)] + [
            (x, core) for x in arrays[2:] for core in range(CORES)
        ]

    array_count = len(arrays) if chunk == 0 else len(arrays) // 2
    tags = [
        jnp.max(ref[at, half:packed].astype(jnp.float32)[TILE - 1 :, width - 1 :]).astype(
            jnp.int32
        )
        for ref, at in units(arrays[:array_count])
    ]
    for tag, (ref, at) in zip(tags, units(arrays[-array_count:])):
        away = tag // slot_count
        place = tag - slot_count * away
        if chunk == 0:
            to = pl.ds(pl.multiple_of(count * away, TILE), packed)
            sums_ref[to] += ref[at, :packed].astype(jnp.float32)
        for part, (turn, _) in enumerate(parts_of(chunk, slot_count)):
            wraps = (place + turn >= slot_count).astype(jnp.int32)
            to = count * away + base + (2 * part + wraps) * half
            block = ref[at, base + part * half : base + (part + 1) * half]
            sums_ref[pl.ds(pl.multiple_of(to, TILE), half)] += block.astype(jnp.float32)

    if chunk == 0:
        col = lax.broadcasted_iota(jnp.int32, (TILE, width), 1)
        for at in (half, count + half):
            sums_ref[at : at + TILE] = jnp.where(col < half, sums_ref[at : at + TILE], 0.0)

    tops = jnp.max(jnp.abs(sums_ref[count:]), axis=0, keepdims=True)
    largest = jnp.max(jnp.broadcast_to(tops, (8, width)), axis=1, keepdims=True)
    power = jnp.floor(jnp.log2(jnp.maximum(largest, 2.0**LEAST_POWER))) - TOP_POWER
    scaled_ref[:count] = sums_ref[count:] * jnp.exp2(-power)[0:1]
    scaled_ref[count:] = jnp.broadcast_to(power[0:1], (TILE, width))


def merge_kernel(keep_ref, got_ref, *refs):
    after_ref, send_refs = refs[0], refs[1:]
    pair_count = keep_ref.shape[0]
    for at in range(1, pair_count):
        send_refs[at - 1][0] = keep_ref[at]
        send_refs[at - 1][1] = got_ref[at]
    if len(send_refs) == pair_count:
        send_refs[-1][...] = after_ref[...]


def join_kernel(chunk, slot_count, sums_ref, far_ref, *refs):
    out_hbm, joined_ref, sems = refs[-3:]
    width = joined_ref.shape[2]
    half, packed = width // 2, packed_rows(width)
    count = sum_rows(chunk, width, slot_count)
    factor = jnp.exp2(far_ref[count : count + 1])
    copies = []

    def joined(first, size):
        return sums_ref[first : first + size] + far_ref[first : first + size] * factor

    def put(block, offset, at):
        place = len(copies)
        joined_ref[place] = block
        copies.append(
            pltpu.make_async_copy(
                joined_ref.at[place],
                out_hbm.at[offset + slot_count - 1, at * half : (at + 1) * half],
                sems.at[place],
            )
        )
        copies[-1].start()

    base = 0
    if chunk == 0:
        base = packed
        for at, block in enumerate(unpack(joined(0, half), joined(half, 8)[:1])):
            put(block, 0, at)
    for part, (turn, at) in enumerate(parts_of(chunk, slot_count)):
        for wraps in range(2):
            first = base + (2 * part + wraps) * half
            put(joined(first, half), turn - slot_count * wraps, at)
    for copy in copies:
        copy.wait()


def shards(solve_cols, region_groups):
    region_count, row_count, col_count = solve_cols.shape
    slot_count = region_groups.shape[1]
    width = col_count // slot_count
    total_groups = lax.axis_size("group")
    half = region_count * slot_count
    span_count = 2 * slot_count - 1
    pair_count = half // CORES
    params = pltpu.CompilerParams(vmem_limit_bytes=VMEM_BYTES)
    light = pl.CostEstimate(flops=0, bytes_accessed=0, transcendentals=0)
    vmem = pl.BlockSpec(memory_space=pltpu.VMEM)
    hbm = pl.BlockSpec(memory_space=pltpu.HBM)

    def permute(values, step):
        pairs = [(d, d ^ step) for d in range(total_groups)]
        return lax.ppermute(values, "group", pairs)

    def blocks(count, chunk):
        first, last = row_range(chunk, width, slot_count)
        return jax.ShapeDtypeStruct((count, last - first, width), solve_cols.dtype)

    sends = pl.pallas_call(
        functools.partial(gram_kernel, total_groups, half),
        in_specs=[hbm] * 2,
        out_specs=[vmem] * (CHUNKS * CORES),
        out_shape=[blocks(pair_count, chunk) for chunk in range(CHUNKS) for _ in range(CORES)],
        scratch_shapes=[
            pltpu.SMEM(region_groups.shape, region_groups.dtype),
            pltpu.VMEM(solve_cols.shape, solve_cols.dtype),
            pltpu.VMEM((half, unit_rows(width, slot_count), width), solve_cols.dtype),
            pltpu.SemaphoreType.DMA,
            pltpu.SemaphoreType.DMA((region_count, COPIES)),
        ],
        cost_estimate=light,
        compiler_params=pltpu.CompilerParams(
            vmem_limit_bytes=VMEM_BYTES, fuse_transposed_lhs_in_matmul=True
        ),
        name="gram_rows",
    )(
        pltpu.with_memory_space_constraint(region_groups, pltpu.HBM),
        pltpu.with_memory_space_constraint(solve_cols, pltpu.HBM),
    )

    pieces, tagged = [], []
    for chunk in range(CHUNKS):
        keep, give = sends[CORES * chunk : CORES * (chunk + 1)]
        gots = [keep, permute(give if chunk == 0 else later, 1)]
        after = sends[CORES + 1] if chunk == 0 else tagged[CORES]
        merged = pl.pallas_call(
            merge_kernel,
            out_shape=[blocks(CORES, chunk)] * (pair_count - 1)
            + ([blocks(pair_count, 1)] if chunk == 0 else []),
            cost_estimate=light,
            compiler_params=params,
            name="merge_units",
        )(*gots, after)
        later = merged[-1]
        for pair in range(pair_count - 1, 0, -1):
            gots.append(permute(merged[pair - 1], CORES * pair))
        tagged = tagged or gots
        count = sum_rows(chunk, width, slot_count)
        sums, scaled = pl.pallas_call(
            functools.partial(sum_kernel, chunk, slot_count),
            out_shape=(
                jax.ShapeDtypeStruct((2 * count, width), jnp.float32),
                jax.ShapeDtypeStruct((count + TILE, width), jnp.float32),
            ),
            cost_estimate=light,
            compiler_params=params,
            name="sum_offsets",
        )(*(tagged if chunk == 0 else tagged + gots))
        far = permute(scaled.astype(jnp.float16), half)
        pieces.append((sums, far.astype(jnp.float32)))

    schur = ()
    for chunk in range(CHUNKS):
        count = 2 * len(parts_of(chunk, slot_count)) + (2 if chunk == 0 else 0)
        schur = (
            pl.pallas_call(
                functools.partial(join_kernel, chunk, slot_count),
                in_specs=[vmem] * 2 + [hbm] * len(schur),
                out_specs=hbm,
                out_shape=jax.ShapeDtypeStruct((span_count, width, width), jnp.float32),
                input_output_aliases={2: 0} if schur else {},
                scratch_shapes=[
                    pltpu.VMEM((count, width // 2, width), jnp.float32),
                    pltpu.SemaphoreType.DMA((count,)),
                ],
                cost_estimate=light,
                compiler_params=params,
                name="join_offsets",
            )(*pieces[chunk], *schur),
        )
    return schur[0][None]


def solution(mesh):
    return jax.shard_map(
        shards,
        mesh=mesh,
        in_specs=(P(("parts", "group"), None, None), P("group", None)),
        out_specs=P(("parts", "group"), None, None, None),
        check_vma=False,
    )
```

```python
import functools

import jax
import jax.numpy as jnp
from jax import lax
from jax.experimental import pallas as pl
from jax.experimental.pallas import tpu as pltpu
from jax.sharding import PartitionSpec as P

VMEM_BYTES = 48 * 1024 * 1024
LEAST_POWER = -100.0
TOP_POWER = 13.0
CHUNKS = 2
CORES = 2
COPIES = 2
TILE = 16


def packed_rows(width):
    return width // 2 + TILE


def unit_rows(width, slot_count):
    return packed_rows(width) + (slot_count - 1) * width


def parts_of(chunk, slot_count):
    halves = [(turn, at) for turn in range(1, slot_count) for at in range(2)]
    size = len(halves) // CHUNKS
    return halves[chunk * size : (chunk + 1) * size]


def row_range(chunk, width, slot_count):
    size = len(parts_of(chunk, slot_count)) * (width // 2)
    first = packed_rows(width) + chunk * size
    return (0 if chunk == 0 else first), first + size


def sum_rows(chunk, width, slot_count):
    count = 2 * len(parts_of(chunk, slot_count)) * (width // 2)
    return count + (packed_rows(width) if chunk == 0 else 0)


def half_iota(width):
    shape = (width // 2, width)
    return (
        lax.broadcasted_iota(jnp.int32, shape, 0),
        lax.broadcasted_iota(jnp.int32, shape, 1),
    )


def pack(block, tag):
    width = block.shape[1]
    half = width // 2
    row, col = half_iota(width)
    lower = pltpu.roll(block[half:], half, 1)
    packed = jnp.where((col >= half) | (row <= col), block[:half], lower)
    diagonal = jnp.sum(jnp.where(row == col, lower, 0.0), axis=0, keepdims=True)
    rest = jnp.where(col[:1] < half, diagonal, tag)
    return packed, jnp.broadcast_to(rest, (TILE, width))


def unpack(packed, diagonal):
    half, width = packed.shape
    row, col = half_iota(width)
    turned = jnp.concatenate([packed, jnp.zeros_like(packed)], axis=0).T
    upper = jnp.where((col >= half) | (row <= col), packed, turned[:half])
    last = jnp.where(row > col, packed, jnp.where(row < col, turned[:half], diagonal))
    return upper, jnp.where(col < half, turned[half:], pltpu.roll(last, half, 1))


def gram_kernel(total_groups, half, groups_hbm, cols_hbm, *refs):
    groups_ref, cols_ref, rows_ref, groups_sem, cols_sems = refs[-5:]
    send_refs = refs[:-5]
    region_count, slot_count = groups_ref.shape
    width = cols_ref.shape[2] // slot_count
    me = lax.axis_index("group")
    my_half, my_slot = me // half, lax.rem(me, half)
    groups_copy = pltpu.make_async_copy(groups_hbm, groups_ref, groups_sem)
    groups_copy.start()

    depth = cols_ref.shape[1] // COPIES

    def cols_copy(region, part):
        rows = pl.ds(part * depth, depth)
        return pltpu.make_async_copy(
            cols_hbm.at[region, rows], cols_ref.at[region, rows], cols_sems.at[region, part]
        )

    for region in range(region_count):
        for part in range(COPIES):
            cols_copy(region, part).start()
    groups_copy.wait()
    packed = packed_rows(width)

    def add_region(region, carry):
        for part in range(COPIES):
            cols_copy(region, part).wait()
        cols = cols_ref[region]
        gram = lax.dot_general(
            cols, cols, (((0,), (0,)), ((), ())), preferred_element_type=jnp.float32
        )
        groups = [groups_ref[region, s] for s in range(slot_count)]

        def ahead(s, t):
            return lax.rem(groups[t] - groups[s] + total_groups, total_groups)

        for s in range(slot_count):
            place = 0
            for t in range(slot_count):
                if t != s:
                    place = place + (ahead(t, s) < slot_count).astype(jnp.int32)
            away = (groups[s] // half != my_half).astype(jnp.int32)
            tag = (place + slot_count * away).astype(jnp.float32)
            slot = lax.rem(groups[s], half) ^ my_slot
            for t in range(slot_count):
                block = gram[s * width : (s + 1) * width, t * width : (t + 1) * width]
                if t == s:
                    block, rest = pack(block, tag)
                    rows_ref[slot, : width // 2] = block.astype(rows_ref.dtype)
                    rows_ref[slot, width // 2 : packed] = rest.astype(rows_ref.dtype)
                else:
                    gap = ahead(s, t)
                    turn = jnp.where(gap < slot_count, gap, gap - total_groups + slot_count)
                    at = pl.multiple_of(packed + (turn - 1) * width, TILE)
                    rows_ref[slot, pl.ds(at, width)] = block.astype(rows_ref.dtype)
        return carry

    lax.fori_loop(0, region_count, add_region, 0, unroll=region_count <= 2)
    for at, send_ref in enumerate(send_refs):
        first, last = row_range(at // CORES, width, slot_count)
        for pair in range(send_ref.shape[0]):
            send_ref[pair] = rows_ref[CORES * pair + at % CORES, first:last]


def sum_kernel(chunk, slot_count, *refs):
    arrays, (sums_ref, scaled_ref) = refs[:-2], refs[-2:]
    width = sums_ref.shape[1]
    half, packed = width // 2, packed_rows(width)
    count = sum_rows(chunk, width, slot_count)
    base = packed if chunk == 0 else 0
    sums_ref[...] = jnp.zeros_like(sums_ref)

    def units(arrays):
        return [(arrays[0], 0), (arrays[1], 0)] + [
            (x, core) for x in arrays[2:] for core in range(CORES)
        ]

    array_count = len(arrays) if chunk == 0 else len(arrays) // 2
    tags = [
        jnp.max(ref[at, half:packed].astype(jnp.float32)[TILE - 1 :, width - 1 :]).astype(
            jnp.int32
        )
        for ref, at in units(arrays[:array_count])
    ]
    for tag, (ref, at) in zip(tags, units(arrays[-array_count:])):
        away = tag // slot_count
        place = tag - slot_count * away
        if chunk == 0:
            to = pl.ds(pl.multiple_of(count * away, TILE), packed)
            sums_ref[to] += ref[at, :packed].astype(jnp.float32)
        for part, (turn, _) in enumerate(parts_of(chunk, slot_count)):
            wraps = (place + turn >= slot_count).astype(jnp.int32)
            to = count * away + base + (2 * part + wraps) * half
            block = ref[at, base + part * half : base + (part + 1) * half]
            sums_ref[pl.ds(pl.multiple_of(to, TILE), half)] += block.astype(jnp.float32)

    if chunk == 0:
        col = lax.broadcasted_iota(jnp.int32, (TILE, width), 1)
        for at in (half, count + half):
            sums_ref[at : at + TILE] = jnp.where(col < half, sums_ref[at : at + TILE], 0.0)

    tops = jnp.max(jnp.abs(sums_ref[count:]), axis=0, keepdims=True)
    largest = jnp.max(jnp.broadcast_to(tops, (8, width)), axis=1, keepdims=True)
    power = jnp.floor(jnp.log2(jnp.maximum(largest, 2.0**LEAST_POWER))) - TOP_POWER
    scaled_ref[:count] = sums_ref[count:] * jnp.exp2(-power)[0:1]
    scaled_ref[count:] = jnp.broadcast_to(power[0:1], (TILE, width))


def merge_kernel(keep_ref, got_ref, *refs):
    after_ref, send_refs = refs[0], refs[1:]
    pair_count = keep_ref.shape[0]
    for at in range(1, pair_count):
        send_refs[at - 1][0] = keep_ref[at]
        send_refs[at - 1][1] = got_ref[at]
    if len(send_refs) == pair_count:
        send_refs[-1][...] = after_ref[...]


def join_kernel(chunk, slot_count, sums_ref, far_ref, *refs):
    out_hbm, joined_ref, sems = refs[-3:]
    width = joined_ref.shape[2]
    half, packed = width // 2, packed_rows(width)
    count = sum_rows(chunk, width, slot_count)
    factor = jnp.exp2(far_ref[count : count + 1])
    copies = []

    def joined(first, size):
        return sums_ref[first : first + size] + far_ref[first : first + size] * factor

    def put(block, offset, at):
        place = len(copies)
        joined_ref[place] = block
        copies.append(
            pltpu.make_async_copy(
                joined_ref.at[place],
                out_hbm.at[offset + slot_count - 1, at * half : (at + 1) * half],
                sems.at[place],
            )
        )
        copies[-1].start()

    base = 0
    if chunk == 0:
        base = packed
        for at, block in enumerate(unpack(joined(0, half), joined(half, 8)[:1])):
            put(block, 0, at)
    for part, (turn, at) in enumerate(parts_of(chunk, slot_count)):
        for wraps in range(2):
            first = base + (2 * part + wraps) * half
            put(joined(first, half), turn - slot_count * wraps, at)
    for copy in copies:
        copy.wait()


def shards(solve_cols, region_groups):
    region_count, row_count, col_count = solve_cols.shape
    slot_count = region_groups.shape[1]
    width = col_count // slot_count
    total_groups = lax.axis_size("group")
    half = region_count * slot_count
    span_count = 2 * slot_count - 1
    pair_count = half // CORES
    params = pltpu.CompilerParams(vmem_limit_bytes=VMEM_BYTES)
    light = pl.CostEstimate(flops=0, bytes_accessed=0, transcendentals=0)
    vmem = pl.BlockSpec(memory_space=pltpu.VMEM)
    hbm = pl.BlockSpec(memory_space=pltpu.HBM)

    def permute(values, step):
        pairs = [(d, d ^ step) for d in range(total_groups)]
        return lax.ppermute(values, "group", pairs)

    def blocks(count, chunk):
        first, last = row_range(chunk, width, slot_count)
        return jax.ShapeDtypeStruct((count, last - first, width), solve_cols.dtype)

    sends = pl.pallas_call(
        functools.partial(gram_kernel, total_groups, half),
        in_specs=[hbm] * 2,
        out_specs=[vmem] * (CHUNKS * CORES),
        out_shape=[blocks(pair_count, chunk) for chunk in range(CHUNKS) for _ in range(CORES)],
        scratch_shapes=[
            pltpu.SMEM(region_groups.shape, region_groups.dtype),
            pltpu.VMEM(solve_cols.shape, solve_cols.dtype),
            pltpu.VMEM((half, unit_rows(width, slot_count), width), solve_cols.dtype),
            pltpu.SemaphoreType.DMA,
            pltpu.SemaphoreType.DMA((region_count, COPIES)),
        ],
        cost_estimate=light,
        compiler_params=params,
        name="gram_rows",
    )(
        pltpu.with_memory_space_constraint(region_groups, pltpu.HBM),
        pltpu.with_memory_space_constraint(solve_cols, pltpu.HBM),
    )

    pieces, tagged = [], []
    for chunk in range(CHUNKS):
        keep, give = sends[CORES * chunk : CORES * (chunk + 1)]
        gots = [keep, permute(give if chunk == 0 else later, 1)]
        after = sends[CORES + 1] if chunk == 0 else tagged[CORES]
        merged = pl.pallas_call(
            merge_kernel,
            out_shape=[blocks(CORES, chunk)] * (pair_count - 1)
            + ([blocks(pair_count, 1)] if chunk == 0 else []),
            cost_estimate=light,
            compiler_params=params,
            name="merge_units",
        )(*gots, after)
        later = merged[-1]
        for pair in sorted(range(1, pair_count), key=lambda p: (p.bit_count(), -p)):
            gots.append(permute(merged[pair - 1], CORES * pair))
        tagged = tagged or gots
        count = sum_rows(chunk, width, slot_count)
        sums, scaled = pl.pallas_call(
            functools.partial(sum_kernel, chunk, slot_count),
            out_shape=(
                jax.ShapeDtypeStruct((2 * count, width), jnp.float32),
                jax.ShapeDtypeStruct((count + TILE, width), jnp.float32),
            ),
            cost_estimate=light,
            compiler_params=params,
            name="sum_offsets",
        )(*(tagged if chunk == 0 else tagged + gots))
        far = permute(scaled.astype(jnp.float16), half)
        pieces.append((sums, far.astype(jnp.float32)))

    schur = ()
    for chunk in range(CHUNKS):
        count = 2 * len(parts_of(chunk, slot_count)) + (2 if chunk == 0 else 0)
        schur = (
            pl.pallas_call(
                functools.partial(join_kernel, chunk, slot_count),
                in_specs=[vmem] * 2 + [hbm] * len(schur),
                out_specs=hbm,
                out_shape=jax.ShapeDtypeStruct((span_count, width, width), jnp.float32),
                input_output_aliases={2: 0} if schur else {},
                scratch_shapes=[
                    pltpu.VMEM((count, width // 2, width), jnp.float32),
                    pltpu.SemaphoreType.DMA((count,)),
                ],
                cost_estimate=light,
                compiler_params=params,
                name="join_offsets",
            )(*pieces[chunk], *schur),
        )
    return schur[0][None]


def solution(mesh):
    return jax.shard_map(
        shards,
        mesh=mesh,
        in_specs=(P(("parts", "group"), None, None), P("group", None)),
        out_specs=P(("parts", "group"), None, None, None),
        check_vma=False,
    )
```

```python
import functools

import jax
import jax.numpy as jnp
from jax import lax
from jax.experimental import pallas as pl
from jax.experimental.pallas import tpu as pltpu
from jax.sharding import PartitionSpec as P

VMEM_BYTES = 48 * 1024 * 1024
LEAST_POWER = -100.0
TOP_POWER = 13.0
CHUNKS = 2
CORES = 2
COPIES = 2
TILE = 16
PRODUCTS = 2


def packed_rows(width):
    return width // 2 + TILE


def unit_rows(width, slot_count):
    return packed_rows(width) + (slot_count - 1) * width


def parts_of(chunk, slot_count):
    halves = [(turn, at) for turn in range(1, slot_count) for at in range(2)]
    size = len(halves) // CHUNKS
    return halves[chunk * size : (chunk + 1) * size]


def row_range(chunk, width, slot_count):
    size = len(parts_of(chunk, slot_count)) * (width // 2)
    first = packed_rows(width) + chunk * size
    return (0 if chunk == 0 else first), first + size


def sum_rows(chunk, width, slot_count):
    count = 2 * len(parts_of(chunk, slot_count)) * (width // 2)
    return count + (packed_rows(width) if chunk == 0 else 0)


def half_iota(width):
    shape = (width // 2, width)
    return (
        lax.broadcasted_iota(jnp.int32, shape, 0),
        lax.broadcasted_iota(jnp.int32, shape, 1),
    )


def pack(block, tag):
    width = block.shape[1]
    half = width // 2
    row, col = half_iota(width)
    lower = pltpu.roll(block[half:], half, 1)
    packed = jnp.where((col >= half) | (row <= col), block[:half], lower)
    diagonal = jnp.sum(jnp.where(row == col, lower, 0.0), axis=0, keepdims=True)
    rest = jnp.where(col[:1] < half, diagonal, tag)
    return packed, jnp.broadcast_to(rest, (TILE, width))


def unpack(packed, diagonal):
    half, width = packed.shape
    row, col = half_iota(width)
    turned = jnp.concatenate([packed, jnp.zeros_like(packed)], axis=0).T
    upper = jnp.where((col >= half) | (row <= col), packed, turned[:half])
    last = jnp.where(row > col, packed, jnp.where(row < col, turned[:half], diagonal))
    return upper, jnp.where(col < half, turned[half:], pltpu.roll(last, half, 1))


def gram_kernel(total_groups, half, groups_hbm, cols_hbm, *refs):
    groups_ref, cols_ref, rows_ref, groups_sem, cols_sems = refs[-5:]
    send_refs = refs[:-5]
    region_count, slot_count = groups_ref.shape
    width = cols_ref.shape[2] // slot_count
    me = lax.axis_index("group")
    my_half, my_slot = me // half, lax.rem(me, half)
    groups_copy = pltpu.make_async_copy(groups_hbm, groups_ref, groups_sem)
    groups_copy.start()

    depth = cols_ref.shape[1] // COPIES

    def cols_copy(region, part):
        rows = pl.ds(part * depth, depth)
        return pltpu.make_async_copy(
            cols_hbm.at[region, rows], cols_ref.at[region, rows], cols_sems.at[region, part]
        )

    for region in range(region_count):
        for part in range(COPIES):
            cols_copy(region, part).start()
    groups_copy.wait()
    packed = packed_rows(width)

    def add_region(region, carry):
        for part in range(COPIES):
            cols_copy(region, part).wait()
        cols = cols_ref[region]
        depth = cols.shape[1] // PRODUCTS
        grams = [
            lax.dot_general(
                cols[:, at * depth : (at + 1) * depth],
                cols,
                (((0,), (0,)), ((), ())),
                preferred_element_type=jnp.float32,
            )
            for at in range(PRODUCTS)
        ]
        groups = [groups_ref[region, s] for s in range(slot_count)]

        def ahead(s, t):
            return lax.rem(groups[t] - groups[s] + total_groups, total_groups)

        for s in range(slot_count):
            place = 0
            for t in range(slot_count):
                if t != s:
                    place = place + (ahead(t, s) < slot_count).astype(jnp.int32)
            away = (groups[s] // half != my_half).astype(jnp.int32)
            tag = (place + slot_count * away).astype(jnp.float32)
            slot = lax.rem(groups[s], half) ^ my_slot
            for t in range(slot_count):
                at = s * width % depth
                block = grams[s * width // depth][at : at + width, t * width : (t + 1) * width]
                if t == s:
                    block, rest = pack(block, tag)
                    rows_ref[slot, : width // 2] = block.astype(rows_ref.dtype)
                    rows_ref[slot, width // 2 : packed] = rest.astype(rows_ref.dtype)
                else:
                    gap = ahead(s, t)
                    turn = jnp.where(gap < slot_count, gap, gap - total_groups + slot_count)
                    at = pl.multiple_of(packed + (turn - 1) * width, TILE)
                    rows_ref[slot, pl.ds(at, width)] = block.astype(rows_ref.dtype)
        return carry

    lax.fori_loop(0, region_count, add_region, 0, unroll=region_count <= 2)
    for at, send_ref in enumerate(send_refs):
        first, last = row_range(at // CORES, width, slot_count)
        for pair in range(send_ref.shape[0]):
            send_ref[pair] = rows_ref[CORES * pair + at % CORES, first:last]


def sum_kernel(chunk, slot_count, *refs):
    arrays, (sums_ref, scaled_ref) = refs[:-2], refs[-2:]
    width = sums_ref.shape[1]
    half, packed = width // 2, packed_rows(width)
    count = sum_rows(chunk, width, slot_count)
    base = packed if chunk == 0 else 0
    sums_ref[...] = jnp.zeros_like(sums_ref)

    def units(arrays):
        return [(arrays[0], 0), (arrays[1], 0)] + [
            (x, core) for x in arrays[2:] for core in range(CORES)
        ]

    array_count = len(arrays) if chunk == 0 else len(arrays) // 2
    tags = [
        jnp.max(ref[at, half:packed].astype(jnp.float32)[TILE - 1 :, width - 1 :]).astype(
            jnp.int32
        )
        for ref, at in units(arrays[:array_count])
    ]
    for tag, (ref, at) in zip(tags, units(arrays[-array_count:])):
        away = tag // slot_count
        place = tag - slot_count * away
        if chunk == 0:
            to = pl.ds(pl.multiple_of(count * away, TILE), packed)
            sums_ref[to] += ref[at, :packed].astype(jnp.float32)
        for part, (turn, _) in enumerate(parts_of(chunk, slot_count)):
            wraps = (place + turn >= slot_count).astype(jnp.int32)
            to = count * away + base + (2 * part + wraps) * half
            block = ref[at, base + part * half : base + (part + 1) * half]
            sums_ref[pl.ds(pl.multiple_of(to, TILE), half)] += block.astype(jnp.float32)

    if chunk == 0:
        col = lax.broadcasted_iota(jnp.int32, (TILE, width), 1)
        for at in (half, count + half):
            sums_ref[at : at + TILE] = jnp.where(col < half, sums_ref[at : at + TILE], 0.0)

    tops = jnp.max(jnp.abs(sums_ref[count:]), axis=0, keepdims=True)
    largest = jnp.max(jnp.broadcast_to(tops, (8, width)), axis=1, keepdims=True)
    power = jnp.floor(jnp.log2(jnp.maximum(largest, 2.0**LEAST_POWER))) - TOP_POWER
    scaled_ref[:count] = sums_ref[count:] * jnp.exp2(-power)[0:1]
    scaled_ref[count:] = jnp.broadcast_to(power[0:1], (TILE, width))


def merge_kernel(keep_ref, got_ref, *refs):
    pair_count = keep_ref.shape[0]
    for at, send_ref in enumerate(refs[1 - pair_count :], 1):
        send_ref[0] = keep_ref[at]
        send_ref[1] = got_ref[at]


def join_kernel(chunk, slot_count, sums_ref, far_ref, *refs):
    out_hbm, joined_ref, sems = refs[-3:]
    width = joined_ref.shape[2]
    half, packed = width // 2, packed_rows(width)
    count = sum_rows(chunk, width, slot_count)
    factor = jnp.exp2(far_ref[count : count + 1])
    copies = []

    def joined(first, size):
        return sums_ref[first : first + size] + far_ref[first : first + size] * factor

    def put(block, offset, at):
        place = len(copies)
        joined_ref[place] = block
        copies.append(
            pltpu.make_async_copy(
                joined_ref.at[place],
                out_hbm.at[offset + slot_count - 1, at * half : (at + 1) * half],
                sems.at[place],
            )
        )
        copies[-1].start()

    base = 0
    if chunk == 0:
        base = packed
        for at, block in enumerate(unpack(joined(0, half), joined(half, 8)[:1])):
            put(block, 0, at)
    for part, (turn, at) in enumerate(parts_of(chunk, slot_count)):
        for wraps in range(2):
            first = base + (2 * part + wraps) * half
            put(joined(first, half), turn - slot_count * wraps, at)
    for copy in copies:
        copy.wait()


def shards(solve_cols, region_groups):
    region_count, row_count, col_count = solve_cols.shape
    slot_count = region_groups.shape[1]
    width = col_count // slot_count
    total_groups = lax.axis_size("group")
    half = region_count * slot_count
    span_count = 2 * slot_count - 1
    pair_count = half // CORES
    params = pltpu.CompilerParams(vmem_limit_bytes=VMEM_BYTES)
    light = pl.CostEstimate(flops=0, bytes_accessed=0, transcendentals=0)
    vmem = pl.BlockSpec(memory_space=pltpu.VMEM)
    hbm = pl.BlockSpec(memory_space=pltpu.HBM)

    def permute(values, step):
        pairs = [(d, d ^ step) for d in range(total_groups)]
        return lax.ppermute(values, "group", pairs)

    def blocks(count, chunk):
        first, last = row_range(chunk, width, slot_count)
        return jax.ShapeDtypeStruct((count, last - first, width), solve_cols.dtype)

    sends = pl.pallas_call(
        functools.partial(gram_kernel, total_groups, half),
        in_specs=[hbm] * 2,
        out_specs=[vmem] * (CHUNKS * CORES),
        out_shape=[blocks(pair_count, chunk) for chunk in range(CHUNKS) for _ in range(CORES)],
        scratch_shapes=[
            pltpu.SMEM(region_groups.shape, region_groups.dtype),
            pltpu.VMEM(solve_cols.shape, solve_cols.dtype),
            pltpu.VMEM((half, unit_rows(width, slot_count), width), solve_cols.dtype),
            pltpu.SemaphoreType.DMA,
            pltpu.SemaphoreType.DMA((region_count, COPIES)),
        ],
        cost_estimate=light,
        compiler_params=params,
        name="gram_rows",
    )(
        pltpu.with_memory_space_constraint(region_groups, pltpu.HBM),
        pltpu.with_memory_space_constraint(solve_cols, pltpu.HBM),
    )

    pieces, tagged = [], []
    for chunk in range(CHUNKS):
        keep, give = sends[CORES * chunk : CORES * (chunk + 1)]
        gots = [keep, permute(give, 1)]
        merged = pl.pallas_call(
            merge_kernel,
            out_shape=[blocks(CORES, chunk)] * (pair_count - 1),
            cost_estimate=light,
            compiler_params=params,
            name="merge_units",
        )(*gots, *tagged[CORES : CORES + chunk])
        for pair in sorted(range(1, pair_count), key=lambda p: (p.bit_count(), -p)):
            gots.append(permute(merged[pair - 1], CORES * pair))
        tagged = tagged or gots
        count = sum_rows(chunk, width, slot_count)
        sums, scaled = pl.pallas_call(
            functools.partial(sum_kernel, chunk, slot_count),
            out_shape=(
                jax.ShapeDtypeStruct((2 * count, width), jnp.float32),
                jax.ShapeDtypeStruct((count + TILE, width), jnp.float32),
            ),
            cost_estimate=light,
            compiler_params=params,
            name="sum_offsets",
        )(*(tagged if chunk == 0 else tagged + gots))
        far = permute(scaled.astype(jnp.float16), half)
        pieces.append((sums, far.astype(jnp.float32)))

    schur = ()
    for chunk in range(CHUNKS):
        count = 2 * len(parts_of(chunk, slot_count)) + (2 if chunk == 0 else 0)
        schur = (
            pl.pallas_call(
                functools.partial(join_kernel, chunk, slot_count),
                in_specs=[vmem] * 2 + [hbm] * len(schur),
                out_specs=hbm,
                out_shape=jax.ShapeDtypeStruct((span_count, width, width), jnp.float32),
                input_output_aliases={2: 0} if schur else {},
                scratch_shapes=[
                    pltpu.VMEM((count, width // 2, width), jnp.float32),
                    pltpu.SemaphoreType.DMA((count,)),
                ],
                cost_estimate=light,
                compiler_params=params,
                name="join_offsets",
            )(*pieces[chunk], *schur),
        )
    return schur[0][None]


def solution(mesh):
    return jax.shard_map(
        shards,
        mesh=mesh,
        in_specs=(P(("parts", "group"), None, None), P("group", None)),
        out_specs=P(("parts", "group"), None, None, None),
        check_vma=False,
    )
```

```python
import functools

import jax
import jax.numpy as jnp
from jax import lax
from jax.experimental import pallas as pl
from jax.experimental.pallas import tpu as pltpu
from jax.sharding import PartitionSpec as P

VMEM_BYTES = 48 * 1024 * 1024
LEAST_POWER = -100.0
TOP_POWER = 13.0
CHUNKS = 2
CORES = 2
COPIES = 2
TILE = 16
PRODUCTS = 2


def packed_rows(width):
    return width // 2 + TILE


def unit_rows(width, slot_count):
    return packed_rows(width) + (slot_count - 1) * width


def parts_of(chunk, slot_count):
    halves = [(turn, at) for turn in range(1, slot_count) for at in range(2)]
    size = len(halves) // CHUNKS
    return halves[chunk * size : (chunk + 1) * size]


def row_range(chunk, width, slot_count):
    size = len(parts_of(chunk, slot_count)) * (width // 2)
    first = packed_rows(width) + chunk * size
    return (0 if chunk == 0 else first), first + size


def sum_rows(chunk, width, slot_count):
    count = 2 * len(parts_of(chunk, slot_count)) * (width // 2)
    return count + (packed_rows(width) if chunk == 0 else 0)


def half_iota(width):
    shape = (width // 2, width)
    return (
        lax.broadcasted_iota(jnp.int32, shape, 0),
        lax.broadcasted_iota(jnp.int32, shape, 1),
    )


def pack(block, tag):
    width = block.shape[1]
    half = width // 2
    row, col = half_iota(width)
    lower = pltpu.roll(block[half:], half, 1)
    packed = jnp.where((col >= half) | (row <= col), block[:half], lower)
    diagonal = jnp.sum(jnp.where(row == col, lower, 0.0), axis=0, keepdims=True)
    rest = jnp.where(col[:1] < half, diagonal, tag)
    return packed, jnp.broadcast_to(rest, (TILE, width))


def unpack(packed, diagonal):
    half, width = packed.shape
    row, col = half_iota(width)
    turned = jnp.concatenate([packed, jnp.zeros_like(packed)], axis=0).T
    upper = jnp.where((col >= half) | (row <= col), packed, turned[:half])
    last = jnp.where(row > col, packed, jnp.where(row < col, turned[:half], diagonal))
    return upper, jnp.where(col < half, turned[half:], pltpu.roll(last, half, 1))


def gram_kernel(total_groups, half, groups_hbm, cols_hbm, *refs):
    groups_ref, cols_ref, rows_ref, groups_sem, cols_sems = refs[-5:]
    send_refs = refs[:-5]
    region_count, slot_count = groups_ref.shape
    width = cols_ref.shape[2] // slot_count
    me = lax.axis_index("group")
    my_half, my_slot = me // half, lax.rem(me, half)
    groups_copy = pltpu.make_async_copy(groups_hbm, groups_ref, groups_sem)
    groups_copy.start()

    depth = cols_ref.shape[1] // COPIES

    def cols_copy(region, part):
        rows = pl.ds(part * depth, depth)
        return pltpu.make_async_copy(
            cols_hbm.at[region, rows], cols_ref.at[region, rows], cols_sems.at[region, part]
        )

    for region in range(region_count):
        for part in range(COPIES):
            cols_copy(region, part).start()
    groups_copy.wait()
    packed = packed_rows(width)

    def add_region(region, carry):
        for part in range(COPIES):
            cols_copy(region, part).wait()
        cols = cols_ref[region]
        depth = cols.shape[1] // PRODUCTS
        grams = [
            lax.dot_general(
                cols[:, at * depth : (at + 1) * depth],
                cols,
                (((0,), (0,)), ((), ())),
                preferred_element_type=jnp.float32,
            )
            for at in range(PRODUCTS)
        ]
        groups = [groups_ref[region, s] for s in range(slot_count)]

        def ahead(s, t):
            return lax.rem(groups[t] - groups[s] + total_groups, total_groups)

        for s in range(slot_count):
            place = 0
            for t in range(slot_count):
                if t != s:
                    place = place + (ahead(t, s) < slot_count).astype(jnp.int32)
            away = (groups[s] // half != my_half).astype(jnp.int32)
            tag = (place + slot_count * away).astype(jnp.float32)
            slot = lax.rem(groups[s], half) ^ my_slot
            for t in range(slot_count):
                at = s * width % depth
                block = grams[s * width // depth][at : at + width, t * width : (t + 1) * width]
                if t == s:
                    block, rest = pack(block, tag)
                    rows_ref[slot, : width // 2] = block.astype(rows_ref.dtype)
                    rows_ref[slot, width // 2 : packed] = rest.astype(rows_ref.dtype)
                else:
                    gap = ahead(s, t)
                    turn = jnp.where(gap < slot_count, gap, gap - total_groups + slot_count)
                    at = pl.multiple_of(packed + (turn - 1) * width, TILE)
                    rows_ref[slot, pl.ds(at, width)] = block.astype(rows_ref.dtype)
        return carry

    lax.fori_loop(0, region_count, add_region, 0, unroll=region_count <= 2)
    for at, send_ref in enumerate(send_refs):
        first, last = row_range(at // CORES, width, slot_count)
        for pair in range(send_ref.shape[0]):
            send_ref[pair] = rows_ref[CORES * pair + at % CORES, first:last]


def sum_kernel(chunk, slot_count, *refs):
    arrays, (sums_ref, scaled_ref) = refs[:-2], refs[-2:]
    width = sums_ref.shape[1]
    half, packed = width // 2, packed_rows(width)
    count = sum_rows(chunk, width, slot_count)
    base = packed if chunk == 0 else 0
    sums_ref[...] = jnp.zeros_like(sums_ref)

    def units(arrays):
        return [(arrays[0], 0), (arrays[1], 0)] + [
            (x, core) for x in arrays[2:] for core in range(CORES)
        ]

    array_count = len(arrays) if chunk == 0 else len(arrays) // 2
    tags = [
        jnp.max(ref[at, half:packed].astype(jnp.float32)[TILE - 1 :, width - 1 :]).astype(
            jnp.int32
        )
        for ref, at in units(arrays[:array_count])
    ]
    for tag, (ref, at) in zip(tags, units(arrays[-array_count:])):
        away = tag // slot_count
        place = tag - slot_count * away
        if chunk == 0:
            to = pl.ds(pl.multiple_of(count * away, TILE), packed)
            sums_ref[to] += ref[at, :packed].astype(jnp.float32)
        for part, (turn, _) in enumerate(parts_of(chunk, slot_count)):
            wraps = (place + turn >= slot_count).astype(jnp.int32)
            to = count * away + base + (2 * part + wraps) * half
            block = ref[at, base + part * half : base + (part + 1) * half]
            sums_ref[pl.ds(pl.multiple_of(to, TILE), half)] += block.astype(jnp.float32)

    if chunk == 0:
        col = lax.broadcasted_iota(jnp.int32, (TILE, width), 1)
        for at in (half, count + half):
            sums_ref[at : at + TILE] = jnp.where(col < half, sums_ref[at : at + TILE], 0.0)

    tops = jnp.max(jnp.abs(sums_ref[count:]), axis=0, keepdims=True)
    largest = jnp.max(jnp.broadcast_to(tops, (8, width)), axis=1, keepdims=True)
    power = jnp.floor(jnp.log2(jnp.maximum(largest, 2.0**LEAST_POWER))) - TOP_POWER
    scaled_ref[:count] = sums_ref[count:] * jnp.exp2(-power)[0:1]
    scaled_ref[count:] = jnp.broadcast_to(power[0:1], (TILE, width))


def merge_kernel(keep_ref, got_ref, *refs):
    pair_count = keep_ref.shape[0]
    for at, send_ref in enumerate(refs[1 - pair_count :], 1):
        send_ref[0] = keep_ref[at]
        send_ref[1] = got_ref[at]


def join_kernel(chunk, slot_count, sums_ref, far_ref, *refs):
    out_hbm, joined_ref, sems = refs[-3:]
    width = joined_ref.shape[2]
    half, packed = width // 2, packed_rows(width)
    count = sum_rows(chunk, width, slot_count)
    factor = jnp.exp2(far_ref[count : count + 1])
    copies = []

    def joined(first, size):
        return sums_ref[first : first + size] + far_ref[first : first + size] * factor

    def put(block, offset, at):
        place = len(copies)
        joined_ref[place] = block
        copies.append(
            pltpu.make_async_copy(
                joined_ref.at[place],
                out_hbm.at[offset + slot_count - 1, at * half : (at + 1) * half],
                sems.at[place],
            )
        )
        copies[-1].start()

    base = 0
    if chunk == 0:
        base = packed
        for at, block in enumerate(unpack(joined(0, half), joined(half, 8)[:1])):
            put(block, 0, at)
    for part, (turn, at) in enumerate(parts_of(chunk, slot_count)):
        for wraps in range(2):
            first = base + (2 * part + wraps) * half
            put(joined(first, half), turn - slot_count * wraps, at)
    for copy in copies:
        copy.wait()


def order_of(chunk, pair):
    return (0 if chunk == 0 else -(pair.bit_length()), pair.bit_count(), -pair)


def shards(solve_cols, region_groups):
    region_count, row_count, col_count = solve_cols.shape
    slot_count = region_groups.shape[1]
    width = col_count // slot_count
    total_groups = lax.axis_size("group")
    half = region_count * slot_count
    span_count = 2 * slot_count - 1
    pair_count = half // CORES
    params = pltpu.CompilerParams(vmem_limit_bytes=VMEM_BYTES)
    light = pl.CostEstimate(flops=0, bytes_accessed=0, transcendentals=0)
    vmem = pl.BlockSpec(memory_space=pltpu.VMEM)
    hbm = pl.BlockSpec(memory_space=pltpu.HBM)

    def permute(values, step):
        pairs = [(d, d ^ step) for d in range(total_groups)]
        return lax.ppermute(values, "group", pairs)

    def blocks(count, chunk):
        first, last = row_range(chunk, width, slot_count)
        return jax.ShapeDtypeStruct((count, last - first, width), solve_cols.dtype)

    sends = pl.pallas_call(
        functools.partial(gram_kernel, total_groups, half),
        in_specs=[hbm] * 2,
        out_specs=[vmem] * (CHUNKS * CORES),
        out_shape=[blocks(pair_count, chunk) for chunk in range(CHUNKS) for _ in range(CORES)],
        scratch_shapes=[
            pltpu.SMEM(region_groups.shape, region_groups.dtype),
            pltpu.VMEM(solve_cols.shape, solve_cols.dtype),
            pltpu.VMEM((half, unit_rows(width, slot_count), width), solve_cols.dtype),
            pltpu.SemaphoreType.DMA,
            pltpu.SemaphoreType.DMA((region_count, COPIES)),
        ],
        cost_estimate=light,
        compiler_params=params,
        name="gram_rows",
    )(
        pltpu.with_memory_space_constraint(region_groups, pltpu.HBM),
        pltpu.with_memory_space_constraint(solve_cols, pltpu.HBM),
    )

    pieces, tagged = [], []
    for chunk in range(CHUNKS):
        keep, give = sends[CORES * chunk : CORES * (chunk + 1)]
        gots = [keep, permute(give, 1)]
        merged = pl.pallas_call(
            merge_kernel,
            out_shape=[blocks(CORES, chunk)] * (pair_count - 1),
            cost_estimate=light,
            compiler_params=params,
            name="merge_units",
        )(*gots, *tagged[CORES : CORES + chunk])
        chips = {}
        for pair in sorted(range(1, pair_count), key=functools.partial(order_of, chunk)):
            chips[pair] = permute(merged[pair - 1], CORES * pair)
        gots += [
            chips[pair]
            for pair in sorted(range(1, pair_count), key=functools.partial(order_of, 0))
        ]
        tagged = tagged or gots
        count = sum_rows(chunk, width, slot_count)
        sums, scaled = pl.pallas_call(
            functools.partial(sum_kernel, chunk, slot_count),
            out_shape=(
                jax.ShapeDtypeStruct((2 * count, width), jnp.float32),
                jax.ShapeDtypeStruct((count + TILE, width), jnp.float32),
            ),
            cost_estimate=light,
            compiler_params=params,
            name="sum_offsets",
        )(*(tagged if chunk == 0 else tagged + gots))
        far = permute(scaled.astype(jnp.float16), half)
        pieces.append((sums, far.astype(jnp.float32)))

    schur = ()
    for chunk in range(CHUNKS):
        count = 2 * len(parts_of(chunk, slot_count)) + (2 if chunk == 0 else 0)
        schur = (
            pl.pallas_call(
                functools.partial(join_kernel, chunk, slot_count),
                in_specs=[vmem] * 2 + [hbm] * len(schur),
                out_specs=hbm,
                out_shape=jax.ShapeDtypeStruct((span_count, width, width), jnp.float32),
                input_output_aliases={2: 0} if schur else {},
                scratch_shapes=[
                    pltpu.VMEM((count, width // 2, width), jnp.float32),
                    pltpu.SemaphoreType.DMA((count,)),
                ],
                cost_estimate=light,
                compiler_params=params,
                name="join_offsets",
            )(*pieces[chunk], *schur),
        )
    return schur[0][None]


def solution(mesh):
    return jax.shard_map(
        shards,
        mesh=mesh,
        in_specs=(P(("parts", "group"), None, None), P("group", None)),
        out_specs=P(("parts", "group"), None, None, None),
        check_vma=False,
    )
```

```python
import functools

import jax
import jax.numpy as jnp
from jax import lax
from jax.experimental import pallas as pl
from jax.experimental.pallas import tpu as pltpu
from jax.sharding import PartitionSpec as P

VMEM_BYTES = 48 * 1024 * 1024
LEAST_POWER = -100.0
TOP_POWER = 13.0
CHUNKS = 2
CORES = 2
COPIES = 2
TILE = 16
PRODUCTS = 2


def packed_rows(width):
    return width // 2 + TILE


def unit_rows(width, slot_count):
    return packed_rows(width) + (slot_count - 1) * width


def parts_of(chunk, slot_count):
    halves = [(turn, at) for turn in range(1, slot_count) for at in range(2)]
    size = len(halves) // CHUNKS
    return halves[chunk * size : (chunk + 1) * size]


def row_range(chunk, width, slot_count):
    size = len(parts_of(chunk, slot_count)) * (width // 2)
    first = packed_rows(width) + chunk * size
    return (0 if chunk == 0 else first), first + size


def sum_rows(chunk, width, slot_count):
    count = 2 * len(parts_of(chunk, slot_count)) * (width // 2)
    return count + (packed_rows(width) if chunk == 0 else 0)


def half_iota(width):
    shape = (width // 2, width)
    return (
        lax.broadcasted_iota(jnp.int32, shape, 0),
        lax.broadcasted_iota(jnp.int32, shape, 1),
    )


def pack(block, tag):
    width = block.shape[1]
    half = width // 2
    row, col = half_iota(width)
    lower = pltpu.roll(block[half:], half, 1)
    packed = jnp.where((col >= half) | (row <= col), block[:half], lower)
    diagonal = jnp.sum(jnp.where(row == col, lower, 0.0), axis=0, keepdims=True)
    rest = jnp.where(col[:1] < half, diagonal, tag)
    return packed, jnp.broadcast_to(rest, (TILE, width))


def unpack(packed, diagonal):
    half, width = packed.shape
    row, col = half_iota(width)
    turned = jnp.concatenate([packed, jnp.zeros_like(packed)], axis=0).T
    upper = jnp.where((col >= half) | (row <= col), packed, turned[:half])
    last = jnp.where(row > col, packed, jnp.where(row < col, turned[:half], diagonal))
    return upper, jnp.where(col < half, turned[half:], pltpu.roll(last, half, 1))


def gram_kernel(total_groups, half, groups_hbm, cols_hbm, *refs):
    groups_ref, cols_ref, rows_ref, groups_sem, cols_sems = refs[-5:]
    send_refs = refs[:-5]
    region_count, slot_count = groups_ref.shape
    width = cols_ref.shape[2] // slot_count
    me = lax.axis_index("group")
    my_half, my_slot = me // half, lax.rem(me, half)
    groups_copy = pltpu.make_async_copy(groups_hbm, groups_ref, groups_sem)
    groups_copy.start()

    depth = cols_ref.shape[1] // COPIES

    def cols_copy(region, part):
        rows = pl.ds(part * depth, depth)
        return pltpu.make_async_copy(
            cols_hbm.at[region, rows], cols_ref.at[region, rows], cols_sems.at[region, part]
        )

    for region in range(region_count):
        for part in range(COPIES):
            cols_copy(region, part).start()
    groups_copy.wait()
    packed = packed_rows(width)

    def add_region(region, carry):
        for part in range(COPIES):
            cols_copy(region, part).wait()
        cols = cols_ref[region]
        depth = cols.shape[1] // PRODUCTS
        grams = [
            lax.dot_general(
                cols[:, at * depth : (at + 1) * depth],
                cols,
                (((0,), (0,)), ((), ())),
                preferred_element_type=jnp.float32,
            )
            for at in range(PRODUCTS)
        ]
        groups = [groups_ref[region, s] for s in range(slot_count)]

        def ahead(s, t):
            return lax.rem(groups[t] - groups[s] + total_groups, total_groups)

        for s in range(slot_count):
            place = 0
            for t in range(slot_count):
                if t != s:
                    place = place + (ahead(t, s) < slot_count).astype(jnp.int32)
            away = (groups[s] // half != my_half).astype(jnp.int32)
            tag = (place + slot_count * away).astype(jnp.float32)
            slot = lax.rem(groups[s], half) ^ my_slot
            for t in range(slot_count):
                at = s * width % depth
                block = grams[s * width // depth][at : at + width, t * width : (t + 1) * width]
                if t == s:
                    block, rest = pack(block, tag)
                    rows_ref[slot, : width // 2] = block.astype(rows_ref.dtype)
                    rows_ref[slot, width // 2 : packed] = rest.astype(rows_ref.dtype)
                else:
                    gap = ahead(s, t)
                    turn = jnp.where(gap < slot_count, gap, gap - total_groups + slot_count)
                    at = pl.multiple_of(packed + (turn - 1) * width, TILE)
                    rows_ref[slot, pl.ds(at, width)] = block.astype(rows_ref.dtype)
        return carry

    lax.fori_loop(0, region_count, add_region, 0, unroll=region_count <= 2)
    for at, send_ref in enumerate(send_refs):
        first, last = row_range(at // CORES, width, slot_count)
        for pair in range(send_ref.shape[0]):
            send_ref[pair] = rows_ref[CORES * pair + at % CORES, first:last]


def order_of(chunk, pair_count):
    def key(pair):
        return (0 if chunk == 0 else -pair.bit_length(), pair.bit_count(), -pair)

    return sorted(range(1, pair_count), key=key)


def sum_kernel(chunk, slot_count, *refs):
    arrays, (sums_ref, scaled_ref) = refs[:-2], refs[-2:]
    width = sums_ref.shape[1]
    half, packed = width // 2, packed_rows(width)
    count = sum_rows(chunk, width, slot_count)
    base = packed if chunk == 0 else 0
    sums_ref[...] = jnp.zeros_like(sums_ref)

    def units(chunk, arrays):
        found = {(0, core): (arrays[core], 0) for core in range(CORES)}
        for pair, ref in zip(order_of(chunk, len(arrays) - CORES + 1), arrays[CORES:]):
            found.update({(pair, core): (ref, core) for core in range(CORES)})
        return found

    array_count = len(arrays) if chunk == 0 else len(arrays) // 2
    tags = {
        unit: jnp.max(
            ref[at, half:packed].astype(jnp.float32)[TILE - 1 :, width - 1 :]
        ).astype(jnp.int32)
        for unit, (ref, at) in units(0, arrays[:array_count]).items()
    }
    for unit, (ref, at) in units(chunk, arrays[-array_count:]).items():
        tag = tags[unit]
        away = tag // slot_count
        place = tag - slot_count * away
        if chunk == 0:
            to = pl.ds(pl.multiple_of(count * away, TILE), packed)
            sums_ref[to] += ref[at, :packed].astype(jnp.float32)
        for part, (turn, _) in enumerate(parts_of(chunk, slot_count)):
            wraps = (place + turn >= slot_count).astype(jnp.int32)
            to = count * away + base + (2 * part + wraps) * half
            block = ref[at, base + part * half : base + (part + 1) * half]
            sums_ref[pl.ds(pl.multiple_of(to, TILE), half)] += block.astype(jnp.float32)

    if chunk == 0:
        col = lax.broadcasted_iota(jnp.int32, (TILE, width), 1)
        for at in (half, count + half):
            sums_ref[at : at + TILE] = jnp.where(col < half, sums_ref[at : at + TILE], 0.0)

    tops = jnp.max(jnp.abs(sums_ref[count:]), axis=0, keepdims=True)
    largest = jnp.max(jnp.broadcast_to(tops, (8, width)), axis=1, keepdims=True)
    power = jnp.floor(jnp.log2(jnp.maximum(largest, 2.0**LEAST_POWER))) - TOP_POWER
    scaled_ref[:count] = sums_ref[count:] * jnp.exp2(-power)[0:1]
    scaled_ref[count:] = jnp.broadcast_to(power[0:1], (TILE, width))


def merge_kernel(keep_ref, got_ref, *refs):
    pair_count = keep_ref.shape[0]
    for at, send_ref in enumerate(refs[1 - pair_count :], 1):
        send_ref[0] = keep_ref[at]
        send_ref[1] = got_ref[at]


def join_kernel(chunk, slot_count, sums_ref, far_ref, *refs):
    out_hbm, joined_ref, sems = refs[-3:]
    width = joined_ref.shape[2]
    half, packed = width // 2, packed_rows(width)
    count = sum_rows(chunk, width, slot_count)
    factor = jnp.exp2(far_ref[count : count + 1])
    copies = []

    def joined(first, size):
        return sums_ref[first : first + size] + far_ref[first : first + size] * factor

    def put(block, offset, at):
        place = len(copies)
        joined_ref[place] = block
        copies.append(
            pltpu.make_async_copy(
                joined_ref.at[place],
                out_hbm.at[offset + slot_count - 1, at * half : (at + 1) * half],
                sems.at[place],
            )
        )
        copies[-1].start()

    base = 0
    if chunk == 0:
        base = packed
        for at, block in enumerate(unpack(joined(0, half), joined(half, 8)[:1])):
            put(block, 0, at)
    for part, (turn, at) in enumerate(parts_of(chunk, slot_count)):
        for wraps in range(2):
            first = base + (2 * part + wraps) * half
            put(joined(first, half), turn - slot_count * wraps, at)
    for copy in copies:
        copy.wait()


def shards(solve_cols, region_groups):
    region_count, row_count, col_count = solve_cols.shape
    slot_count = region_groups.shape[1]
    width = col_count // slot_count
    total_groups = lax.axis_size("group")
    half = region_count * slot_count
    span_count = 2 * slot_count - 1
    pair_count = half // CORES
    params = pltpu.CompilerParams(vmem_limit_bytes=VMEM_BYTES)
    light = pl.CostEstimate(flops=0, bytes_accessed=0, transcendentals=0)
    vmem = pl.BlockSpec(memory_space=pltpu.VMEM)
    hbm = pl.BlockSpec(memory_space=pltpu.HBM)

    def permute(values, step):
        pairs = [(d, d ^ step) for d in range(total_groups)]
        return lax.ppermute(values, "group", pairs)

    def blocks(count, chunk):
        first, last = row_range(chunk, width, slot_count)
        return jax.ShapeDtypeStruct((count, last - first, width), solve_cols.dtype)

    sends = pl.pallas_call(
        functools.partial(gram_kernel, total_groups, half),
        in_specs=[hbm] * 2,
        out_specs=[vmem] * (CHUNKS * CORES),
        out_shape=[blocks(pair_count, chunk) for chunk in range(CHUNKS) for _ in range(CORES)],
        scratch_shapes=[
            pltpu.SMEM(region_groups.shape, region_groups.dtype),
            pltpu.VMEM(solve_cols.shape, solve_cols.dtype),
            pltpu.VMEM((half, unit_rows(width, slot_count), width), solve_cols.dtype),
            pltpu.SemaphoreType.DMA,
            pltpu.SemaphoreType.DMA((region_count, COPIES)),
        ],
        cost_estimate=light,
        compiler_params=params,
        name="gram_rows",
    )(
        pltpu.with_memory_space_constraint(region_groups, pltpu.HBM),
        pltpu.with_memory_space_constraint(solve_cols, pltpu.HBM),
    )

    pieces, tagged = [], []
    for chunk in range(CHUNKS):
        keep, give = sends[CORES * chunk : CORES * (chunk + 1)]
        gots = [keep, permute(give, 1)]
        merged = pl.pallas_call(
            merge_kernel,
            out_shape=[blocks(CORES, chunk)] * (pair_count - 1),
            cost_estimate=light,
            compiler_params=params,
            name="merge_units",
        )(*gots, *tagged[CORES : CORES + chunk])
        for pair in order_of(chunk, pair_count):
            gots.append(permute(merged[pair - 1], CORES * pair))
        tagged = tagged or gots
        count = sum_rows(chunk, width, slot_count)
        sums, scaled = pl.pallas_call(
            functools.partial(sum_kernel, chunk, slot_count),
            out_shape=(
                jax.ShapeDtypeStruct((2 * count, width), jnp.float32),
                jax.ShapeDtypeStruct((count + TILE, width), jnp.float32),
            ),
            cost_estimate=light,
            compiler_params=params,
            name="sum_offsets",
        )(*(tagged if chunk == 0 else tagged + gots))
        far = permute(scaled.astype(jnp.float16), half)
        pieces.append((sums, far.astype(jnp.float32)))

    schur = ()
    for chunk in range(CHUNKS):
        count = 2 * len(parts_of(chunk, slot_count)) + (2 if chunk == 0 else 0)
        schur = (
            pl.pallas_call(
                functools.partial(join_kernel, chunk, slot_count),
                in_specs=[vmem] * 2 + [hbm] * len(schur),
                out_specs=hbm,
                out_shape=jax.ShapeDtypeStruct((span_count, width, width), jnp.float32),
                input_output_aliases={2: 0} if schur else {},
                scratch_shapes=[
                    pltpu.VMEM((count, width // 2, width), jnp.float32),
                    pltpu.SemaphoreType.DMA((count,)),
                ],
                cost_estimate=light,
                compiler_params=params,
                name="join_offsets",
            )(*pieces[chunk], *schur),
        )
    return schur[0][None]


def solution(mesh):
    return jax.shard_map(
        shards,
        mesh=mesh,
        in_specs=(P(("parts", "group"), None, None), P("group", None)),
        out_specs=P(("parts", "group"), None, None, None),
        check_vma=False,
    )
```

```python
import functools

import jax
import jax.numpy as jnp
from jax import lax
from jax.experimental import pallas as pl
from jax.experimental.pallas import tpu as pltpu
from jax.sharding import PartitionSpec as P

VMEM_BYTES = 48 * 1024 * 1024
LEAST_POWER = -100.0
TOP_POWER = 13.0
CHUNKS = 2
CORES = 2
COPIES = 2
TILE = 16
PRODUCTS = 2


def packed_rows(width):
    return width // 2 + TILE


def unit_rows(width, slot_count):
    return packed_rows(width) + (slot_count - 1) * width


def parts_of(chunk, slot_count):
    turns = range(1, 2) if chunk == 0 else range(2, slot_count)
    return [(turn, at) for turn in turns for at in range(2)]


def row_range(chunk, width, slot_count):
    last = packed_rows(width)
    for at in range(chunk + 1):
        first = last if at else 0
        last += len(parts_of(at, slot_count)) * (width // 2)
    return first, last


def sum_rows(chunk, width, slot_count):
    count = 2 * len(parts_of(chunk, slot_count)) * (width // 2)
    return count + (packed_rows(width) if chunk == 0 else 0)


def piece_rows(chunk, width, slot_count):
    count = sum_rows(chunk, width, slot_count)
    size = count if chunk == 0 else 3 * (width // 2)
    return [(at, min(at + size, count)) for at in range(0, count, size)]


def half_iota(width):
    shape = (width // 2, width)
    return (
        lax.broadcasted_iota(jnp.int32, shape, 0),
        lax.broadcasted_iota(jnp.int32, shape, 1),
    )


def pack(block, tag):
    width = block.shape[1]
    half = width // 2
    row, col = half_iota(width)
    lower = pltpu.roll(block[half:], half, 1)
    packed = jnp.where((col >= half) | (row <= col), block[:half], lower)
    diagonal = jnp.sum(jnp.where(row == col, lower, 0.0), axis=0, keepdims=True)
    rest = jnp.where(col[:1] < half, diagonal, tag)
    return packed, jnp.broadcast_to(rest, (TILE, width))


def unpack(packed, diagonal):
    half, width = packed.shape
    row, col = half_iota(width)
    turned = jnp.concatenate([packed, jnp.zeros_like(packed)], axis=0).T
    upper = jnp.where((col >= half) | (row <= col), packed, turned[:half])
    last = jnp.where(row > col, packed, jnp.where(row < col, turned[:half], diagonal))
    return upper, jnp.where(col < half, turned[half:], pltpu.roll(last, half, 1))


def gram_kernel(total_groups, half, groups_hbm, cols_hbm, *refs):
    groups_ref, cols_ref, rows_ref, groups_sem, cols_sems = refs[-5:]
    send_refs = refs[:-5]
    region_count, slot_count = groups_ref.shape
    width = cols_ref.shape[2] // slot_count
    me = lax.axis_index("group")
    my_half, my_slot = me // half, lax.rem(me, half)
    groups_copy = pltpu.make_async_copy(groups_hbm, groups_ref, groups_sem)
    groups_copy.start()

    depth = cols_ref.shape[1] // COPIES

    def cols_copy(region, part):
        rows = pl.ds(part * depth, depth)
        return pltpu.make_async_copy(
            cols_hbm.at[region, rows], cols_ref.at[region, rows], cols_sems.at[region, part]
        )

    for region in range(region_count):
        for part in range(COPIES):
            cols_copy(region, part).start()
    groups_copy.wait()
    packed = packed_rows(width)

    def add_region(region, carry):
        for part in range(COPIES):
            cols_copy(region, part).wait()
        cols = cols_ref[region]
        depth = cols.shape[1] // PRODUCTS
        grams = [
            lax.dot_general(
                cols[:, at * depth : (at + 1) * depth],
                cols,
                (((0,), (0,)), ((), ())),
                preferred_element_type=jnp.float32,
            )
            for at in range(PRODUCTS)
        ]
        groups = [groups_ref[region, s] for s in range(slot_count)]

        def ahead(s, t):
            return lax.rem(groups[t] - groups[s] + total_groups, total_groups)

        for s in range(slot_count):
            place = 0
            for t in range(slot_count):
                if t != s:
                    place = place + (ahead(t, s) < slot_count).astype(jnp.int32)
            away = (groups[s] // half != my_half).astype(jnp.int32)
            tag = (place + slot_count * away).astype(jnp.float32)
            slot = lax.rem(groups[s], half) ^ my_slot
            for t in range(slot_count):
                at = s * width % depth
                block = grams[s * width // depth][at : at + width, t * width : (t + 1) * width]
                if t == s:
                    block, rest = pack(block, tag)
                    rows_ref[slot, : width // 2] = block.astype(rows_ref.dtype)
                    rows_ref[slot, width // 2 : packed] = rest.astype(rows_ref.dtype)
                else:
                    gap = ahead(s, t)
                    turn = jnp.where(gap < slot_count, gap, gap - total_groups + slot_count)
                    at = pl.multiple_of(packed + (turn - 1) * width, TILE)
                    rows_ref[slot, pl.ds(at, width)] = block.astype(rows_ref.dtype)
        return carry

    lax.fori_loop(0, region_count, add_region, 0, unroll=region_count <= 2)
    for at, send_ref in enumerate(send_refs):
        first, last = row_range(at // CORES, width, slot_count)
        for pair in range(send_ref.shape[0]):
            send_ref[pair] = rows_ref[CORES * pair + at % CORES, first:last]


def order_of(chunk, pair_count):
    def key(pair):
        return (0 if chunk == 0 else -pair.bit_length(), pair.bit_count(), -pair)

    return sorted(range(1, pair_count), key=key)


def sum_kernel(chunk, slot_count, *refs):
    width = refs[-1].shape[1]
    pieces = piece_rows(chunk, width, slot_count)
    at = len(refs) - len(pieces) - 1
    arrays, sums_ref, scaled_refs = refs[:at], refs[at], refs[at + 1 :]
    half, packed = width // 2, packed_rows(width)
    count = sum_rows(chunk, width, slot_count)
    base = packed if chunk == 0 else 0
    sums_ref[...] = jnp.zeros_like(sums_ref)

    def units(chunk, arrays):
        found = {(0, core): (arrays[core], 0) for core in range(CORES)}
        for pair, ref in zip(order_of(chunk, len(arrays) - CORES + 1), arrays[CORES:]):
            found.update({(pair, core): (ref, core) for core in range(CORES)})
        return found

    array_count = len(arrays) if chunk == 0 else len(arrays) // 2
    tags = {
        unit: jnp.max(
            ref[at, half:packed].astype(jnp.float32)[TILE - 1 :, width - 1 :]
        ).astype(jnp.int32)
        for unit, (ref, at) in units(0, arrays[:array_count]).items()
    }
    for unit, (ref, at) in units(chunk, arrays[-array_count:]).items():
        tag = tags[unit]
        away = tag // slot_count
        place = tag - slot_count * away
        if chunk == 0:
            to = pl.ds(pl.multiple_of(count * away, TILE), packed)
            sums_ref[to] += ref[at, :packed].astype(jnp.float32)
        for part, (turn, _) in enumerate(parts_of(chunk, slot_count)):
            wraps = (place + turn >= slot_count).astype(jnp.int32)
            to = count * away + base + (2 * part + wraps) * half
            block = ref[at, base + part * half : base + (part + 1) * half]
            sums_ref[pl.ds(pl.multiple_of(to, TILE), half)] += block.astype(jnp.float32)

    if chunk == 0:
        col = lax.broadcasted_iota(jnp.int32, (TILE, width), 1)
        for at in (half, count + half):
            sums_ref[at : at + TILE] = jnp.where(col < half, sums_ref[at : at + TILE], 0.0)

    tops = jnp.max(jnp.abs(sums_ref[count:]), axis=0, keepdims=True)
    largest = jnp.max(jnp.broadcast_to(tops, (8, width)), axis=1, keepdims=True)
    power = jnp.floor(jnp.log2(jnp.maximum(largest, 2.0**LEAST_POWER))) - TOP_POWER
    factor = jnp.exp2(-power)[0:1]
    for scaled_ref, (first, last) in zip(scaled_refs, pieces):
        scaled_ref[: last - first] = sums_ref[count + first : count + last] * factor
        scaled_ref[last - first :] = jnp.broadcast_to(power[0:1], (TILE, width))


def merge_kernel(keep_ref, got_ref, *refs):
    pair_count = keep_ref.shape[0]
    for at, send_ref in enumerate(refs[1 - pair_count :], 1):
        send_ref[0] = keep_ref[at]
        send_ref[1] = got_ref[at]


def join_kernel(chunk, slot_count, sums_ref, *refs):
    out_hbm, joined_ref, sems = refs[-3:]
    width = joined_ref.shape[2]
    half, packed = width // 2, packed_rows(width)
    pieces = piece_rows(chunk, width, slot_count)
    size = pieces[0][1]
    factors = [
        jnp.exp2(ref[last - first : last - first + 1])
        for ref, (first, last) in zip(refs, pieces)
    ]
    copies = []

    def joined(first, rows):
        piece, at = first // size, first % size
        far = refs[piece][at : at + rows] * factors[piece]
        return sums_ref[first : first + rows] + far

    def put(block, offset, at):
        place = len(copies)
        joined_ref[place] = block
        copies.append(
            pltpu.make_async_copy(
                joined_ref.at[place],
                out_hbm.at[offset + slot_count - 1, at * half : (at + 1) * half],
                sems.at[place],
            )
        )
        copies[-1].start()

    base = 0
    if chunk == 0:
        base = packed
        for at, block in enumerate(unpack(joined(0, half), joined(half, 8)[:1])):
            put(block, 0, at)
    for part, (turn, at) in enumerate(parts_of(chunk, slot_count)):
        for wraps in range(2):
            first = base + (2 * part + wraps) * half
            put(joined(first, half), turn - slot_count * wraps, at)
    for copy in copies:
        copy.wait()


def shards(solve_cols, region_groups):
    region_count, row_count, col_count = solve_cols.shape
    slot_count = region_groups.shape[1]
    width = col_count // slot_count
    total_groups = lax.axis_size("group")
    half = region_count * slot_count
    span_count = 2 * slot_count - 1
    pair_count = half // CORES
    params = pltpu.CompilerParams(vmem_limit_bytes=VMEM_BYTES)
    light = pl.CostEstimate(flops=0, bytes_accessed=0, transcendentals=0)
    vmem = pl.BlockSpec(memory_space=pltpu.VMEM)
    hbm = pl.BlockSpec(memory_space=pltpu.HBM)

    def permute(values, step):
        pairs = [(d, d ^ step) for d in range(total_groups)]
        return lax.ppermute(values, "group", pairs)

    def blocks(count, chunk):
        first, last = row_range(chunk, width, slot_count)
        return jax.ShapeDtypeStruct((count, last - first, width), solve_cols.dtype)

    sends = pl.pallas_call(
        functools.partial(gram_kernel, total_groups, half),
        in_specs=[hbm] * 2,
        out_specs=[vmem] * (CHUNKS * CORES),
        out_shape=[blocks(pair_count, chunk) for chunk in range(CHUNKS) for _ in range(CORES)],
        scratch_shapes=[
            pltpu.SMEM(region_groups.shape, region_groups.dtype),
            pltpu.VMEM(solve_cols.shape, solve_cols.dtype),
            pltpu.VMEM((half, unit_rows(width, slot_count), width), solve_cols.dtype),
            pltpu.SemaphoreType.DMA,
            pltpu.SemaphoreType.DMA((region_count, COPIES)),
        ],
        cost_estimate=light,
        compiler_params=params,
        name="gram_rows",
    )(
        pltpu.with_memory_space_constraint(region_groups, pltpu.HBM),
        pltpu.with_memory_space_constraint(solve_cols, pltpu.HBM),
    )

    pieces, tagged = [], []
    for chunk in range(CHUNKS):
        keep, give = sends[CORES * chunk : CORES * (chunk + 1)]
        gots = [keep, permute(give, 1)]
        merged = pl.pallas_call(
            merge_kernel,
            out_shape=[blocks(CORES, chunk)] * (pair_count - 1),
            cost_estimate=light,
            compiler_params=params,
            name="merge_units",
        )(*gots, *tagged[CORES : CORES + chunk])
        for pair in order_of(chunk, pair_count):
            gots.append(permute(merged[pair - 1], CORES * pair))
        tagged = tagged or gots
        count = sum_rows(chunk, width, slot_count)
        sums, *scaled = pl.pallas_call(
            functools.partial(sum_kernel, chunk, slot_count),
            out_shape=[jax.ShapeDtypeStruct((2 * count, width), jnp.float32)]
            + [
                jax.ShapeDtypeStruct((last - first + TILE, width), jnp.float32)
                for first, last in piece_rows(chunk, width, slot_count)
            ],
            cost_estimate=light,
            compiler_params=params,
            name="sum_offsets",
        )(*(tagged if chunk == 0 else tagged + gots))
        far = [permute(piece.astype(jnp.float16), half) for piece in scaled]
        pieces.append([sums] + [piece.astype(jnp.float32) for piece in far])

    schur = ()
    for chunk in range(CHUNKS):
        count = 2 * len(parts_of(chunk, slot_count)) + (2 if chunk == 0 else 0)
        schur = (
            pl.pallas_call(
                functools.partial(join_kernel, chunk, slot_count),
                in_specs=[vmem] * len(pieces[chunk]) + [hbm] * len(schur),
                out_specs=hbm,
                out_shape=jax.ShapeDtypeStruct((span_count, width, width), jnp.float32),
                input_output_aliases={len(pieces[chunk]): 0} if schur else {},
                scratch_shapes=[
                    pltpu.VMEM((count, width // 2, width), jnp.float32),
                    pltpu.SemaphoreType.DMA((count,)),
                ],
                cost_estimate=light,
                compiler_params=params,
                name="join_offsets",
            )(*pieces[chunk], *schur),
        )
    return schur[0][None]


def solution(mesh):
    return jax.shard_map(
        shards,
        mesh=mesh,
        in_specs=(P(("parts", "group"), None, None), P("group", None)),
        out_specs=P(("parts", "group"), None, None, None),
        check_vma=False,
    )
```

```python
import functools

import jax
import jax.numpy as jnp
from jax import lax
from jax.experimental import pallas as pl
from jax.experimental.pallas import tpu as pltpu
from jax.sharding import PartitionSpec as P

VMEM_BYTES = 48 * 1024 * 1024
LEAST_POWER = -100.0
TOP_POWER = 13.0
CHUNKS = 2
CORES = 2
COPIES = 2
TILE = 16
PRODUCTS = 2


def packed_rows(width):
    return width // 2 + TILE


def unit_rows(width, slot_count):
    return packed_rows(width) + (slot_count - 1) * width


def parts_of(chunk, slot_count):
    halves = [(turn, at) for turn in range(1, slot_count) for at in range(2)]
    size = len(halves) // CHUNKS
    return halves[chunk * size : (chunk + 1) * size]


def row_range(chunk, width, slot_count):
    size = len(parts_of(chunk, slot_count)) * (width // 2)
    first = packed_rows(width) + chunk * size
    return (0 if chunk == 0 else first), first + size


def sum_rows(chunk, width, slot_count):
    count = 2 * len(parts_of(chunk, slot_count)) * (width // 2)
    return count + (packed_rows(width) if chunk == 0 else 0)


def half_iota(width):
    shape = (width // 2, width)
    return (
        lax.broadcasted_iota(jnp.int32, shape, 0),
        lax.broadcasted_iota(jnp.int32, shape, 1),
    )


def pack(block, tag):
    width = block.shape[1]
    half = width // 2
    row, col = half_iota(width)
    lower = pltpu.roll(block[half:], half, 1)
    packed = jnp.where((col >= half) | (row <= col), block[:half], lower)
    diagonal = jnp.sum(jnp.where(row == col, lower, 0.0), axis=0, keepdims=True)
    rest = jnp.where(col[:1] < half, diagonal, tag)
    return packed, jnp.broadcast_to(rest, (TILE, width))


def unpack(packed, diagonal):
    half, width = packed.shape
    row, col = half_iota(width)
    turned = jnp.concatenate([packed, jnp.zeros_like(packed)], axis=0).T
    upper = jnp.where((col >= half) | (row <= col), packed, turned[:half])
    last = jnp.where(row > col, packed, jnp.where(row < col, turned[:half], diagonal))
    return upper, jnp.where(col < half, turned[half:], pltpu.roll(last, half, 1))


def gram_kernel(total_groups, half, groups_hbm, cols_hbm, *refs):
    groups_ref, cols_ref, rows_ref, groups_sem, cols_sems = refs[-5:]
    send_refs = refs[:-5]
    region_count, slot_count = groups_ref.shape
    width = cols_ref.shape[2] // slot_count
    me = lax.axis_index("group")
    my_half, my_slot = me // half, lax.rem(me, half)
    groups_copy = pltpu.make_async_copy(groups_hbm, groups_ref, groups_sem)
    groups_copy.start()

    depth = cols_ref.shape[1] // COPIES

    def cols_copy(region, part):
        rows = pl.ds(part * depth, depth)
        return pltpu.make_async_copy(
            cols_hbm.at[region, rows], cols_ref.at[region, rows], cols_sems.at[region, part]
        )

    for region in range(region_count):
        for part in range(COPIES):
            cols_copy(region, part).start()
    groups_copy.wait()
    packed = packed_rows(width)

    def add_region(region, carry):
        for part in range(COPIES):
            cols_copy(region, part).wait()
        cols = cols_ref[region]
        depth = cols.shape[1] // PRODUCTS
        grams = [
            lax.dot_general(
                cols[:, at * depth : (at + 1) * depth],
                cols,
                (((0,), (0,)), ((), ())),
                preferred_element_type=jnp.float32,
            )
            for at in range(PRODUCTS)
        ]
        groups = [groups_ref[region, s] for s in range(slot_count)]

        def ahead(s, t):
            return lax.rem(groups[t] - groups[s] + total_groups, total_groups)

        for s in range(slot_count):
            place = 0
            for t in range(slot_count):
                if t != s:
                    place = place + (ahead(t, s) < slot_count).astype(jnp.int32)
            away = (groups[s] // half != my_half).astype(jnp.int32)
            tag = (place + slot_count * away).astype(jnp.float32)
            slot = lax.rem(groups[s], half) ^ my_slot
            for t in range(slot_count):
                at = s * width % depth
                block = grams[s * width // depth][at : at + width, t * width : (t + 1) * width]
                if t == s:
                    block, rest = pack(block, tag)
                    rows_ref[slot, : width // 2] = block.astype(rows_ref.dtype)
                    rows_ref[slot, width // 2 : packed] = rest.astype(rows_ref.dtype)
                else:
                    gap = ahead(s, t)
                    turn = jnp.where(gap < slot_count, gap, gap - total_groups + slot_count)
                    at = pl.multiple_of(packed + (turn - 1) * width, TILE)
                    rows_ref[slot, pl.ds(at, width)] = block.astype(rows_ref.dtype)
        return carry

    lax.fori_loop(0, region_count, add_region, 0, unroll=region_count <= 2)
    for at, send_ref in enumerate(send_refs):
        first, last = row_range(at // CORES, width, slot_count)
        for pair in range(send_ref.shape[0]):
            send_ref[pair] = rows_ref[CORES * pair + at % CORES, first:last]


def order_of(chunk, pair_count):
    def key(pair):
        return (0 if chunk == 0 else -pair.bit_length(), pair.bit_count(), -pair)

    return sorted(range(1, pair_count), key=key)


def sum_kernel(chunk, slot_count, last, *refs):
    width = refs[-1].shape[1]
    half, packed = width // 2, packed_rows(width)
    count = sum_rows(chunk, width, slot_count)
    base = packed if chunk == 0 else 0
    if last:
        before_ref, *arrays, sums_ref, scaled_ref = refs
        sums_ref[...] = before_ref[...]
    else:
        *arrays, sums_ref = refs
        sums_ref[...] = jnp.zeros_like(sums_ref)

    def units(arrays):
        own = 0 if last else CORES
        return [(ref, 0) for ref in arrays[:own]] + [
            (ref, core) for ref in arrays[own:] for core in range(CORES)
        ]

    array_count = len(arrays) // (chunk + 1)
    tags = [
        jnp.max(ref[at, half:packed].astype(jnp.float32)[TILE - 1 :, width - 1 :]).astype(
            jnp.int32
        )
        for ref, at in units(arrays[:array_count])
    ]
    for tag, (ref, at) in zip(tags, units(arrays[-array_count:])):
        away = tag // slot_count
        place = tag - slot_count * away
        if chunk == 0:
            to = pl.ds(pl.multiple_of(count * away, TILE), packed)
            sums_ref[to] += ref[at, :packed].astype(jnp.float32)
        for part, (turn, _) in enumerate(parts_of(chunk, slot_count)):
            wraps = (place + turn >= slot_count).astype(jnp.int32)
            to = count * away + base + (2 * part + wraps) * half
            block = ref[at, base + part * half : base + (part + 1) * half]
            sums_ref[pl.ds(pl.multiple_of(to, TILE), half)] += block.astype(jnp.float32)

    if not last:
        return
    if chunk == 0:
        col = lax.broadcasted_iota(jnp.int32, (TILE, width), 1)
        for at in (half, count + half):
            sums_ref[at : at + TILE] = jnp.where(col < half, sums_ref[at : at + TILE], 0.0)

    tops = jnp.max(jnp.abs(sums_ref[count:]), axis=0, keepdims=True)
    largest = jnp.max(jnp.broadcast_to(tops, (8, width)), axis=1, keepdims=True)
    power = jnp.floor(jnp.log2(jnp.maximum(largest, 2.0**LEAST_POWER))) - TOP_POWER
    scaled_ref[:count] = sums_ref[count:] * jnp.exp2(-power)[0:1]
    scaled_ref[count:] = jnp.broadcast_to(power[0:1], (TILE, width))


def merge_kernel(keep_ref, got_ref, *refs):
    pair_count = keep_ref.shape[0]
    for at, send_ref in enumerate(refs[1 - pair_count :], 1):
        send_ref[0] = keep_ref[at]
        send_ref[1] = got_ref[at]


def join_kernel(chunk, slot_count, sums_ref, far_ref, *refs):
    out_hbm, joined_ref, sems = refs[-3:]
    width = joined_ref.shape[2]
    half, packed = width // 2, packed_rows(width)
    count = sum_rows(chunk, width, slot_count)
    factor = jnp.exp2(far_ref[count : count + 1])
    copies = []

    def joined(first, size):
        return sums_ref[first : first + size] + far_ref[first : first + size] * factor

    def put(block, offset, at):
        place = len(copies)
        joined_ref[place] = block
        copies.append(
            pltpu.make_async_copy(
                joined_ref.at[place],
                out_hbm.at[offset + slot_count - 1, at * half : (at + 1) * half],
                sems.at[place],
            )
        )
        copies[-1].start()

    base = 0
    if chunk == 0:
        base = packed
        for at, block in enumerate(unpack(joined(0, half), joined(half, 8)[:1])):
            put(block, 0, at)
    for part, (turn, at) in enumerate(parts_of(chunk, slot_count)):
        for wraps in range(2):
            first = base + (2 * part + wraps) * half
            put(joined(first, half), turn - slot_count * wraps, at)
    for copy in copies:
        copy.wait()


def shards(solve_cols, region_groups):
    region_count, row_count, col_count = solve_cols.shape
    slot_count = region_groups.shape[1]
    width = col_count // slot_count
    total_groups = lax.axis_size("group")
    half = region_count * slot_count
    span_count = 2 * slot_count - 1
    pair_count = half // CORES
    params = pltpu.CompilerParams(vmem_limit_bytes=VMEM_BYTES)
    light = pl.CostEstimate(flops=0, bytes_accessed=0, transcendentals=0)
    vmem = pl.BlockSpec(memory_space=pltpu.VMEM)
    hbm = pl.BlockSpec(memory_space=pltpu.HBM)

    def permute(values, step):
        pairs = [(d, d ^ step) for d in range(total_groups)]
        return lax.ppermute(values, "group", pairs)

    def blocks(count, chunk):
        first, last = row_range(chunk, width, slot_count)
        return jax.ShapeDtypeStruct((count, last - first, width), solve_cols.dtype)

    sends = pl.pallas_call(
        functools.partial(gram_kernel, total_groups, half),
        in_specs=[hbm] * 2,
        out_specs=[vmem] * (CHUNKS * CORES),
        out_shape=[blocks(pair_count, chunk) for chunk in range(CHUNKS) for _ in range(CORES)],
        scratch_shapes=[
            pltpu.SMEM(region_groups.shape, region_groups.dtype),
            pltpu.VMEM(solve_cols.shape, solve_cols.dtype),
            pltpu.VMEM((half, unit_rows(width, slot_count), width), solve_cols.dtype),
            pltpu.SemaphoreType.DMA,
            pltpu.SemaphoreType.DMA((region_count, COPIES)),
        ],
        cost_estimate=light,
        compiler_params=params,
        name="gram_rows",
    )(
        pltpu.with_memory_space_constraint(region_groups, pltpu.HBM),
        pltpu.with_memory_space_constraint(solve_cols, pltpu.HBM),
    )

    pieces, tagged = [], []
    for chunk in range(CHUNKS):
        keep, give = sends[CORES * chunk : CORES * (chunk + 1)]
        gots = [keep, permute(give, 1)]
        merged = pl.pallas_call(
            merge_kernel,
            out_shape=[blocks(CORES, chunk)] * (pair_count - 1),
            cost_estimate=light,
            compiler_params=params,
            name="merge_units",
        )(*gots, *tagged[CORES : CORES + chunk])
        for pair in order_of(chunk, pair_count):
            gots.append(permute(merged[pair - 1], CORES * pair))
        tagged = tagged or gots
        count = sum_rows(chunk, width, slot_count)
        shape = jax.ShapeDtypeStruct((2 * count, width), jnp.float32)
        scaled = jax.ShapeDtypeStruct((count + TILE, width), jnp.float32)
        by_chip = dict(zip(order_of(0, pair_count), tagged[CORES:]))
        tags = tagged[:CORES] + [by_chip[pair] for pair in order_of(chunk, pair_count)]
        sums = ()
        for last, arrays in ((False, slice(0, -1)), (True, slice(-1, None))):
            sums = pl.pallas_call(
                functools.partial(sum_kernel, chunk, slot_count, last),
                out_shape=(shape, scaled) if last else (shape,),
                cost_estimate=light,
                compiler_params=params,
                name="sum_offsets",
            )(*sums, *(tags[arrays] if chunk else ()), *gots[arrays])
        sums, scaled = sums
        far = permute(scaled.astype(jnp.float16), half)
        pieces.append((sums, far.astype(jnp.float32)))

    schur = ()
    for chunk in range(CHUNKS):
        count = 2 * len(parts_of(chunk, slot_count)) + (2 if chunk == 0 else 0)
        schur = (
            pl.pallas_call(
                functools.partial(join_kernel, chunk, slot_count),
                in_specs=[vmem] * 2 + [hbm] * len(schur),
                out_specs=hbm,
                out_shape=jax.ShapeDtypeStruct((span_count, width, width), jnp.float32),
                input_output_aliases={2: 0} if schur else {},
                scratch_shapes=[
                    pltpu.VMEM((count, width // 2, width), jnp.float32),
                    pltpu.SemaphoreType.DMA((count,)),
                ],
                cost_estimate=light,
                compiler_params=params,
                name="join_offsets",
            )(*pieces[chunk], *schur),
        )
    return schur[0][None]


def solution(mesh):
    return jax.shard_map(
        shards,
        mesh=mesh,
        in_specs=(P(("parts", "group"), None, None), P("group", None)),
        out_specs=P(("parts", "group"), None, None, None),
        check_vma=False,
    )
```

```python
import functools

import jax
import jax.numpy as jnp
from jax import lax
from jax.experimental import pallas as pl
from jax.experimental.pallas import tpu as pltpu
from jax.sharding import PartitionSpec as P

VMEM_BYTES = 48 * 1024 * 1024
LEAST_POWER = -100.0
TOP_POWER = 13.0
CHUNKS = 2
CORES = 2
COPIES = 2
TILE = 16
PRODUCTS = 2


def packed_rows(width):
    return width // 2 + TILE


def unit_rows(width, slot_count):
    return packed_rows(width) + (slot_count - 1) * width


def parts_of(chunk, slot_count):
    halves = [(turn, at) for turn in range(1, slot_count) for at in range(2)]
    size = len(halves) // CHUNKS
    return halves[chunk * size : (chunk + 1) * size]


def row_range(chunk, width, slot_count):
    size = len(parts_of(chunk, slot_count)) * (width // 2)
    first = packed_rows(width) + chunk * size
    return (0 if chunk == 0 else first), first + size


def sum_rows(chunk, width, slot_count):
    count = 2 * len(parts_of(chunk, slot_count)) * (width // 2)
    return count + (packed_rows(width) if chunk == 0 else 0)


def half_iota(width):
    shape = (width // 2, width)
    return (
        lax.broadcasted_iota(jnp.int32, shape, 0),
        lax.broadcasted_iota(jnp.int32, shape, 1),
    )


def pack(block, tag):
    width = block.shape[1]
    half = width // 2
    row, col = half_iota(width)
    lower = pltpu.roll(block[half:], half, 1)
    packed = jnp.where((col >= half) | (row <= col), block[:half], lower)
    diagonal = jnp.sum(jnp.where(row == col, lower, 0.0), axis=0, keepdims=True)
    rest = jnp.where(col[:1] < half, diagonal, tag)
    return packed, jnp.broadcast_to(rest, (TILE, width))


def unpack(packed, diagonal):
    half, width = packed.shape
    row, col = half_iota(width)
    turned = jnp.concatenate([packed, jnp.zeros_like(packed)], axis=0).T
    upper = jnp.where((col >= half) | (row <= col), packed, turned[:half])
    last = jnp.where(row > col, packed, jnp.where(row < col, turned[:half], diagonal))
    return upper, jnp.where(col < half, turned[half:], pltpu.roll(last, half, 1))


def gram_kernel(total_groups, half, groups_hbm, cols_hbm, *refs):
    groups_ref, cols_ref, rows_ref, groups_sem, cols_sems = refs[-5:]
    send_refs = refs[:-5]
    region_count, slot_count = groups_ref.shape
    width = cols_ref.shape[2] // slot_count
    me = lax.axis_index("group")
    my_half, my_slot = me // half, lax.rem(me, half)
    groups_copy = pltpu.make_async_copy(groups_hbm, groups_ref, groups_sem)
    groups_copy.start()

    depth = cols_ref.shape[1] // COPIES

    def cols_copy(region, part):
        rows = pl.ds(part * depth, depth)
        return pltpu.make_async_copy(
            cols_hbm.at[region, rows], cols_ref.at[region, rows], cols_sems.at[region, part]
        )

    for region in range(region_count):
        for part in range(COPIES):
            cols_copy(region, part).start()
    groups_copy.wait()
    for region in range(region_count):
        for part in range(COPIES):
            cols_copy(region, part).wait()
    packed = packed_rows(width)

    def add_region(region, carry):
        cols = cols_ref[region]
        depth = cols.shape[1] // PRODUCTS
        grams = [
            lax.dot_general(
                cols[:, at * depth : (at + 1) * depth],
                cols,
                (((0,), (0,)), ((), ())),
                preferred_element_type=jnp.float32,
            )
            for at in range(PRODUCTS)
        ]
        groups = [groups_ref[region, s] for s in range(slot_count)]

        def ahead(s, t):
            return lax.rem(groups[t] - groups[s] + total_groups, total_groups)

        for s in range(slot_count):
            place = 0
            for t in range(slot_count):
                if t != s:
                    place = place + (ahead(t, s) < slot_count).astype(jnp.int32)
            away = (groups[s] // half != my_half).astype(jnp.int32)
            tag = (place + slot_count * away).astype(jnp.float32)
            slot = lax.rem(groups[s], half) ^ my_slot
            for t in range(slot_count):
                at = s * width % depth
                block = grams[s * width // depth][at : at + width, t * width : (t + 1) * width]
                if t == s:
                    block, rest = pack(block, tag)
                    rows_ref[slot, : width // 2] = block.astype(rows_ref.dtype)
                    rows_ref[slot, width // 2 : packed] = rest.astype(rows_ref.dtype)
                else:
                    gap = ahead(s, t)
                    turn = jnp.where(gap < slot_count, gap, gap - total_groups + slot_count)
                    at = pl.multiple_of(packed + (turn - 1) * width, TILE)
                    rows_ref[slot, pl.ds(at, width)] = block.astype(rows_ref.dtype)
        return carry

    lax.fori_loop(0, region_count, add_region, 0, unroll=region_count <= 2)
    for at, send_ref in enumerate(send_refs):
        first, last = row_range(at // CORES, width, slot_count)
        for pair in range(send_ref.shape[0]):
            send_ref[pair] = rows_ref[CORES * pair + at % CORES, first:last]


def order_of(chunk, pair_count):
    def key(pair):
        return (0 if chunk == 0 else -pair.bit_length(), pair.bit_count(), -pair)

    return sorted(range(1, pair_count), key=key)


def sum_kernel(chunk, slot_count, first, last, *refs):
    width = refs[-1].shape[1]
    half, packed = width // 2, packed_rows(width)
    count = sum_rows(chunk, width, slot_count)
    base = packed if chunk == 0 else 0
    arrays = list(refs)
    scaled_ref = arrays.pop() if last else None
    sums_ref = arrays.pop()
    sums_ref[...] = jnp.zeros_like(sums_ref) if first else arrays.pop(0)[...]

    def units(arrays):
        own = CORES if first else 0
        return [(ref, 0) for ref in arrays[:own]] + [
            (ref, core) for ref in arrays[own:] for core in range(CORES)
        ]

    array_count = len(arrays) // (chunk + 1)
    tags = [
        jnp.max(ref[at, half:packed].astype(jnp.float32)[TILE - 1 :, width - 1 :]).astype(
            jnp.int32
        )
        for ref, at in units(arrays[:array_count])
    ]
    for tag, (ref, at) in zip(tags, units(arrays[-array_count:])):
        away = tag // slot_count
        place = tag - slot_count * away
        if chunk == 0:
            to = pl.ds(pl.multiple_of(count * away, TILE), packed)
            sums_ref[to] += ref[at, :packed].astype(jnp.float32)
        for part, (turn, _) in enumerate(parts_of(chunk, slot_count)):
            wraps = (place + turn >= slot_count).astype(jnp.int32)
            to = count * away + base + (2 * part + wraps) * half
            block = ref[at, base + part * half : base + (part + 1) * half]
            sums_ref[pl.ds(pl.multiple_of(to, TILE), half)] += block.astype(jnp.float32)

    if not last:
        return
    if chunk == 0:
        col = lax.broadcasted_iota(jnp.int32, (TILE, width), 1)
        for at in (half, count + half):
            sums_ref[at : at + TILE] = jnp.where(col < half, sums_ref[at : at + TILE], 0.0)

    tops = jnp.max(jnp.abs(sums_ref[count:]), axis=0, keepdims=True)
    largest = jnp.max(jnp.broadcast_to(tops, (8, width)), axis=1, keepdims=True)
    power = jnp.floor(jnp.log2(jnp.maximum(largest, 2.0**LEAST_POWER))) - TOP_POWER
    scaled_ref[:count] = sums_ref[count:] * jnp.exp2(-power)[0:1]
    scaled_ref[count:] = jnp.broadcast_to(power[0:1], (TILE, width))


def merge_kernel(keep_ref, got_ref, *refs):
    pair_count = keep_ref.shape[0]
    for at, send_ref in enumerate(refs[1 - pair_count :], 1):
        send_ref[0] = keep_ref[at]
        send_ref[1] = got_ref[at]


def join_kernel(chunk, slot_count, sums_ref, far_ref, *refs):
    out_hbm, joined_ref, sems = refs[-3:]
    width = joined_ref.shape[2]
    half, packed = width // 2, packed_rows(width)
    count = sum_rows(chunk, width, slot_count)
    factor = jnp.exp2(far_ref[count : count + 1])
    copies = []

    def joined(first, size):
        return sums_ref[first : first + size] + far_ref[first : first + size] * factor

    def put(block, offset, at):
        place = len(copies)
        joined_ref[place] = block
        copies.append(
            pltpu.make_async_copy(
                joined_ref.at[place],
                out_hbm.at[offset + slot_count - 1, at * half : (at + 1) * half],
                sems.at[place],
            )
        )
        copies[-1].start()

    base = 0
    if chunk == 0:
        base = packed
        for at, block in enumerate(unpack(joined(0, half), joined(half, 8)[:1])):
            put(block, 0, at)
    for part, (turn, at) in enumerate(parts_of(chunk, slot_count)):
        for wraps in range(2):
            first = base + (2 * part + wraps) * half
            put(joined(first, half), turn - slot_count * wraps, at)
    for copy in copies:
        copy.wait()


def shards(solve_cols, region_groups):
    region_count, row_count, col_count = solve_cols.shape
    slot_count = region_groups.shape[1]
    width = col_count // slot_count
    total_groups = lax.axis_size("group")
    half = region_count * slot_count
    span_count = 2 * slot_count - 1
    pair_count = half // CORES
    params = pltpu.CompilerParams(vmem_limit_bytes=VMEM_BYTES)
    light = pl.CostEstimate(flops=0, bytes_accessed=0, transcendentals=0)
    vmem = pl.BlockSpec(memory_space=pltpu.VMEM)
    hbm = pl.BlockSpec(memory_space=pltpu.HBM)

    def permute(values, step):
        pairs = [(d, d ^ step) for d in range(total_groups)]
        return lax.ppermute(values, "group", pairs)

    def blocks(count, chunk):
        first, last = row_range(chunk, width, slot_count)
        return jax.ShapeDtypeStruct((count, last - first, width), solve_cols.dtype)

    sends = pl.pallas_call(
        functools.partial(gram_kernel, total_groups, half),
        in_specs=[hbm] * 2,
        out_specs=[vmem] * (CHUNKS * CORES),
        out_shape=[blocks(pair_count, chunk) for chunk in range(CHUNKS) for _ in range(CORES)],
        scratch_shapes=[
            pltpu.SMEM(region_groups.shape, region_groups.dtype),
            pltpu.VMEM(solve_cols.shape, solve_cols.dtype),
            pltpu.VMEM((half, unit_rows(width, slot_count), width), solve_cols.dtype),
            pltpu.SemaphoreType.DMA,
            pltpu.SemaphoreType.DMA((region_count, COPIES)),
        ],
        cost_estimate=light,
        compiler_params=params,
        name="gram_rows",
    )(
        pltpu.with_memory_space_constraint(region_groups, pltpu.HBM),
        pltpu.with_memory_space_constraint(solve_cols, pltpu.HBM),
    )

    pieces, tagged = [], []
    for chunk in range(CHUNKS):
        keep, give = sends[CORES * chunk : CORES * (chunk + 1)]
        gots = [keep, permute(give, 1)]
        merged = pl.pallas_call(
            merge_kernel,
            out_shape=[blocks(CORES, chunk)] * (pair_count - 1),
            cost_estimate=light,
            compiler_params=params,
            name="merge_units",
        )(*gots, *tagged[CORES : CORES + chunk])
        for pair in order_of(chunk, pair_count):
            gots.append(permute(merged[pair - 1], CORES * pair))
        tagged = tagged or gots
        count = sum_rows(chunk, width, slot_count)
        shape = jax.ShapeDtypeStruct((2 * count, width), jnp.float32)
        scaled = jax.ShapeDtypeStruct((count + TILE, width), jnp.float32)
        by_chip = dict(zip(order_of(0, pair_count), tagged[CORES:]))
        tags = tagged[:CORES] + [by_chip[pair] for pair in order_of(chunk, pair_count)]
        sums = ()
        calls = [(0, -1), (-1, None)] if chunk == 0 else [(0, None)]
        for begin, end in calls:
            first, last, arrays = begin == 0, end is None, slice(begin, end)
            sums = pl.pallas_call(
                functools.partial(sum_kernel, chunk, slot_count, first, last),
                out_shape=(shape, scaled) if last else (shape,),
                cost_estimate=light,
                compiler_params=params,
                name="sum_offsets",
            )(*sums, *(tags[arrays] if chunk else ()), *gots[arrays])
        sums, scaled = sums
        far = permute(scaled.astype(jnp.float16), half)
        pieces.append((sums, far.astype(jnp.float32)))

    schur = ()
    for chunk in range(CHUNKS):
        count = 2 * len(parts_of(chunk, slot_count)) + (2 if chunk == 0 else 0)
        schur = (
            pl.pallas_call(
                functools.partial(join_kernel, chunk, slot_count),
                in_specs=[vmem] * 2 + [hbm] * len(schur),
                out_specs=hbm,
                out_shape=jax.ShapeDtypeStruct((span_count, width, width), jnp.float32),
                input_output_aliases={2: 0} if schur else {},
                scratch_shapes=[
                    pltpu.VMEM((count, width // 2, width), jnp.float32),
                    pltpu.SemaphoreType.DMA((count,)),
                ],
                cost_estimate=light,
                compiler_params=params,
                name="join_offsets",
            )(*pieces[chunk], *schur),
        )
    return schur[0][None]


def solution(mesh):
    return jax.shard_map(
        shards,
        mesh=mesh,
        in_specs=(P(("parts", "group"), None, None), P("group", None)),
        out_specs=P(("parts", "group"), None, None, None),
        check_vma=False,
    )
```

```python
import functools

import jax
import jax.numpy as jnp
from jax import lax
from jax.experimental import pallas as pl
from jax.experimental.pallas import tpu as pltpu
from jax.sharding import PartitionSpec as P

VMEM_BYTES = 48 * 1024 * 1024
LEAST_POWER = -100.0
TOP_POWER = 13.0
CHUNKS = 2
CORES = 2
COPIES = 2
TILE = 16
PRODUCTS = 2


def packed_rows(width):
    return width // 2 + TILE


def unit_rows(width, slot_count):
    return packed_rows(width) + (slot_count - 1) * width


def parts_of(chunk, slot_count):
    halves = [(turn, at) for turn in range(1, slot_count) for at in range(2)]
    size = len(halves) // CHUNKS
    return halves[chunk * size : (chunk + 1) * size]


def row_range(chunk, width, slot_count):
    size = len(parts_of(chunk, slot_count)) * (width // 2)
    first = packed_rows(width) + chunk * size
    return (0 if chunk == 0 else first), first + size


def sum_rows(chunk, width, slot_count):
    count = 2 * len(parts_of(chunk, slot_count)) * (width // 2)
    return count + (packed_rows(width) if chunk == 0 else 0)


def half_iota(width):
    shape = (width // 2, width)
    return (
        lax.broadcasted_iota(jnp.int32, shape, 0),
        lax.broadcasted_iota(jnp.int32, shape, 1),
    )


def pack(block, tag):
    width = block.shape[1]
    half = width // 2
    row, col = half_iota(width)
    lower = pltpu.roll(block[half:], half, 1)
    packed = jnp.where((col >= half) | (row <= col), block[:half], lower)
    diagonal = jnp.sum(jnp.where(row == col, lower, 0.0), axis=0, keepdims=True)
    rest = jnp.where(col[:1] < half, diagonal, tag)
    return packed, jnp.broadcast_to(rest, (TILE, width))


def unpack(packed, diagonal):
    half, width = packed.shape
    row, col = half_iota(width)
    turned = jnp.concatenate([packed, jnp.zeros_like(packed)], axis=0).T
    upper = jnp.where((col >= half) | (row <= col), packed, turned[:half])
    last = jnp.where(row > col, packed, jnp.where(row < col, turned[:half], diagonal))
    return upper, jnp.where(col < half, turned[half:], pltpu.roll(last, half, 1))


def gram_kernel(total_groups, half, groups_hbm, cols_hbm, *refs):
    groups_ref, cols_ref, rows_ref, groups_sem, cols_sems = refs[-5:]
    send_refs = refs[:-5]
    region_count, slot_count = groups_ref.shape
    width = cols_ref.shape[2] // slot_count
    me = lax.axis_index("group")
    my_half, my_slot = me // half, lax.rem(me, half)
    groups_copy = pltpu.make_async_copy(groups_hbm, groups_ref, groups_sem)
    groups_copy.start()

    depth = cols_ref.shape[1] // COPIES

    def cols_copy(region, part):
        rows = pl.ds(part * depth, depth)
        return pltpu.make_async_copy(
            cols_hbm.at[region, rows], cols_ref.at[region, rows], cols_sems.at[region, part]
        )

    for region in range(region_count):
        for part in range(COPIES):
            cols_copy(region, part).start()
    groups_copy.wait()
    for region in range(region_count):
        for part in range(COPIES):
            cols_copy(region, part).wait()
    packed = packed_rows(width)

    def add_region(region, carry):
        cols = cols_ref[region]
        depth = cols.shape[1] // PRODUCTS
        grams = [
            lax.dot_general(
                cols[:, at * depth : (at + 1) * depth],
                cols,
                (((0,), (0,)), ((), ())),
                preferred_element_type=jnp.float32,
            )
            for at in range(PRODUCTS)
        ]
        groups = [groups_ref[region, s] for s in range(slot_count)]

        def ahead(s, t):
            return lax.rem(groups[t] - groups[s] + total_groups, total_groups)

        for s in range(slot_count):
            place = 0
            for t in range(slot_count):
                if t != s:
                    place = place + (ahead(t, s) < slot_count).astype(jnp.int32)
            away = (groups[s] // half != my_half).astype(jnp.int32)
            tag = (place + slot_count * away).astype(jnp.float32)
            slot = lax.rem(groups[s], half) ^ my_slot
            for t in range(slot_count):
                at = s * width % depth
                block = grams[s * width // depth][at : at + width, t * width : (t + 1) * width]
                if t == s:
                    block, rest = pack(block, tag)
                    rows_ref[slot, : width // 2] = block.astype(rows_ref.dtype)
                    rows_ref[slot, width // 2 : packed] = rest.astype(rows_ref.dtype)
                else:
                    gap = ahead(s, t)
                    turn = jnp.where(gap < slot_count, gap, gap - total_groups + slot_count)
                    at = pl.multiple_of(packed + (turn - 1) * width, TILE)
                    rows_ref[slot, pl.ds(at, width)] = block.astype(rows_ref.dtype)
        return carry

    lax.fori_loop(0, region_count, add_region, 0, unroll=region_count <= 2)
    for at, send_ref in enumerate(send_refs):
        first, last = row_range(at // CORES, width, slot_count)
        for pair in range(send_ref.shape[0]):
            send_ref[pair] = rows_ref[CORES * pair + at % CORES, first:last]


def order_of(pair_count):
    def key(pair):
        return (-pair.bit_length(), pair.bit_count(), -pair)

    return sorted(range(1, pair_count), key=key)


def sum_kernel(chunk, slot_count, *refs):
    width = refs[-1].shape[1]
    half, packed = width // 2, packed_rows(width)
    count = sum_rows(chunk, width, slot_count)
    base = packed if chunk == 0 else 0
    *arrays, sums_ref, scaled_ref = refs
    sums_ref[...] = jnp.zeros_like(sums_ref)

    def units(arrays):
        return [(ref, 0) for ref in arrays[:CORES]] + [
            (ref, core) for ref in arrays[CORES:] for core in range(CORES)
        ]

    array_count = len(arrays) // (chunk + 1)
    tags = [
        jnp.max(ref[at, half:packed].astype(jnp.float32)[TILE - 1 :, width - 1 :]).astype(
            jnp.int32
        )
        for ref, at in units(arrays[:array_count])
    ]
    for tag, (ref, at) in zip(tags, units(arrays[-array_count:])):
        away = tag // slot_count
        place = tag - slot_count * away
        if chunk == 0:
            to = pl.ds(pl.multiple_of(count * away, TILE), packed)
            sums_ref[to] += ref[at, :packed].astype(jnp.float32)
        for part, (turn, _) in enumerate(parts_of(chunk, slot_count)):
            wraps = (place + turn >= slot_count).astype(jnp.int32)
            to = count * away + base + (2 * part + wraps) * half
            block = ref[at, base + part * half : base + (part + 1) * half]
            sums_ref[pl.ds(pl.multiple_of(to, TILE), half)] += block.astype(jnp.float32)

    if chunk == 0:
        col = lax.broadcasted_iota(jnp.int32, (TILE, width), 1)
        for at in (half, count + half):
            sums_ref[at : at + TILE] = jnp.where(col < half, sums_ref[at : at + TILE], 0.0)

    tops = jnp.max(jnp.abs(sums_ref[count:]), axis=0, keepdims=True)
    largest = jnp.max(jnp.broadcast_to(tops, (8, width)), axis=1, keepdims=True)
    power = jnp.floor(jnp.log2(jnp.maximum(largest, 2.0**LEAST_POWER))) - TOP_POWER
    scaled_ref[:count] = sums_ref[count:] * jnp.exp2(-power)[0:1]
    scaled_ref[count:] = jnp.broadcast_to(power[0:1], (TILE, width))


def merge_kernel(keep_ref, got_ref, *refs):
    pair_count = keep_ref.shape[0]
    for at, send_ref in enumerate(refs[1 - pair_count :], 1):
        send_ref[0] = keep_ref[at]
        send_ref[1] = got_ref[at]


def join_kernel(chunk, slot_count, sums_ref, far_ref, *refs):
    out_hbm, joined_ref, sems = refs[-3:]
    width = joined_ref.shape[2]
    half, packed = width // 2, packed_rows(width)
    count = sum_rows(chunk, width, slot_count)
    factor = jnp.exp2(far_ref[count : count + 1])
    copies = []

    def joined(first, size):
        return sums_ref[first : first + size] + far_ref[first : first + size] * factor

    def put(block, offset, at):
        place = len(copies)
        joined_ref[place] = block
        copies.append(
            pltpu.make_async_copy(
                joined_ref.at[place],
                out_hbm.at[offset + slot_count - 1, at * half : (at + 1) * half],
                sems.at[place],
            )
        )
        copies[-1].start()

    base = 0
    if chunk == 0:
        base = packed
        for at, block in enumerate(unpack(joined(0, half), joined(half, 8)[:1])):
            put(block, 0, at)
    for part, (turn, at) in enumerate(parts_of(chunk, slot_count)):
        for wraps in range(2):
            first = base + (2 * part + wraps) * half
            put(joined(first, half), turn - slot_count * wraps, at)
    for copy in copies:
        copy.wait()


def shards(solve_cols, region_groups):
    region_count, row_count, col_count = solve_cols.shape
    slot_count = region_groups.shape[1]
    width = col_count // slot_count
    total_groups = lax.axis_size("group")
    half = region_count * slot_count
    span_count = 2 * slot_count - 1
    pair_count = half // CORES
    params = pltpu.CompilerParams(vmem_limit_bytes=VMEM_BYTES)
    light = pl.CostEstimate(flops=0, bytes_accessed=0, transcendentals=0)
    vmem = pl.BlockSpec(memory_space=pltpu.VMEM)
    hbm = pl.BlockSpec(memory_space=pltpu.HBM)

    def permute(values, step):
        pairs = [(d, d ^ step) for d in range(total_groups)]
        return lax.ppermute(values, "group", pairs)

    def blocks(count, chunk):
        first, last = row_range(chunk, width, slot_count)
        return jax.ShapeDtypeStruct((count, last - first, width), solve_cols.dtype)

    sends = pl.pallas_call(
        functools.partial(gram_kernel, total_groups, half),
        in_specs=[hbm] * 2,
        out_specs=[vmem] * (CHUNKS * CORES),
        out_shape=[blocks(pair_count, chunk) for chunk in range(CHUNKS) for _ in range(CORES)],
        scratch_shapes=[
            pltpu.SMEM(region_groups.shape, region_groups.dtype),
            pltpu.VMEM(solve_cols.shape, solve_cols.dtype),
            pltpu.VMEM((half, unit_rows(width, slot_count), width), solve_cols.dtype),
            pltpu.SemaphoreType.DMA,
            pltpu.SemaphoreType.DMA((region_count, COPIES)),
        ],
        cost_estimate=light,
        compiler_params=params,
        name="gram_rows",
    )(
        pltpu.with_memory_space_constraint(region_groups, pltpu.HBM),
        pltpu.with_memory_space_constraint(solve_cols, pltpu.HBM),
    )

    pieces, tagged = [], []
    for chunk in range(CHUNKS):
        keep, give = sends[CORES * chunk : CORES * (chunk + 1)]
        gots = [keep, permute(give, 1)]
        merged = pl.pallas_call(
            merge_kernel,
            out_shape=[blocks(CORES, chunk)] * (pair_count - 1),
            cost_estimate=light,
            compiler_params=params,
            name="merge_units",
        )(*gots, *tagged[CORES : CORES + chunk])
        for pair in order_of(pair_count):
            gots.append(permute(merged[pair - 1], CORES * pair))
        tagged = tagged or gots
        count = sum_rows(chunk, width, slot_count)
        shape = jax.ShapeDtypeStruct((2 * count, width), jnp.float32)
        scaled = jax.ShapeDtypeStruct((count + TILE, width), jnp.float32)
        sums, scaled = pl.pallas_call(
            functools.partial(sum_kernel, chunk, slot_count),
            out_shape=(shape, scaled),
            cost_estimate=light,
            compiler_params=params,
            name="sum_offsets",
        )(*(tagged if chunk else ()), *gots)
        far = permute(scaled.astype(jnp.float16), half)
        pieces.append((sums, far.astype(jnp.float32)))

    schur = ()
    for chunk in range(CHUNKS):
        count = 2 * len(parts_of(chunk, slot_count)) + (2 if chunk == 0 else 0)
        schur = (
            pl.pallas_call(
                functools.partial(join_kernel, chunk, slot_count),
                in_specs=[vmem] * 2 + [hbm] * len(schur),
                out_specs=hbm,
                out_shape=jax.ShapeDtypeStruct((span_count, width, width), jnp.float32),
                input_output_aliases={2: 0} if schur else {},
                scratch_shapes=[
                    pltpu.VMEM((count, width // 2, width), jnp.float32),
                    pltpu.SemaphoreType.DMA((count,)),
                ],
                cost_estimate=light,
                compiler_params=params,
                name="join_offsets",
            )(*pieces[chunk], *schur),
        )
    return schur[0][None]


def solution(mesh):
    return jax.shard_map(
        shards,
        mesh=mesh,
        in_specs=(P(("parts", "group"), None, None), P("group", None)),
        out_specs=P(("parts", "group"), None, None, None),
        check_vma=False,
    )
```

```python
import functools

import jax
import jax.numpy as jnp
from jax import lax
from jax.experimental import pallas as pl
from jax.experimental.pallas import tpu as pltpu
from jax.sharding import PartitionSpec as P

VMEM_BYTES = 48 * 1024 * 1024
LEAST_POWER = -100.0
TOP_POWER = 13.0
CHUNKS = 2
CORES = 2
COPIES = 2
TILE = 16
PRODUCTS = 2


def packed_rows(width):
    return width // 2 + TILE


def unit_rows(width, slot_count):
    return packed_rows(width) + (slot_count - 1) * width


def parts_of(chunk, slot_count):
    halves = [(turn, at) for turn in range(1, slot_count) for at in range(2)]
    size = len(halves) // CHUNKS
    return halves[chunk * size : (chunk + 1) * size]


def row_range(chunk, width, slot_count):
    size = len(parts_of(chunk, slot_count)) * (width // 2)
    first = packed_rows(width) + chunk * size
    return (0 if chunk == 0 else first), first + size


def sum_rows(chunk, width, slot_count):
    count = 2 * len(parts_of(chunk, slot_count)) * (width // 2)
    return count + (packed_rows(width) if chunk == 0 else 0)


def half_iota(width):
    shape = (width // 2, width)
    return (
        lax.broadcasted_iota(jnp.int32, shape, 0),
        lax.broadcasted_iota(jnp.int32, shape, 1),
    )


def pack(block, tag):
    width = block.shape[1]
    half = width // 2
    row, col = half_iota(width)
    lower = pltpu.roll(block[half:], half, 1)
    packed = jnp.where((col >= half) | (row <= col), block[:half], lower)
    diagonal = jnp.sum(jnp.where(row == col, lower, 0.0), axis=0, keepdims=True)
    rest = jnp.where(col[:1] < half, diagonal, tag)
    return packed, jnp.broadcast_to(rest, (TILE, width))


def unpack(packed, diagonal):
    half, width = packed.shape
    row, col = half_iota(width)
    turned = jnp.concatenate([packed, jnp.zeros_like(packed)], axis=0).T
    upper = jnp.where((col >= half) | (row <= col), packed, turned[:half])
    last = jnp.where(row > col, packed, jnp.where(row < col, turned[:half], diagonal))
    return upper, jnp.where(col < half, turned[half:], pltpu.roll(last, half, 1))


def gram_kernel(total_groups, half, groups_hbm, cols_hbm, *refs):
    groups_ref, cols_ref, rows_ref, groups_sem, cols_sems = refs[-5:]
    send_refs = refs[:-5]
    region_count, slot_count = groups_ref.shape
    width = cols_ref.shape[2] // slot_count
    me = lax.axis_index("group")
    my_half, my_slot = me // half, lax.rem(me, half)
    groups_copy = pltpu.make_async_copy(groups_hbm, groups_ref, groups_sem)
    groups_copy.start()

    depth = cols_ref.shape[1] // COPIES

    def cols_copy(region, part):
        rows = pl.ds(part * depth, depth)
        return pltpu.make_async_copy(
            cols_hbm.at[region, rows], cols_ref.at[region, rows], cols_sems.at[region, part]
        )

    for region in range(region_count):
        for part in range(COPIES):
            cols_copy(region, part).start()
    groups_copy.wait()
    for region in range(region_count):
        for part in range(COPIES):
            cols_copy(region, part).wait()
    packed = packed_rows(width)

    def add_region(region, carry):
        cols = cols_ref[region]
        depth = cols.shape[1] // PRODUCTS
        grams = [
            lax.dot_general(
                cols[:, at * depth : (at + 1) * depth],
                cols,
                (((0,), (0,)), ((), ())),
                preferred_element_type=jnp.float32,
            )
            for at in range(PRODUCTS)
        ]
        groups = [groups_ref[region, s] for s in range(slot_count)]

        def ahead(s, t):
            return lax.rem(groups[t] - groups[s] + total_groups, total_groups)

        for s in range(slot_count):
            place = 0
            for t in range(slot_count):
                if t != s:
                    place = place + (ahead(t, s) < slot_count).astype(jnp.int32)
            away = (groups[s] // half != my_half).astype(jnp.int32)
            tag = (place + slot_count * away).astype(jnp.float32)
            slot = lax.rem(groups[s], half) ^ my_slot
            for t in range(slot_count):
                at = s * width % depth
                block = grams[s * width // depth][at : at + width, t * width : (t + 1) * width]
                if t == s:
                    block, rest = pack(block, tag)
                    rows_ref[slot, : width // 2] = block.astype(rows_ref.dtype)
                    rows_ref[slot, width // 2 : packed] = rest.astype(rows_ref.dtype)
                else:
                    gap = ahead(s, t)
                    turn = jnp.where(gap < slot_count, gap, gap - total_groups + slot_count)
                    at = pl.multiple_of(packed + (turn - 1) * width, TILE)
                    rows_ref[slot, pl.ds(at, width)] = block.astype(rows_ref.dtype)
        return carry

    lax.fori_loop(0, region_count, add_region, 0, unroll=region_count <= 2)
    for at, send_ref in enumerate(send_refs):
        first, last = row_range(at // CORES, width, slot_count)
        for pair in range(send_ref.shape[0]):
            send_ref[pair] = rows_ref[CORES * pair + at % CORES, first:last]


def order_of(chunk, pair_count):
    def key(pair):
        return (0 if chunk == 0 else -pair.bit_length(), pair.bit_count(), -pair)

    return sorted(range(1, pair_count), key=key)


def sum_kernel(chunk, slot_count, first, last, *refs):
    width = refs[-1].shape[1]
    half, packed = width // 2, packed_rows(width)
    count = sum_rows(chunk, width, slot_count)
    base = packed if chunk == 0 else 0
    arrays = list(refs)
    scaled_ref = arrays.pop() if last else None
    sums_ref = arrays.pop()
    sums_ref[...] = jnp.zeros_like(sums_ref) if first else arrays.pop(0)[...]

    def units(arrays):
        own = CORES if first else 0
        return [(ref, 0) for ref in arrays[:own]] + [
            (ref, core) for ref in arrays[own:] for core in range(CORES)
        ]

    array_count = len(arrays) // (chunk + 1)
    tags = [
        jnp.max(ref[at, half:packed].astype(jnp.float32)[TILE - 1 :, width - 1 :]).astype(
            jnp.int32
        )
        for ref, at in units(arrays[:array_count])
    ]
    for tag, (ref, at) in zip(tags, units(arrays[-array_count:])):
        away = tag // slot_count
        place = tag - slot_count * away
        if chunk == 0:
            to = pl.ds(pl.multiple_of(count * away, TILE), packed)
            sums_ref[to] += ref[at, :packed].astype(jnp.float32)
        for part, (turn, _) in enumerate(parts_of(chunk, slot_count)):
            wraps = (place + turn >= slot_count).astype(jnp.int32)
            to = count * away + base + (2 * part + wraps) * half
            block = ref[at, base + part * half : base + (part + 1) * half]
            sums_ref[pl.ds(pl.multiple_of(to, TILE), half)] += block.astype(jnp.float32)

    if not last:
        return
    if chunk == 0:
        col = lax.broadcasted_iota(jnp.int32, (TILE, width), 1)
        for at in (half, count + half):
            sums_ref[at : at + TILE] = jnp.where(col < half, sums_ref[at : at + TILE], 0.0)

    tops = jnp.max(jnp.abs(sums_ref[count:]), axis=0, keepdims=True)
    largest = jnp.max(jnp.broadcast_to(tops, (8, width)), axis=1, keepdims=True)
    power = jnp.floor(jnp.log2(jnp.maximum(largest, 2.0**LEAST_POWER))) - TOP_POWER
    scaled_ref[:count] = sums_ref[count:] * jnp.exp2(-power)[0:1]
    if chunk == 0:
        scaled_ref[half:packed] = jnp.where(col < half, scaled_ref[half:packed], power[0:1])
    else:
        scaled_ref[count:] = jnp.broadcast_to(power[0:1], (TILE, width))


def merge_kernel(keep_ref, got_ref, *refs):
    pair_count = keep_ref.shape[0]
    for at, send_ref in enumerate(refs[1 - pair_count :], 1):
        send_ref[0] = keep_ref[at]
        send_ref[1] = got_ref[at]


def join_kernel(chunk, slot_count, sums_ref, far_ref, *refs):
    out_hbm, joined_ref, sems = refs[-3:]
    width = joined_ref.shape[2]
    half, packed = width // 2, packed_rows(width)
    at = half if chunk == 0 else sum_rows(chunk, width, slot_count)
    factor = jnp.exp2(far_ref[at : at + 8][:1, width - 1 :])
    copies = []

    def joined(first, size):
        return sums_ref[first : first + size] + far_ref[first : first + size] * factor

    def put(block, offset, at):
        place = len(copies)
        joined_ref[place] = block
        copies.append(
            pltpu.make_async_copy(
                joined_ref.at[place],
                out_hbm.at[offset + slot_count - 1, at * half : (at + 1) * half],
                sems.at[place],
            )
        )
        copies[-1].start()

    base = 0
    if chunk == 0:
        base = packed
        for at, block in enumerate(unpack(joined(0, half), joined(half, 8)[:1])):
            put(block, 0, at)
    for part, (turn, at) in enumerate(parts_of(chunk, slot_count)):
        for wraps in range(2):
            first = base + (2 * part + wraps) * half
            put(joined(first, half), turn - slot_count * wraps, at)
    for copy in copies:
        copy.wait()


def shards(solve_cols, region_groups):
    region_count, row_count, col_count = solve_cols.shape
    slot_count = region_groups.shape[1]
    width = col_count // slot_count
    total_groups = lax.axis_size("group")
    half = region_count * slot_count
    span_count = 2 * slot_count - 1
    pair_count = half // CORES
    params = pltpu.CompilerParams(vmem_limit_bytes=VMEM_BYTES)
    light = pl.CostEstimate(flops=0, bytes_accessed=0, transcendentals=0)
    vmem = pl.BlockSpec(memory_space=pltpu.VMEM)
    hbm = pl.BlockSpec(memory_space=pltpu.HBM)

    def permute(values, step):
        pairs = [(d, d ^ step) for d in range(total_groups)]
        return lax.ppermute(values, "group", pairs)

    def blocks(count, chunk):
        first, last = row_range(chunk, width, slot_count)
        return jax.ShapeDtypeStruct((count, last - first, width), solve_cols.dtype)

    sends = pl.pallas_call(
        functools.partial(gram_kernel, total_groups, half),
        in_specs=[hbm] * 2,
        out_specs=[vmem] * (CHUNKS * CORES),
        out_shape=[blocks(pair_count, chunk) for chunk in range(CHUNKS) for _ in range(CORES)],
        scratch_shapes=[
            pltpu.SMEM(region_groups.shape, region_groups.dtype),
            pltpu.VMEM(solve_cols.shape, solve_cols.dtype),
            pltpu.VMEM((half, unit_rows(width, slot_count), width), solve_cols.dtype),
            pltpu.SemaphoreType.DMA,
            pltpu.SemaphoreType.DMA((region_count, COPIES)),
        ],
        cost_estimate=light,
        compiler_params=params,
        name="gram_rows",
    )(
        pltpu.with_memory_space_constraint(region_groups, pltpu.HBM),
        pltpu.with_memory_space_constraint(solve_cols, pltpu.HBM),
    )

    pieces, tagged = [], []
    for chunk in range(CHUNKS):
        keep, give = sends[CORES * chunk : CORES * (chunk + 1)]
        gots = [keep, permute(give, 1)]
        merged = pl.pallas_call(
            merge_kernel,
            out_shape=[blocks(CORES, chunk)] * (pair_count - 1),
            cost_estimate=light,
            compiler_params=params,
            name="merge_units",
        )(*gots, *tagged[CORES : CORES + chunk])
        for pair in order_of(chunk, pair_count):
            gots.append(permute(merged[pair - 1], CORES * pair))
        tagged = tagged or gots
        count = sum_rows(chunk, width, slot_count)
        shape = jax.ShapeDtypeStruct((2 * count, width), jnp.float32)
        scaled = jax.ShapeDtypeStruct((count + TILE * chunk, width), jnp.float32)
        by_chip = dict(zip(order_of(0, pair_count), tagged[CORES:]))
        tags = tagged[:CORES] + [by_chip[pair] for pair in order_of(chunk, pair_count)]
        sums = ()
        calls = [(0, -1), (-1, None)] if chunk == 0 else [(0, None)]
        for begin, end in calls:
            first, last, arrays = begin == 0, end is None, slice(begin, end)
            sums = pl.pallas_call(
                functools.partial(sum_kernel, chunk, slot_count, first, last),
                out_shape=(shape, scaled) if last else (shape,),
                cost_estimate=light,
                compiler_params=params,
                name="sum_offsets",
            )(*sums, *(tags[arrays] if chunk else ()), *gots[arrays])
        sums, scaled = sums
        far = permute(scaled.astype(jnp.float16), half)
        pieces.append((sums, far.astype(jnp.float32)))

    schur = ()
    for chunk in range(CHUNKS):
        count = 2 * len(parts_of(chunk, slot_count)) + (2 if chunk == 0 else 0)
        schur = (
            pl.pallas_call(
                functools.partial(join_kernel, chunk, slot_count),
                in_specs=[vmem] * 2 + [hbm] * len(schur),
                out_specs=hbm,
                out_shape=jax.ShapeDtypeStruct((span_count, width, width), jnp.float32),
                input_output_aliases={2: 0} if schur else {},
                scratch_shapes=[
                    pltpu.VMEM((count, width // 2, width), jnp.float32),
                    pltpu.SemaphoreType.DMA((count,)),
                ],
                cost_estimate=light,
                compiler_params=params,
                name="join_offsets",
            )(*pieces[chunk], *schur),
        )
    return schur[0][None]


def solution(mesh):
    return jax.shard_map(
        shards,
        mesh=mesh,
        in_specs=(P(("parts", "group"), None, None), P("group", None)),
        out_specs=P(("parts", "group"), None, None, None),
        check_vma=False,
    )
```

```python
import functools

import jax
import jax.numpy as jnp
from jax import lax
from jax.experimental import pallas as pl
from jax.experimental.pallas import tpu as pltpu
from jax.sharding import PartitionSpec as P

VMEM_BYTES = 48 * 1024 * 1024
LEAST_POWER = -100.0
TOP_POWER = 13.0
CHUNKS = 2
CORES = 2
COPIES = 2
TILE = 16
PRODUCTS = 2


def packed_rows(width):
    return width // 2 + TILE


def unit_rows(width, slot_count):
    return packed_rows(width) + (slot_count - 1) * width


def parts_of(chunk, slot_count):
    halves = [(turn, at) for turn in range(1, slot_count) for at in range(2)]
    size = len(halves) // CHUNKS
    return halves[chunk * size : (chunk + 1) * size]


def row_range(chunk, width, slot_count):
    size = len(parts_of(chunk, slot_count)) * (width // 2)
    first = packed_rows(width) + chunk * size
    return (0 if chunk == 0 else first), first + size


def sum_rows(chunk, width, slot_count):
    count = 2 * len(parts_of(chunk, slot_count)) * (width // 2)
    return count + (packed_rows(width) if chunk == 0 else 0)


def half_iota(width):
    shape = (width // 2, width)
    return (
        lax.broadcasted_iota(jnp.int32, shape, 0),
        lax.broadcasted_iota(jnp.int32, shape, 1),
    )


def pack(block, tag):
    width = block.shape[1]
    half = width // 2
    row, col = half_iota(width)
    lower = pltpu.roll(block[half:], half, 1)
    packed = jnp.where((col >= half) | (row <= col), block[:half], lower)
    diagonal = jnp.sum(jnp.where(row == col, lower, 0.0), axis=0, keepdims=True)
    rest = jnp.where(col[:1] < half, diagonal, tag)
    return packed, jnp.broadcast_to(rest, (TILE, width))


def unpack(packed, diagonal):
    half, width = packed.shape
    row, col = half_iota(width)
    turned = jnp.concatenate([packed, jnp.zeros_like(packed)], axis=0).T
    upper = jnp.where((col >= half) | (row <= col), packed, turned[:half])
    last = jnp.where(row > col, packed, jnp.where(row < col, turned[:half], diagonal))
    return upper, jnp.where(col < half, turned[half:], pltpu.roll(last, half, 1))


def gram_kernel(total_groups, half, groups_hbm, cols_hbm, *refs):
    groups_ref, cols_ref, rows_ref, groups_sem, cols_sems = refs[-5:]
    send_refs = refs[:-5]
    region_count, slot_count = groups_ref.shape
    width = cols_ref.shape[2] // slot_count
    me = lax.axis_index("group")
    my_half, my_slot = me // half, lax.rem(me, half)
    groups_copy = pltpu.make_async_copy(groups_hbm, groups_ref, groups_sem)
    groups_copy.start()

    depth = cols_ref.shape[1] // COPIES

    def cols_copy(region, part):
        rows = pl.ds(part * depth, depth)
        return pltpu.make_async_copy(
            cols_hbm.at[region, rows], cols_ref.at[region, rows], cols_sems.at[region, part]
        )

    for region in range(region_count):
        for part in range(COPIES):
            cols_copy(region, part).start()
    groups_copy.wait()
    for region in range(region_count):
        for part in range(COPIES):
            cols_copy(region, part).wait()
    packed = packed_rows(width)

    def add_region(region, carry):
        cols = cols_ref[region]
        depth = cols.shape[1] // PRODUCTS
        grams = [
            lax.dot_general(
                cols[:, at * depth : (at + 1) * depth],
                cols,
                (((0,), (0,)), ((), ())),
                preferred_element_type=jnp.float32,
            )
            for at in range(PRODUCTS)
        ]
        groups = [groups_ref[region, s] for s in range(slot_count)]

        def ahead(s, t):
            return lax.rem(groups[t] - groups[s] + total_groups, total_groups)

        for s in range(slot_count):
            place = 0
            for t in range(slot_count):
                if t != s:
                    place = place + (ahead(t, s) < slot_count).astype(jnp.int32)
            away = (groups[s] // half != my_half).astype(jnp.int32)
            tag = (place + slot_count * away).astype(jnp.float32)
            slot = lax.rem(groups[s], half) ^ my_slot
            for t in range(slot_count):
                at = s * width % depth
                block = grams[s * width // depth][at : at + width, t * width : (t + 1) * width]
                if t == s:
                    block, rest = pack(block, tag)
                    rows_ref[slot, : width // 2] = block.astype(rows_ref.dtype)
                    rows_ref[slot, width // 2 : packed] = rest.astype(rows_ref.dtype)
                else:
                    gap = ahead(s, t)
                    turn = jnp.where(gap < slot_count, gap, gap - total_groups + slot_count)
                    at = pl.multiple_of(packed + (turn - 1) * width, TILE)
                    rows_ref[slot, pl.ds(at, width)] = block.astype(rows_ref.dtype)
        return carry

    lax.fori_loop(0, region_count, add_region, 0, unroll=region_count <= 2)
    for at, send_ref in enumerate(send_refs):
        first, last = row_range(at // CORES, width, slot_count)
        for pair in range(send_ref.shape[0]):
            send_ref[pair] = rows_ref[CORES * pair + at % CORES, first:last]


def order_of(chunk, pair_count):
    def key(pair):
        return (0 if chunk == 0 else -pair.bit_length(), pair.bit_count(), -pair)

    return sorted(range(1, pair_count), key=key)


def sum_kernel(chunk, slot_count, first, last, *refs):
    width = refs[-1].shape[1]
    half, packed = width // 2, packed_rows(width)
    count = sum_rows(chunk, width, slot_count)
    base = packed if chunk == 0 else 0
    arrays = list(refs)
    scaled_ref = arrays.pop() if last else None
    sums_ref = arrays.pop()
    sums_ref[...] = jnp.zeros_like(sums_ref) if first else arrays.pop(0)[...]

    def units(arrays):
        own = CORES if first else 0
        return [(ref, 0) for ref in arrays[:own]] + [
            (ref, core) for ref in arrays[own:] for core in range(CORES)
        ]

    array_count = len(arrays) // (chunk + 1)
    tags = [
        jnp.max(ref[at, half:packed].astype(jnp.float32)[TILE - 1 :, width - 1 :]).astype(
            jnp.int32
        )
        for ref, at in units(arrays[:array_count])
    ]
    for tag, (ref, at) in zip(tags, units(arrays[-array_count:])):
        away = tag // slot_count
        place = tag - slot_count * away
        if chunk == 0:
            to = pl.ds(pl.multiple_of(count * away, TILE), packed)
            sums_ref[to] += ref[at, :packed].astype(jnp.float32)
        for part, (turn, _) in enumerate(parts_of(chunk, slot_count)):
            wraps = (place + turn >= slot_count).astype(jnp.int32)
            to = count * away + base + (2 * part + wraps) * half
            block = ref[at, base + part * half : base + (part + 1) * half]
            sums_ref[pl.ds(pl.multiple_of(to, TILE), half)] += block.astype(jnp.float32)

    if not last:
        return
    if chunk == 0:
        col = lax.broadcasted_iota(jnp.int32, (TILE, width), 1)
        for at in (half, count + half):
            sums_ref[at : at + TILE] = jnp.where(col < half, sums_ref[at : at + TILE], 0.0)

    tops = jnp.max(jnp.abs(sums_ref[count:]), axis=0, keepdims=True)
    largest = jnp.max(jnp.broadcast_to(tops, (8, width)), axis=1, keepdims=True)
    power = jnp.floor(jnp.log2(jnp.maximum(largest, 2.0**LEAST_POWER))) - TOP_POWER
    scaled_ref[:count] = sums_ref[count:] * jnp.exp2(-power)[0:1]
    if chunk == 0:
        scaled_ref[half:packed] = jnp.where(col < half, scaled_ref[half:packed], power[0:1])
    else:
        scaled_ref[count:] = jnp.broadcast_to(power[0:1], (TILE, width))


def merge_kernel(keep_ref, got_ref, *refs):
    pair_count = keep_ref.shape[0]
    for at, send_ref in enumerate(refs[1 - pair_count :], 1):
        send_ref[0] = keep_ref[at]
        send_ref[1] = got_ref[at]


def join_kernel(chunk, slot_count, sums_ref, far_ref, *refs):
    out_hbm, joined_ref, sems = refs[-3:]
    width = joined_ref.shape[2]
    half, packed = width // 2, packed_rows(width)
    at = half if chunk == 0 else sum_rows(chunk, width, slot_count)
    factor = jnp.exp2(far_ref[at : at + 8][:1, width - 1 :])
    copies = []

    def joined(first, size):
        return sums_ref[first : first + size] + far_ref[first : first + size] * factor

    def put(block, offset, at):
        place = len(copies)
        joined_ref[place] = block
        copies.append(
            pltpu.make_async_copy(
                joined_ref.at[place],
                out_hbm.at[offset + slot_count - 1, at * half : (at + 1) * half],
                sems.at[place],
            )
        )
        copies[-1].start()

    base = 0
    if chunk == 0:
        base = packed
        for at, block in enumerate(unpack(joined(0, half), joined(half, 8)[:1])):
            put(block, 0, at)
    for part, (turn, at) in enumerate(parts_of(chunk, slot_count)):
        for wraps in range(2):
            first = base + (2 * part + wraps) * half
            put(joined(first, half), turn - slot_count * wraps, at)
    for copy in copies:
        copy.wait()


def shards(solve_cols, region_groups):
    region_count, row_count, col_count = solve_cols.shape
    slot_count = region_groups.shape[1]
    width = col_count // slot_count
    total_groups = lax.axis_size("group")
    half = region_count * slot_count
    span_count = 2 * slot_count - 1
    pair_count = half // CORES
    params = pltpu.CompilerParams(vmem_limit_bytes=VMEM_BYTES)
    light = pl.CostEstimate(flops=0, bytes_accessed=0, transcendentals=0)
    vmem = pl.BlockSpec(memory_space=pltpu.VMEM)
    hbm = pl.BlockSpec(memory_space=pltpu.HBM)

    def permute(values, step):
        pairs = [(d, d ^ step) for d in range(total_groups)]
        return lax.ppermute(values, "group", pairs)

    def blocks(count, chunk):
        first, last = row_range(chunk, width, slot_count)
        return jax.ShapeDtypeStruct((count, last - first, width), solve_cols.dtype)

    sends = pl.pallas_call(
        functools.partial(gram_kernel, total_groups, half),
        in_specs=[hbm] * 2,
        out_specs=[vmem] * (CHUNKS * CORES),
        out_shape=[blocks(pair_count, chunk) for chunk in range(CHUNKS) for _ in range(CORES)],
        scratch_shapes=[
            pltpu.SMEM(region_groups.shape, region_groups.dtype),
            pltpu.VMEM(solve_cols.shape, solve_cols.dtype),
            pltpu.VMEM((half, unit_rows(width, slot_count), width), solve_cols.dtype),
            pltpu.SemaphoreType.DMA,
            pltpu.SemaphoreType.DMA((region_count, COPIES)),
        ],
        cost_estimate=light,
        compiler_params=params,
        name="gram_rows",
    )(
        pltpu.with_memory_space_constraint(region_groups, pltpu.HBM),
        pltpu.with_memory_space_constraint(solve_cols, pltpu.HBM),
    )

    pieces, tagged = [], []
    for chunk in range(CHUNKS):
        keep, give = sends[CORES * chunk : CORES * (chunk + 1)]
        gots = [keep, permute(give, 1)]
        merged = pl.pallas_call(
            merge_kernel,
            out_shape=[blocks(CORES, chunk)] * (pair_count - 1),
            cost_estimate=light,
            compiler_params=params,
            name="merge_units",
        )(*gots, *tagged[CORES + 1 : CORES + 1 + chunk])
        for pair in order_of(chunk, pair_count):
            gots.append(permute(merged[pair - 1], CORES * pair))
        tagged = tagged or gots
        count = sum_rows(chunk, width, slot_count)
        shape = jax.ShapeDtypeStruct((2 * count, width), jnp.float32)
        scaled = jax.ShapeDtypeStruct((count + TILE * chunk, width), jnp.float32)
        by_chip = dict(zip(order_of(0, pair_count), tagged[CORES:]))
        tags = tagged[:CORES] + [by_chip[pair] for pair in order_of(chunk, pair_count)]
        sums = ()
        calls = [(0, -1), (-1, None)] if chunk == 0 else [(0, None)]
        for begin, end in calls:
            first, last, arrays = begin == 0, end is None, slice(begin, end)
            sums = pl.pallas_call(
                functools.partial(sum_kernel, chunk, slot_count, first, last),
                out_shape=(shape, scaled) if last else (shape,),
                cost_estimate=light,
                compiler_params=params,
                name="sum_offsets",
            )(*sums, *(tags[arrays] if chunk else ()), *gots[arrays])
        sums, scaled = sums
        far = permute(scaled.astype(jnp.float16), half)
        pieces.append((sums, far.astype(jnp.float32)))

    schur = ()
    for chunk in range(CHUNKS):
        count = 2 * len(parts_of(chunk, slot_count)) + (2 if chunk == 0 else 0)
        schur = (
            pl.pallas_call(
                functools.partial(join_kernel, chunk, slot_count),
                in_specs=[vmem] * 2 + [hbm] * len(schur),
                out_specs=hbm,
                out_shape=jax.ShapeDtypeStruct((span_count, width, width), jnp.float32),
                input_output_aliases={2: 0} if schur else {},
                scratch_shapes=[
                    pltpu.VMEM((count, width // 2, width), jnp.float32),
                    pltpu.SemaphoreType.DMA((count,)),
                ],
                cost_estimate=light,
                compiler_params=params,
                name="join_offsets",
            )(*pieces[chunk], *schur),
        )
    return schur[0][None]


def solution(mesh):
    return jax.shard_map(
        shards,
        mesh=mesh,
        in_specs=(P(("parts", "group"), None, None), P("group", None)),
        out_specs=P(("parts", "group"), None, None, None),
        check_vma=False,
    )
```

```python
import functools

import jax
import jax.numpy as jnp
from jax import lax
from jax.experimental import pallas as pl
from jax.experimental.pallas import tpu as pltpu
from jax.sharding import PartitionSpec as P

VMEM_BYTES = 48 * 1024 * 1024
LEAST_POWER = -100.0
TOP_POWER = 13.0
CHUNKS = 2
CORES = 2
COPIES = 2
TILE = 16
PRODUCTS = 2


def packed_rows(width):
    return width // 2 + TILE


def unit_rows(width, slot_count):
    return packed_rows(width) + (slot_count - 1) * width


def parts_of(chunk, slot_count):
    halves = [(turn, at) for turn in range(1, slot_count) for at in range(2)]
    size = len(halves) // CHUNKS
    return halves[chunk * size : (chunk + 1) * size]


def row_range(chunk, width, slot_count):
    size = len(parts_of(chunk, slot_count)) * (width // 2)
    first = packed_rows(width) + chunk * size
    return (0 if chunk == 0 else first), first + size


def sum_rows(chunk, width, slot_count):
    count = 2 * len(parts_of(chunk, slot_count)) * (width // 2)
    return count + (packed_rows(width) if chunk == 0 else 0)


def half_iota(width):
    shape = (width // 2, width)
    return (
        lax.broadcasted_iota(jnp.int32, shape, 0),
        lax.broadcasted_iota(jnp.int32, shape, 1),
    )


def pack(block, tag):
    width = block.shape[1]
    half = width // 2
    row, col = half_iota(width)
    lower = pltpu.roll(block[half:], half, 1)
    packed = jnp.where((col >= half) | (row <= col), block[:half], lower)
    diagonal = jnp.sum(jnp.where(row == col, lower, 0.0), axis=0, keepdims=True)
    rest = jnp.where(col[:1] < half, diagonal, tag)
    return packed, jnp.broadcast_to(rest, (TILE, width))


def unpack(packed, diagonal):
    half, width = packed.shape
    row, col = half_iota(width)
    turned = jnp.concatenate([packed, jnp.zeros_like(packed)], axis=0).T
    upper = jnp.where((col >= half) | (row <= col), packed, turned[:half])
    last = jnp.where(row > col, packed, jnp.where(row < col, turned[:half], diagonal))
    return upper, jnp.where(col < half, turned[half:], pltpu.roll(last, half, 1))


def gram_kernel(total_groups, half, groups_hbm, cols_hbm, *refs):
    groups_ref, cols_ref, rows_ref, groups_sem, cols_sems = refs[-5:]
    send_refs = refs[:-5]
    region_count, slot_count = groups_ref.shape
    width = cols_ref.shape[2] // slot_count
    me = lax.axis_index("group")
    my_half, my_slot = me // half, lax.rem(me, half)
    groups_copy = pltpu.make_async_copy(groups_hbm, groups_ref, groups_sem)
    groups_copy.start()

    depth = cols_ref.shape[1] // COPIES

    def cols_copy(region, part):
        rows = pl.ds(part * depth, depth)
        return pltpu.make_async_copy(
            cols_hbm.at[region, rows], cols_ref.at[region, rows], cols_sems.at[region, part]
        )

    for region in range(region_count):
        for part in range(COPIES):
            cols_copy(region, part).start()
    groups_copy.wait()
    for region in range(region_count):
        for part in range(COPIES):
            cols_copy(region, part).wait()
    packed = packed_rows(width)

    def add_region(region, carry):
        cols = cols_ref[region]
        depth = cols.shape[1] // PRODUCTS
        grams = [
            lax.dot_general(
                cols[:, at * depth : (at + 1) * depth],
                cols,
                (((0,), (0,)), ((), ())),
                preferred_element_type=jnp.float32,
            )
            for at in range(PRODUCTS)
        ]
        groups = [groups_ref[region, s] for s in range(slot_count)]

        def ahead(s, t):
            return lax.rem(groups[t] - groups[s] + total_groups, total_groups)

        for s in range(slot_count):
            place = 0
            for t in range(slot_count):
                if t != s:
                    place = place + (ahead(t, s) < slot_count).astype(jnp.int32)
            away = (groups[s] // half != my_half).astype(jnp.int32)
            tag = (place + slot_count * away).astype(jnp.float32)
            slot = lax.rem(groups[s], half) ^ my_slot
            for t in range(slot_count):
                at = s * width % depth
                block = grams[s * width // depth][at : at + width, t * width : (t + 1) * width]
                if t == s:
                    block, rest = pack(block, tag)
                    rows_ref[slot, : width // 2] = block.astype(rows_ref.dtype)
                    rows_ref[slot, width // 2 : packed] = rest.astype(rows_ref.dtype)
                else:
                    gap = ahead(s, t)
                    turn = jnp.where(gap < slot_count, gap, gap - total_groups + slot_count)
                    at = pl.multiple_of(packed + (turn - 1) * width, TILE)
                    rows_ref[slot, pl.ds(at, width)] = block.astype(rows_ref.dtype)
        return carry

    lax.fori_loop(0, region_count, add_region, 0, unroll=region_count <= 2)
    for at, send_ref in enumerate(send_refs):
        first, last = row_range(at // CORES, width, slot_count)
        for pair in range(send_ref.shape[0]):
            send_ref[pair] = rows_ref[CORES * pair + at % CORES, first:last]


def order_of(chunk, pair_count):
    def key(pair):
        return (0 if chunk == 0 else -pair.bit_length(), pair.bit_count(), -pair)

    return sorted(range(1, pair_count), key=key)


def sum_kernel(chunk, slot_count, first, last, *refs):
    width = refs[-1].shape[1]
    half, packed = width // 2, packed_rows(width)
    count = sum_rows(chunk, width, slot_count)
    base = packed if chunk == 0 else 0
    arrays = list(refs)
    scaled_ref = arrays.pop() if last else None
    sums_ref = arrays.pop()
    sums_ref[...] = jnp.zeros_like(sums_ref) if first else arrays.pop(0)[...]

    def units(arrays):
        own = CORES if first else 0
        return [(ref, 0) for ref in arrays[:own]] + [
            (ref, core) for ref in arrays[own:] for core in range(CORES)
        ]

    array_count = len(arrays) // (chunk + 1)
    tags = [
        jnp.max(ref[at, half:packed].astype(jnp.float32)[TILE - 1 :, width - 1 :]).astype(
            jnp.int32
        )
        for ref, at in units(arrays[:array_count])
    ]
    for tag, (ref, at) in zip(tags, units(arrays[-array_count:])):
        away = tag // slot_count
        place = tag - slot_count * away
        if chunk == 0:
            to = pl.ds(pl.multiple_of(count * away, TILE), packed)
            sums_ref[to] += ref[at, :packed].astype(jnp.float32)
        for part, (turn, _) in enumerate(parts_of(chunk, slot_count)):
            wraps = (place + turn >= slot_count).astype(jnp.int32)
            to = count * away + base + (2 * part + wraps) * half
            block = ref[at, base + part * half : base + (part + 1) * half]
            sums_ref[pl.ds(pl.multiple_of(to, TILE), half)] += block.astype(jnp.float32)

    if not last:
        return
    if chunk == 0:
        col = lax.broadcasted_iota(jnp.int32, (TILE, width), 1)
        for at in (half, count + half):
            sums_ref[at : at + TILE] = jnp.where(col < half, sums_ref[at : at + TILE], 0.0)

    tops = jnp.max(jnp.abs(sums_ref[count:]), axis=0, keepdims=True)
    largest = jnp.max(jnp.broadcast_to(tops, (8, width)), axis=1, keepdims=True)
    power = jnp.floor(jnp.log2(jnp.maximum(largest, 2.0**LEAST_POWER))) - TOP_POWER
    scaled_ref[:count] = sums_ref[count:] * jnp.exp2(-power)[0:1]
    if chunk == 0:
        scaled_ref[half:packed] = jnp.where(col < half, scaled_ref[half:packed], power[0:1])
    else:
        scaled_ref[count:] = jnp.broadcast_to(power[0:1], (TILE, width))


def merge_kernel(keep_ref, got_ref, *refs):
    pair_count = keep_ref.shape[0]
    for at, send_ref in enumerate(refs[1 - pair_count :], 1):
        send_ref[0] = keep_ref[at]
        send_ref[1] = got_ref[at]


def join_kernel(chunk, slot_count, sums_ref, far_ref, *refs):
    out_hbm, joined_ref, sems = refs[-3:]
    width = joined_ref.shape[2]
    half, packed = width // 2, packed_rows(width)
    at = half if chunk == 0 else sum_rows(chunk, width, slot_count)
    factor = jnp.exp2(far_ref[at : at + 8][:1, width - 1 :])
    copies = []

    def joined(first, size):
        return sums_ref[first : first + size] + far_ref[first : first + size] * factor

    def put(block, offset, at):
        place = len(copies)
        joined_ref[place] = block
        copies.append(
            pltpu.make_async_copy(
                joined_ref.at[place],
                out_hbm.at[offset + slot_count - 1, at * half : (at + 1) * half],
                sems.at[place],
            )
        )
        copies[-1].start()

    base = 0
    if chunk == 0:
        base = packed
        for at, block in enumerate(unpack(joined(0, half), joined(half, 8)[:1])):
            put(block, 0, at)
    for part, (turn, at) in enumerate(parts_of(chunk, slot_count)):
        for wraps in range(2):
            first = base + (2 * part + wraps) * half
            put(joined(first, half), turn - slot_count * wraps, at)
    for copy in copies:
        copy.wait()


def shards(solve_cols, region_groups):
    region_count, row_count, col_count = solve_cols.shape
    slot_count = region_groups.shape[1]
    width = col_count // slot_count
    total_groups = lax.axis_size("group")
    half = region_count * slot_count
    span_count = 2 * slot_count - 1
    pair_count = half // CORES
    params = pltpu.CompilerParams(vmem_limit_bytes=VMEM_BYTES)
    light = pl.CostEstimate(flops=0, bytes_accessed=0, transcendentals=0)
    vmem = pl.BlockSpec(memory_space=pltpu.VMEM)
    hbm = pl.BlockSpec(memory_space=pltpu.HBM)

    def permute(values, step):
        pairs = [(d, d ^ step) for d in range(total_groups)]
        return lax.ppermute(values, "group", pairs)

    def blocks(count, chunk):
        first, last = row_range(chunk, width, slot_count)
        return jax.ShapeDtypeStruct((count, last - first, width), solve_cols.dtype)

    sends = pl.pallas_call(
        functools.partial(gram_kernel, total_groups, half),
        in_specs=[hbm] * 2,
        out_specs=[vmem] * (CHUNKS * CORES),
        out_shape=[blocks(pair_count, chunk) for chunk in range(CHUNKS) for _ in range(CORES)],
        scratch_shapes=[
            pltpu.SMEM(region_groups.shape, region_groups.dtype),
            pltpu.VMEM(solve_cols.shape, solve_cols.dtype),
            pltpu.VMEM((half, unit_rows(width, slot_count), width), solve_cols.dtype),
            pltpu.SemaphoreType.DMA,
            pltpu.SemaphoreType.DMA((region_count, COPIES)),
        ],
        cost_estimate=light,
        compiler_params=params,
        name="gram_rows",
    )(
        pltpu.with_memory_space_constraint(region_groups, pltpu.HBM),
        pltpu.with_memory_space_constraint(solve_cols, pltpu.HBM),
    )

    pieces, tagged = [], []
    for chunk in range(CHUNKS):
        keep, give = sends[CORES * chunk : CORES * (chunk + 1)]
        gots = [keep, permute(give, 1)]
        merged = pl.pallas_call(
            merge_kernel,
            out_shape=[blocks(CORES, chunk)] * (pair_count - 1),
            cost_estimate=light,
            compiler_params=params,
            name="merge_units",
        )(*gots)
        for pair in order_of(chunk, pair_count):
            gots.append(permute(merged[pair - 1], CORES * pair))
        tagged = tagged or gots
        count = sum_rows(chunk, width, slot_count)
        shape = jax.ShapeDtypeStruct((2 * count, width), jnp.float32)
        scaled = jax.ShapeDtypeStruct((count + TILE * chunk, width), jnp.float32)
        by_chip = dict(zip(order_of(0, pair_count), tagged[CORES:]))
        tags = tagged[:CORES] + [by_chip[pair] for pair in order_of(chunk, pair_count)]
        sums = ()
        calls = [(0, -1), (-1, None)] if chunk == 0 else [(0, None)]
        for begin, end in calls:
            first, last, arrays = begin == 0, end is None, slice(begin, end)
            sums = pl.pallas_call(
                functools.partial(sum_kernel, chunk, slot_count, first, last),
                out_shape=(shape, scaled) if last else (shape,),
                cost_estimate=light,
                compiler_params=params,
                name="sum_offsets",
            )(*sums, *(tags[arrays] if chunk else ()), *gots[arrays])
        sums, scaled = sums
        far = permute(scaled.astype(jnp.float16), half)
        pieces.append((sums, far.astype(jnp.float32)))

    schur = ()
    for chunk in range(CHUNKS):
        count = 2 * len(parts_of(chunk, slot_count)) + (2 if chunk == 0 else 0)
        schur = (
            pl.pallas_call(
                functools.partial(join_kernel, chunk, slot_count),
                in_specs=[vmem] * 2 + [hbm] * len(schur),
                out_specs=hbm,
                out_shape=jax.ShapeDtypeStruct((span_count, width, width), jnp.float32),
                input_output_aliases={2: 0} if schur else {},
                scratch_shapes=[
                    pltpu.VMEM((count, width // 2, width), jnp.float32),
                    pltpu.SemaphoreType.DMA((count,)),
                ],
                cost_estimate=light,
                compiler_params=params,
                name="join_offsets",
            )(*pieces[chunk], *schur),
        )
    return schur[0][None]


def solution(mesh):
    return jax.shard_map(
        shards,
        mesh=mesh,
        in_specs=(P(("parts", "group"), None, None), P("group", None)),
        out_specs=P(("parts", "group"), None, None, None),
        check_vma=False,
    )
```

```python
import functools

import jax
import jax.numpy as jnp
from jax import lax
from jax.experimental import pallas as pl
from jax.experimental.pallas import tpu as pltpu
from jax.sharding import PartitionSpec as P

VMEM_BYTES = 48 * 1024 * 1024
LEAST_POWER = -100.0
TOP_POWER = 13.0
CHUNKS = 2
CORES = 2
COPIES = 2
TILE = 16
PRODUCTS = 2


def packed_rows(width):
    return width // 2 + TILE


def unit_rows(width, slot_count):
    return packed_rows(width) + (slot_count - 1) * width


def parts_of(chunk, slot_count):
    halves = [(turn, at) for turn in range(1, slot_count) for at in range(2)]
    size = len(halves) // CHUNKS
    return halves[chunk * size : (chunk + 1) * size]


def row_range(chunk, width, slot_count):
    size = len(parts_of(chunk, slot_count)) * (width // 2)
    first = packed_rows(width) + chunk * size
    return (0 if chunk == 0 else first), first + size


def sum_rows(chunk, width, slot_count):
    count = 2 * len(parts_of(chunk, slot_count)) * (width // 2)
    return count + (packed_rows(width) if chunk == 0 else 0)


def half_iota(width):
    shape = (width // 2, width)
    return (
        lax.broadcasted_iota(jnp.int32, shape, 0),
        lax.broadcasted_iota(jnp.int32, shape, 1),
    )


def pack(block, tag):
    width = block.shape[1]
    half = width // 2
    row, col = half_iota(width)
    lower = pltpu.roll(block[half:], half, 1)
    packed = jnp.where((col >= half) | (row <= col), block[:half], lower)
    diagonal = jnp.sum(jnp.where(row == col, lower, 0.0), axis=0, keepdims=True)
    rest = jnp.where(col[:1] < half, diagonal, tag)
    return packed, jnp.broadcast_to(rest, (TILE, width))


def unpack(packed, diagonal):
    half, width = packed.shape
    row, col = half_iota(width)
    turned = jnp.concatenate([packed, jnp.zeros_like(packed)], axis=0).T
    upper = jnp.where((col >= half) | (row <= col), packed, turned[:half])
    last = jnp.where(row > col, packed, jnp.where(row < col, turned[:half], diagonal))
    return upper, jnp.where(col < half, turned[half:], pltpu.roll(last, half, 1))


def gram_kernel(total_groups, half, groups_hbm, cols_hbm, *refs):
    groups_ref, cols_ref, rows_ref, groups_sem, cols_sems = refs[-5:]
    send_refs = refs[:-5]
    region_count, slot_count = groups_ref.shape
    width = cols_ref.shape[2] // slot_count
    me = lax.axis_index("group")
    my_half, my_slot = me // half, lax.rem(me, half)
    groups_copy = pltpu.make_async_copy(groups_hbm, groups_ref, groups_sem)
    groups_copy.start()

    depth = cols_ref.shape[1] // COPIES

    def cols_copy(region, part):
        rows = pl.ds(part * depth, depth)
        return pltpu.make_async_copy(
            cols_hbm.at[region, rows], cols_ref.at[region, rows], cols_sems.at[region, part]
        )

    for region in range(region_count):
        for part in range(COPIES):
            cols_copy(region, part).start()
    groups_copy.wait()
    for region in range(region_count):
        for part in range(COPIES):
            cols_copy(region, part).wait()
    packed = packed_rows(width)

    def add_region(region, carry):
        cols = cols_ref[region]
        depth = cols.shape[1] // PRODUCTS
        grams = [
            lax.dot_general(
                cols[:, at * depth : (at + 1) * depth],
                cols,
                (((0,), (0,)), ((), ())),
                preferred_element_type=jnp.float32,
            )
            for at in range(PRODUCTS)
        ]
        groups = [groups_ref[region, s] for s in range(slot_count)]

        def ahead(s, t):
            return lax.rem(groups[t] - groups[s] + total_groups, total_groups)

        for s in range(slot_count):
            place = 0
            for t in range(slot_count):
                if t != s:
                    place = place + (ahead(t, s) < slot_count).astype(jnp.int32)
            away = (groups[s] // half != my_half).astype(jnp.int32)
            tag = (place + slot_count * away).astype(jnp.float32)
            slot = lax.rem(groups[s], half) ^ my_slot
            for t in range(slot_count):
                at = s * width % depth
                block = grams[s * width // depth][at : at + width, t * width : (t + 1) * width]
                if t == s:
                    block, rest = pack(block, tag)
                    rows_ref[slot, : width // 2] = block.astype(rows_ref.dtype)
                    rows_ref[slot, width // 2 : packed] = rest.astype(rows_ref.dtype)
                else:
                    gap = ahead(s, t)
                    turn = jnp.where(gap < slot_count, gap, gap - total_groups + slot_count)
                    at = pl.multiple_of(packed + (turn - 1) * width, TILE)
                    rows_ref[slot, pl.ds(at, width)] = block.astype(rows_ref.dtype)
        return carry

    lax.fori_loop(0, region_count, add_region, 0, unroll=region_count <= 2)
    for at, send_ref in enumerate(send_refs):
        first, last = row_range(at // CORES, width, slot_count)
        for pair in range(send_ref.shape[0]):
            send_ref[pair] = rows_ref[CORES * pair + at % CORES, first:last]


def order_of(chunk, pair_count):
    def key(pair):
        return (pair.bit_count(), -pair)

    return sorted(range(1, pair_count), key=key)


def sum_kernel(chunk, slot_count, first, last, *refs):
    width = refs[-1].shape[1]
    half, packed = width // 2, packed_rows(width)
    count = sum_rows(chunk, width, slot_count)
    base = packed if chunk == 0 else 0
    arrays = list(refs)
    scaled_ref = arrays.pop() if last else None
    sums_ref = arrays.pop()
    sums_ref[...] = jnp.zeros_like(sums_ref) if first else arrays.pop(0)[...]

    def units(arrays):
        own = CORES if first else 0
        return [(ref, 0) for ref in arrays[:own]] + [
            (ref, core) for ref in arrays[own:] for core in range(CORES)
        ]

    array_count = len(arrays) // (chunk + 1)
    tags = [
        jnp.max(ref[at, half:packed].astype(jnp.float32)[TILE - 1 :, width - 1 :]).astype(
            jnp.int32
        )
        for ref, at in units(arrays[:array_count])
    ]
    for tag, (ref, at) in zip(tags, units(arrays[-array_count:])):
        away = tag // slot_count
        place = tag - slot_count * away
        if chunk == 0:
            to = pl.ds(pl.multiple_of(count * away, TILE), packed)
            sums_ref[to] += ref[at, :packed].astype(jnp.float32)
        for part, (turn, _) in enumerate(parts_of(chunk, slot_count)):
            wraps = (place + turn >= slot_count).astype(jnp.int32)
            to = count * away + base + (2 * part + wraps) * half
            block = ref[at, base + part * half : base + (part + 1) * half]
            sums_ref[pl.ds(pl.multiple_of(to, TILE), half)] += block.astype(jnp.float32)

    if not last:
        return
    if chunk == 0:
        col = lax.broadcasted_iota(jnp.int32, (TILE, width), 1)
        for at in (half, count + half):
            sums_ref[at : at + TILE] = jnp.where(col < half, sums_ref[at : at + TILE], 0.0)

    tops = jnp.max(jnp.abs(sums_ref[count:]), axis=0, keepdims=True)
    largest = jnp.max(jnp.broadcast_to(tops, (8, width)), axis=1, keepdims=True)
    power = jnp.floor(jnp.log2(jnp.maximum(largest, 2.0**LEAST_POWER))) - TOP_POWER
    scaled_ref[:count] = sums_ref[count:] * jnp.exp2(-power)[0:1]
    if chunk == 0:
        scaled_ref[half:packed] = jnp.where(col < half, scaled_ref[half:packed], power[0:1])
    else:
        scaled_ref[count:] = jnp.broadcast_to(power[0:1], (TILE, width))


def merge_kernel(keep_ref, got_ref, *refs):
    pair_count = keep_ref.shape[0]
    for at, send_ref in enumerate(refs[1 - pair_count :], 1):
        send_ref[0] = keep_ref[at]
        send_ref[1] = got_ref[at]


def join_kernel(chunk, slot_count, sums_ref, far_ref, *refs):
    out_hbm, joined_ref, sems = refs[-3:]
    width = joined_ref.shape[2]
    half, packed = width // 2, packed_rows(width)
    at = half if chunk == 0 else sum_rows(chunk, width, slot_count)
    factor = jnp.exp2(far_ref[at : at + 8][:1, width - 1 :])
    copies = []

    def joined(first, size):
        return sums_ref[first : first + size] + far_ref[first : first + size] * factor

    def put(block, offset, at):
        place = len(copies)
        joined_ref[place] = block
        copies.append(
            pltpu.make_async_copy(
                joined_ref.at[place],
                out_hbm.at[offset + slot_count - 1, at * half : (at + 1) * half],
                sems.at[place],
            )
        )
        copies[-1].start()

    base = 0
    if chunk == 0:
        base = packed
        for at, block in enumerate(unpack(joined(0, half), joined(half, 8)[:1])):
            put(block, 0, at)
    for part, (turn, at) in enumerate(parts_of(chunk, slot_count)):
        for wraps in range(2):
            first = base + (2 * part + wraps) * half
            put(joined(first, half), turn - slot_count * wraps, at)
    for copy in copies:
        copy.wait()


def shards(solve_cols, region_groups):
    region_count, row_count, col_count = solve_cols.shape
    slot_count = region_groups.shape[1]
    width = col_count // slot_count
    total_groups = lax.axis_size("group")
    half = region_count * slot_count
    span_count = 2 * slot_count - 1
    pair_count = half // CORES
    params = pltpu.CompilerParams(vmem_limit_bytes=VMEM_BYTES)
    light = pl.CostEstimate(flops=0, bytes_accessed=0, transcendentals=0)
    vmem = pl.BlockSpec(memory_space=pltpu.VMEM)
    hbm = pl.BlockSpec(memory_space=pltpu.HBM)

    def permute(values, step):
        pairs = [(d, d ^ step) for d in range(total_groups)]
        return lax.ppermute(values, "group", pairs)

    def blocks(count, chunk):
        first, last = row_range(chunk, width, slot_count)
        return jax.ShapeDtypeStruct((count, last - first, width), solve_cols.dtype)

    sends = pl.pallas_call(
        functools.partial(gram_kernel, total_groups, half),
        in_specs=[hbm] * 2,
        out_specs=[vmem] * (CHUNKS * CORES),
        out_shape=[blocks(pair_count, chunk) for chunk in range(CHUNKS) for _ in range(CORES)],
        scratch_shapes=[
            pltpu.SMEM(region_groups.shape, region_groups.dtype),
            pltpu.VMEM(solve_cols.shape, solve_cols.dtype),
            pltpu.VMEM((half, unit_rows(width, slot_count), width), solve_cols.dtype),
            pltpu.SemaphoreType.DMA,
            pltpu.SemaphoreType.DMA((region_count, COPIES)),
        ],
        cost_estimate=light,
        compiler_params=params,
        name="gram_rows",
    )(
        pltpu.with_memory_space_constraint(region_groups, pltpu.HBM),
        pltpu.with_memory_space_constraint(solve_cols, pltpu.HBM),
    )

    pieces, tagged = [], []
    for chunk in range(CHUNKS):
        keep, give = sends[CORES * chunk : CORES * (chunk + 1)]
        gots = [keep, permute(give, 1)]
        merged = pl.pallas_call(
            merge_kernel,
            out_shape=[blocks(CORES, chunk)] * (pair_count - 1),
            cost_estimate=light,
            compiler_params=params,
            name="merge_units",
        )(*gots, *tagged[CORES : CORES + chunk])
        for pair in order_of(chunk, pair_count):
            gots.append(permute(merged[pair - 1], CORES * pair))
        tagged = tagged or gots
        count = sum_rows(chunk, width, slot_count)
        shape = jax.ShapeDtypeStruct((2 * count, width), jnp.float32)
        scaled = jax.ShapeDtypeStruct((count + TILE * chunk, width), jnp.float32)
        by_chip = dict(zip(order_of(0, pair_count), tagged[CORES:]))
        tags = tagged[:CORES] + [by_chip[pair] for pair in order_of(chunk, pair_count)]
        sums = ()
        calls = [(0, -1), (-1, None)] if chunk == 0 else [(0, None)]
        for begin, end in calls:
            first, last, arrays = begin == 0, end is None, slice(begin, end)
            sums = pl.pallas_call(
                functools.partial(sum_kernel, chunk, slot_count, first, last),
                out_shape=(shape, scaled) if last else (shape,),
                cost_estimate=light,
                compiler_params=params,
                name="sum_offsets",
            )(*sums, *(tags[arrays] if chunk else ()), *gots[arrays])
        sums, scaled = sums
        far = permute(scaled.astype(jnp.float16), half)
        pieces.append((sums, far.astype(jnp.float32)))

    schur = ()
    for chunk in range(CHUNKS):
        count = 2 * len(parts_of(chunk, slot_count)) + (2 if chunk == 0 else 0)
        schur = (
            pl.pallas_call(
                functools.partial(join_kernel, chunk, slot_count),
                in_specs=[vmem] * 2 + [hbm] * len(schur),
                out_specs=hbm,
                out_shape=jax.ShapeDtypeStruct((span_count, width, width), jnp.float32),
                input_output_aliases={2: 0} if schur else {},
                scratch_shapes=[
                    pltpu.VMEM((count, width // 2, width), jnp.float32),
                    pltpu.SemaphoreType.DMA((count,)),
                ],
                cost_estimate=light,
                compiler_params=params,
                name="join_offsets",
            )(*pieces[chunk], *schur),
        )
    return schur[0][None]


def solution(mesh):
    return jax.shard_map(
        shards,
        mesh=mesh,
        in_specs=(P(("parts", "group"), None, None), P("group", None)),
        out_specs=P(("parts", "group"), None, None, None),
        check_vma=False,
    )
```
